32 devices in a mesh: ctx: 8 (over y, x, core), tp: 4 (over z).
Axes of the slice: x: 2, y: 2, z: 4, core: 2. Of those that a mesh axis runs over, the one named last changes fastest.
Arguments:
- queries: bfloat16 [2048, 2048], P('ctx', 'tp'), may hold values from -70 to 70
- keys: bfloat16 [2048, 1024], P('ctx', 'tp'), may hold values from -6 to 6
- values: bfloat16 [2048, 1024], P('ctx', 'tp'), may hold values from -6 to 6
- grad_out: bfloat16 [2048, 5376], P(('ctx', 'tp')), may hold values from -24 to 24
- out_weight: bfloat16 [2048, 5376], P('tp'), may hold values from -0.078125 to 0.078125
Outputs:
- grad_queries: float32 [2048, 2048], P('ctx', 'tp')
- grad_keys: float32 [2048, 1024], P('ctx', 'tp')
- grad_values: float32 [2048, 1024], P('ctx', 'tp')
The draws below stay inside these ranges and needn't reach their ends.
All inputs are finite; a program needn't handle non-finite values.
Results may differ from the reference program's by a relative error of at most 0.014.
Values may be sent and summed in bfloat16 or wider, within the bound.
No kernel may reach another device: no remote copies, remote signals or barrier semaphores. Data moves between devices by JAX's collectives and lax.ppermute only.
A program may use at most 64 MiB of HBM per device.

```python
import jax
import jax.numpy as jnp
from jax import lax

D = 5376
HQ = 16
KV = 8
HD = 128
WIN = 1024
SEQ_DEV = 256
TOKENS = 2048


def drawn_pair(key):
    query_seed = jax.random.fold_in(key, 101)
    key_seed = jax.random.fold_in(key, 202)
    base_query = jnp.clip(jax.random.normal(query_seed, (TOKENS, HQ * HD), jnp.float32), -6.0, 6.0)
    base_key = jnp.clip(jax.random.normal(key_seed, (TOKENS, KV * HD), jnp.float32), -6.0, 6.0)
    return (base_query, base_key)


def draw_queries(key, part):
    return drawn_pair(key)[0].astype(jnp.bfloat16)


def draw_keys(key, part):
    return drawn_pair(key)[1].astype(jnp.bfloat16)


def level_of(stream_key, extent, split, low, high):
    gain = 1.0
    for dim, shards_of in split:
        steps = jax.random.uniform(jax.random.fold_in(jax.random.fold_in(stream_key, 6), dim), (shards_of,), jnp.float32, low / len(split), high / len(split))
        gain = gain * jnp.repeat(jnp.exp(steps), extent[dim] // shards_of).reshape((-1,) + (1,) * (len(extent) - 1 - dim))
    return gain


def noise(key, dims, scale, bound, shards=(), kind=jnp.bfloat16):
    drawn = scale * jax.random.normal(key, dims, jnp.float32)
    if shards:
        drawn = drawn * level_of(key, dims, shards, -0.22, 0.18)
    return jnp.clip(drawn, -bound, bound).astype(kind)


def setup_inputs(seed: int = 0) -> dict:
    streams_of = jax.random.split(jax.random.key(seed), 6)
    queries = draw_queries(jax.random.fold_in(streams_of[5], 71), 0)
    keys = draw_keys(jax.random.fold_in(streams_of[5], 71), 0)
    values = noise(streams_of[2], (TOKENS, KV * HD), 1.0, 6.0, ((0, 8), (1, 4)))
    grad_out = noise(streams_of[3], (TOKENS, D), 4.0, 24.0, ((0, 32),))
    out_weight = noise(streams_of[4], (HQ * HD, D), D ** -0.5, 0.078125, ((0, 4),))
    return dict(queries=queries, keys=keys, values=values, grad_out=grad_out, out_weight=out_weight)


score_scale = 168.0 ** -0.5


def band_grads(query_block, dout_block, key_span, value_span, query_pos, key_pos):
    shard_rows = query_block.shape[0]
    span_rows = key_span.shape[0]
    kv_heads = KV
    group_size = HQ // KV
    query_heads = query_block.astype(jnp.float32).reshape(shard_rows, kv_heads, group_size, HD)
    dout_heads = dout_block.astype(jnp.float32).reshape(shard_rows, kv_heads, group_size, HD)
    key_heads = key_span.astype(jnp.float32).reshape(span_rows, kv_heads, HD)
    value_heads = value_span.astype(jnp.float32).reshape(span_rows, kv_heads, HD)
    scores = jnp.einsum('sgrd,egd->grse', query_heads, key_heads) * score_scale
    allowed = (key_pos[None, :] <= query_pos[:, None]) & (key_pos[None, :] > query_pos[:, None] - WIN) & (key_pos[None, :] >= 0)
    scores = jnp.where(allowed, scores, -1e30)
    row_max = jnp.max(scores, axis=-1, keepdims=True)
    weights = jnp.where(allowed, jnp.exp(scores - row_max), 0.0)
    probability = weights / jnp.sum(weights, axis=-1, keepdims=True)
    dprobs = jnp.einsum('sgrd,egd->grse', dout_heads, value_heads)
    row_delta = jnp.sum(probability * dprobs, axis=-1, keepdims=True)
    dscores = probability * (dprobs - row_delta)
    probs_low = probability.astype(jnp.bfloat16).astype(jnp.float32)
    dscores_low = dscores.astype(jnp.bfloat16).astype(jnp.float32)
    grad_value = jnp.einsum('grse,sgrd->egd', probs_low, dout_heads)
    grad_query = score_scale * jnp.einsum('grse,egd->sgrd', dscores_low, key_heads)
    grad_key = score_scale * jnp.einsum('grse,sgrd->egd', dscores_low, query_heads)
    return (grad_query.reshape(shard_rows, -1), grad_key.reshape(span_rows, -1),
            grad_value.reshape(span_rows, -1))


def round_earlier(span_terms):
    earlier = lax.optimization_barrier(span_terms[:WIN].astype(jnp.bfloat16)).astype(jnp.float32)
    return jnp.concatenate([earlier, span_terms[WIN:]], axis=0)


def reference(queries, keys, values, grad_out, out_weight):
    dout = jnp.dot(grad_out, out_weight.T, preferred_element_type=jnp.float32).astype(jnp.bfloat16)
    kv_width = keys.shape[1]
    leading = jnp.zeros((WIN, kv_width), keys.dtype)
    key_padded = jnp.concatenate([leading, keys], axis=0)
    value_padded = jnp.concatenate([leading, values], axis=0)
    span_rows = WIN + SEQ_DEV

    def step(carry, block_index):
        key_total, value_total = carry
        start = (block_index * SEQ_DEV).astype(jnp.int32)
        query_block = lax.dynamic_slice_in_dim(queries, start, SEQ_DEV, 0)
        dout_block = lax.dynamic_slice_in_dim(dout, start, SEQ_DEV, 0)
        key_span = lax.dynamic_slice_in_dim(key_padded, start, span_rows, 0)
        value_span = lax.dynamic_slice_in_dim(value_padded, start, span_rows, 0)
        query_pos = start + jnp.arange(SEQ_DEV, dtype=jnp.int32)
        key_pos = start - WIN + jnp.arange(span_rows, dtype=jnp.int32)
        grad_query, grad_key, grad_value = band_grads(query_block, dout_block, key_span, value_span, query_pos, key_pos)
        grad_key = round_earlier(grad_key)
        grad_value = round_earlier(grad_value)
        key_total = lax.dynamic_update_slice_in_dim(
            key_total, lax.dynamic_slice_in_dim(key_total, start, span_rows, 0) + grad_key, start, 0)
        value_total = lax.dynamic_update_slice_in_dim(
            value_total, lax.dynamic_slice_in_dim(value_total, start, span_rows, 0) + grad_value, start, 0)
        return (key_total, value_total), grad_query

    initial = (jnp.zeros((TOKENS + WIN, kv_width), jnp.float32), jnp.zeros((TOKENS + WIN, kv_width), jnp.float32))
    (key_total, value_total), grad_queries = lax.scan(step, initial, jnp.arange(TOKENS // SEQ_DEV, dtype=jnp.int32))
    return grad_queries.reshape(TOKENS, HQ * HD), key_total[WIN:], value_total[WIN:]
```

```python
import functools

import jax
import jax.numpy as jnp
from jax import lax
from jax.experimental import pallas as pl
from jax.experimental.pallas import tpu as pltpu
from jax.sharding import PartitionSpec as P

HD = 128
WIN = 1024
SPAN_BLOCKS = 5
SCALE = 168.0 ** (-0.5)
NT = (((1,), (1,)), ((), ()))
NN = (((1,), (0,)), ((), ()))
F32 = jnp.float32
BF16 = jnp.bfloat16


def dot(a, b, dims):
    return lax.dot_general(a, b, dims, preferred_element_type=F32)


def pieces(x):
    hi = x.astype(BF16)
    rest = x - hi.astype(F32)
    mid = rest.astype(BF16)
    low = (rest - mid.astype(F32)).astype(BF16)
    return hi.astype(F32), mid.astype(F32), low.astype(F32)


def spread(x, first, width):
    lane = lax.broadcasted_iota(jnp.int32, (x.shape[0], width), 1)
    out = jnp.zeros((x.shape[0], width), F32)
    for n, piece in enumerate(pieces(x)):
        out = jnp.where(lane == first + n, piece, out)
    return out


def minus_ones(rows, first):
    lane = lax.broadcasted_iota(jnp.int32, (rows, HD), 1)
    return jnp.where((lane >= first) & (lane < first + 3), -1.0, 0.0).astype(BF16)


def params(limit=48 * 2**20):
    return pltpu.CompilerParams(vmem_limit_bytes=limit)


def probs_kernel(info, own, peer, recv, exch, probs, mixed, stats, span):
    head = pl.program_id(0)
    rows = own.shape[0]
    width = recv.shape[1]
    kv_width = width // 2
    core, shard = info[0], info[1]

    @pl.when(head == 0)
    def _():
        stats[...] = jnp.zeros_like(stats)
        span[4 * rows :, :] = own[:, :width]
        span[rows : 2 * rows, :] = exch[:rows, :]

        @pl.when(core == 0)
        def _():
            span[:rows, :] = exch[rows:, :]
            span[2 * rows : 4 * rows, :] = recv[...]

        @pl.when(core == 1)
        def _():
            span[:rows, :] = recv[:rows, :]
            span[2 * rows : 3 * rows, :] = exch[rows:, :]
            span[3 * rows : 4 * rows, :] = peer[:, :width]

    group = head // 2
    key = span[:, pl.ds(pl.multiple_of(group * HD, HD), HD)]
    value = span[:, pl.ds(pl.multiple_of(kv_width + group * HD, HD), HD)]
    query = own[:, pl.ds(pl.multiple_of(width + head * HD, HD), HD)]
    scores = dot(query, key, NT) * SCALE
    row = lax.broadcasted_iota(jnp.int32, (rows, 1), 0)
    col = lax.broadcasted_iota(jnp.int32, scores.shape, 1)
    first = jnp.maximum(row + 1, (SPAN_BLOCKS - 1 - shard) * rows)
    scores = jnp.where((col >= first) & (col <= row + WIN), scores, -1e30)
    top = jnp.max(scores, axis=1, keepdims=True)
    weights = jnp.exp(scores - top)
    total = jnp.sum(weights, axis=1, keepdims=True)
    probability = (weights * (1.0 / total)).astype(BF16)
    probs[0] = probability
    mixed[...] = dot(probability, value, NN)
    level = (top + jnp.log(total)) * (1.0 / SCALE)
    stats[...] += spread(level, 8 * head, HD).astype(BF16)


def attention_probs(info, own, peer, recv, exch):
    rows = own.shape[0]
    width = recv.shape[1]
    heads = (own.shape[1] - width) // HD
    span_rows = SPAN_BLOCKS * rows
    whole = lambda a: pl.BlockSpec(a.shape, lambda h, info: (0,) * a.ndim)
    return pl.pallas_call(
        probs_kernel,
        out_shape=(
            jax.ShapeDtypeStruct((heads, rows, span_rows), BF16),
            jax.ShapeDtypeStruct((rows, heads * HD), F32),
            jax.ShapeDtypeStruct((rows, HD), BF16),
            jax.ShapeDtypeStruct((span_rows, width), BF16),
        ),
        grid_spec=pltpu.PrefetchScalarGridSpec(
            num_scalar_prefetch=1,
            grid=(heads,),
            in_specs=[whole(own), whole(peer), whole(recv), whole(exch)],
            out_specs=(
                pl.BlockSpec((1, rows, span_rows), lambda h, info: (h, 0, 0)),
                pl.BlockSpec((rows, HD), lambda h, info: (0, h)),
                pl.BlockSpec((rows, HD), lambda h, info: (0, 0)),
                pl.BlockSpec((span_rows, width), lambda h, info: (0, 0)),
            ),
        ),
        compiler_params=params(),
        cost_estimate=pl.CostEstimate(
            flops=4 * heads * rows * span_rows * HD, bytes_accessed=8 * 2**20, transcendentals=heads * rows * span_rows
        ),
        name="attention_probs",
    )(info, own, peer, recv, exch)


def dout_kernel(slots, info, *refs):
    count = len(slots)
    sources = refs[: sum(slots.values())]
    weight, mixed, stats, pay, acc = refs[len(sources) :]
    step = pl.program_id(0)
    parts = []
    at = 0
    for n in slots.values():
        part = sources[at][...]
        for other in sources[at + 1 : at + n]:
            part = part + other[...]
        parts.append(part)
        at += n
    block = parts[0] if count == 1 else jnp.concatenate(parts, axis=0)

    @pl.when(step == 0)
    def _():
        acc[...] = jnp.zeros_like(acc)

    acc[...] += dot(block, weight[...], NT)

    @pl.when(step == pl.num_programs(0) - 1)
    def _():
        heads = weight.shape[0] // HD
        part_rows = acc.shape[0] // count
        for n, slot in enumerate(slots):
            start = pl.multiple_of(info[2 + slot], 16)
            dout = acc[n * part_rows : (n + 1) * part_rows, :].astype(BF16)
            row_stats = stats[pl.ds(start, part_rows), :].astype(F32)
            out_rows = mixed[pl.ds(start, part_rows), :]
            for head in range(heads):
                cols = slice(head * HD, (head + 1) * HD)
                delta = jnp.sum(dout[:, cols].astype(F32) * out_rows[:, cols], axis=1, keepdims=True)
                row_stats = row_stats + spread(delta, 8 * head + 3, HD)
            pay[n * part_rows : (n + 1) * part_rows, : heads * HD] = dout
            pay[n * part_rows : (n + 1) * part_rows, heads * HD :] = row_stats.astype(BF16)


def dout_rows(info, slots, sources, weight, mixed, stats, steps=3):
    rows = sources[0].shape[0]
    total = rows * len(slots)
    depth = weight.shape[1] // steps
    heads = weight.shape[0] // HD
    whole = lambda a: pl.BlockSpec(a.shape, lambda s, info: (0,) * a.ndim)
    return pl.pallas_call(
        functools.partial(dout_kernel, slots),
        out_shape=jax.ShapeDtypeStruct((total, (heads + 1) * HD), BF16),
        grid_spec=pltpu.PrefetchScalarGridSpec(
            num_scalar_prefetch=1,
            grid=(steps,),
            in_specs=[pl.BlockSpec((rows, depth), lambda s, info: (0, s)) for _ in sources]
            + [pl.BlockSpec((weight.shape[0], depth), lambda s, info: (0, s)), whole(mixed), whole(stats)],
            out_specs=pl.BlockSpec((total, (heads + 1) * HD), lambda s, info: (0, 0)),
            scratch_shapes=[pltpu.VMEM((total, heads * HD), F32)],
        ),
        compiler_params=params(),
        cost_estimate=pl.CostEstimate(
            flops=2 * total * weight.size, bytes_accessed=2 * weight.size + 4 * total * weight.shape[1], transcendentals=0
        ),
        name="dout_rows",
    )(info, *sources, weight, mixed, stats)


def query_kernel(slots, info, pay, probs, span, *refs):
    head = pl.program_id(0)
    before, out = refs if len(refs) == 2 else (None, refs[0])
    heads = pl.num_programs(0)
    kv_width = span.shape[1] // 2
    group = head // 2
    key = span[:, pl.ds(pl.multiple_of(group * HD, HD), HD)]
    value = span[:, pl.ds(pl.multiple_of(kv_width + group * HD, HD), HD)]
    dout = pay[:, pl.ds(pl.multiple_of(head * HD, HD), HD)]
    extra = pay[:, pay.shape[1] - HD :]
    value_more = jnp.concatenate([value, minus_ones(value.shape[0], 8 * head + 3)], axis=1)
    centred = dot(jnp.concatenate([dout, extra], axis=1), value_more, NT)
    part_rows = pay.shape[0] // len(slots)
    if before is not None:
        out[...] = before[...]
    else:
        out[...] = jnp.zeros_like(out)
    parts = []
    for n, slot in enumerate(slots):
        start = pl.multiple_of(info[2 + slot], 16)
        weights = probs[0, pl.ds(start, part_rows), :].astype(F32)
        parts.append((weights * centred[n * part_rows : (n + 1) * part_rows, :]).astype(BF16))
    dscores = parts[0] if len(parts) == 1 else jnp.concatenate(parts, axis=0)
    grads = dot(dscores, key, NN) * SCALE
    for n, slot in enumerate(slots):
        start = pl.multiple_of(info[2 + slot], 16)
        out[pl.ds(start, part_rows), :] = grads[n * part_rows : (n + 1) * part_rows, :]


def query_grads(info, slots, pay, probs, span, before=None):
    heads, rows, span_rows = probs.shape
    whole = lambda a: pl.BlockSpec(a.shape, lambda h, info: (0,) * a.ndim)
    column = pl.BlockSpec((rows, HD), lambda h, info: (0, h))
    return pl.pallas_call(
        functools.partial(query_kernel, slots),
        out_shape=jax.ShapeDtypeStruct((rows, heads * HD), F32),
        grid_spec=pltpu.PrefetchScalarGridSpec(
            num_scalar_prefetch=1,
            grid=(heads,),
            in_specs=[whole(pay), pl.BlockSpec((1, rows, span_rows), lambda h, info: (h, 0, 0)), whole(span)]
            + ([] if before is None else [column]),
            out_specs=column,
        ),
        compiler_params=params(),
        cost_estimate=pl.CostEstimate(
            flops=4 * heads * pay.shape[0] * span_rows * HD, bytes_accessed=5 * 2**20, transcendentals=0
        ),
        name="query_grads",
    )(info, pay, probs, span, *(() if before is None else (before,)))


def key_kernel(
    slots, with_before, info, own, peer, recv_q, exch_q, pay, pay_peer, pay_recv, pay_exch, *refs
):
    if with_before:
        before_k, before_v, grad_k, grad_v, q_cat, d_cat = refs
    else:
        grad_k, grad_v, q_cat, d_cat = refs
    core = info[0]
    rows = own.shape[0]
    kv_width = grad_k.shape[1]
    width = recv_q.shape[1]
    q_at = own.shape[1] - width
    total = pay.shape[0]
    part_rows = total // len(slots)

    def put(distance, q_ref, q_row, q_col, d_ref, d_row):
        for n, slot in enumerate(slots):
            start = pl.multiple_of(info[2 + slot] + q_row, 16)
            at = distance * total + n * part_rows
            q_cat[at : at + part_rows, :] = q_ref[pl.ds(start, part_rows), q_col : q_col + width]
        d_cat[distance * total : (distance + 1) * total, :] = d_ref[d_row : d_row + total, :]

    put(0, own, 0, q_at, pay, 0)
    put(3, recv_q, rows, 0, pay_recv, total)

    @pl.when(core == 0)
    def _():
        put(1, peer, 0, q_at, pay_peer, 0)
        put(2, recv_q, 0, 0, pay_recv, 0)
        put(4, exch_q, rows, 0, pay_exch, total)

    @pl.when(core == 1)
    def _():
        put(1, exch_q, 0, 0, pay_exch, 0)
        put(2, exch_q, rows, 0, pay_exch, total)
        put(4, recv_q, 0, 0, pay_recv, 0)

    lanes = SPAN_BLOCKS * total
    lane = lax.broadcasted_iota(jnp.int32, (1, lanes), 1)
    low = jnp.zeros((1, lanes), jnp.int32)
    high = jnp.full((1, lanes), rows, jnp.int32)
    for n, slot in enumerate(slots):
        at = n * part_rows
        inside = (lane >= at) & (lane < at + part_rows)
        high = jnp.where(inside, lane - at + info[2 + slot], high)
        at = (SPAN_BLOCKS - 1) * total + n * part_rows
        inside = (lane >= at) & (lane < at + part_rows)
        low = jnp.where(inside, lane - at + info[2 + slot] + 1, low)
    key_row = lax.broadcasted_iota(jnp.int32, (rows, lanes), 0)
    allowed = (key_row >= low) & (key_row <= high)
    extra = d_cat[:, width:]
    for group in range(kv_width // HD):
        cols = slice(group * HD, (group + 1) * HD)
        key = own[:, group * HD : (group + 1) * HD]
        value = own[:, kv_width + group * HD : kv_width + (group + 1) * HD]
        sum_k = None
        sum_v = None
        for head in (2 * group, 2 * group + 1):
            query = q_cat[:, head * HD : (head + 1) * HD]
            dout = d_cat[:, head * HD : (head + 1) * HD]
            scores = dot(
                jnp.concatenate([key, minus_ones(rows, 8 * head)], axis=1),
                jnp.concatenate([query, extra], axis=1),
                NT,
            )
            probability = jnp.where(allowed, jnp.exp(scores * SCALE), 0.0)
            centred = dot(
                jnp.concatenate([value, minus_ones(rows, 8 * head + 3)], axis=1),
                jnp.concatenate([dout, extra], axis=1),
                NT,
            )
            dscores = (probability * centred).astype(BF16)
            term_v = dot(probability.astype(BF16), dout, NN)
            term_k = dot(dscores, query, NN)
            sum_v = term_v if sum_v is None else sum_v + term_v
            sum_k = term_k if sum_k is None else sum_k + term_k
        sum_k = sum_k * SCALE
        if with_before:
            sum_k = sum_k + before_k[:, cols]
            sum_v = sum_v + before_v[:, cols]
        grad_k[:, cols] = sum_k
        grad_v[:, cols] = sum_v


def key_grads(info, slots, own, peer, recv_q, exch_q, pays, before=()):
    rows = own.shape[0]
    width = recv_q.shape[1]
    kv_width = (own.shape[1] - width) // 2
    total = pays[0].shape[0]
    vmem = pl.BlockSpec(memory_space=pltpu.VMEM)
    arrays = (own, peer, recv_q, exch_q, *pays, *before)
    return pl.pallas_call(
        functools.partial(key_kernel, slots, bool(before)),
        out_shape=(jax.ShapeDtypeStruct((rows, kv_width), F32),) * 2,
        in_specs=[pl.BlockSpec(memory_space=pltpu.SMEM)] + [vmem] * len(arrays),
        out_specs=(vmem, vmem),
        scratch_shapes=[
            pltpu.VMEM((SPAN_BLOCKS * total, width), BF16),
            pltpu.VMEM((SPAN_BLOCKS * total, width + HD), BF16),
        ],
        compiler_params=params(),
        cost_estimate=pl.CostEstimate(
            flops=8 * rows * width * SPAN_BLOCKS * total, bytes_accessed=6 * 2**20, transcendentals=4 * rows * total * 5
        ),
        name="key_grads",
    )(info, *arrays)


def on_device(ctx, queries, keys, values, grad_out, out_weight):
    rows = queries.shape[0]
    slot_rows = grad_out.shape[0]
    width = queries.shape[1]
    chips = ctx // 2
    swap = [(i, i ^ 1) for i in range(ctx)]
    ahead = [(2 * c + k, 2 * (c + 1 + k) + k) for c in range(chips) for k in (0, 1) if c + 1 + k < chips]
    back = [(d, s) for s, d in ahead]
    along = lambda x, pairs: lax.ppermute(x, "ctx", pairs)
    over = lambda x, pairs: lax.ppermute(x, "tp", pairs)

    shard = lax.axis_index("ctx")
    tp = lax.axis_index("tp")
    low_side = tp < 2
    slot_at = [tp, tp ^ 1, jnp.where(low_side, 2, 1), jnp.where(low_side, 3, 0)]
    info = jnp.stack([shard % 2, shard] + [s * slot_rows for s in slot_at]).astype(jnp.int32)

    middle = [(1, 2), (2, 1)]
    ends = [(0, 1), (1, 0), (2, 3), (3, 2)]
    outward = [(1, 0), (2, 3)]
    mid_first = over(grad_out, middle)
    end_first = over(grad_out, ends)

    own = jnp.concatenate([keys, values, queries], axis=1)
    peer = along(own, swap)
    kv_width = own.shape[1] - width
    kv_pair = jnp.concatenate([own[:, :kv_width], peer[:, :kv_width]], axis=0)
    q_pair = jnp.concatenate([own[:, kv_width:], peer[:, kv_width:]], axis=0)
    recv_kv = along(kv_pair, ahead)
    recv_q = along(q_pair, back)
    exch_kv = along(recv_kv, swap)
    exch_q = along(recv_q, swap)

    out_second = over(mid_first, outward)
    mid_second = over(end_first, middle)
    out_third = over(mid_second, outward)

    probs, mixed, stats, span = attention_probs(info, own, peer, recv_kv, exch_kv)

    def send(pay):
        pay_peer = along(pay, swap)
        pay_recv = along(jnp.concatenate([pay, pay_peer], axis=0), back)
        pay_exch = along(pay_recv, swap)
        return pay, pay_peer, pay_recv, pay_exch

    pay = dout_rows(
        info, {0: 1, 1: 1, 2: 2}, [grad_out, end_first, mid_first, out_second], out_weight, mixed, stats
    )
    pays = send(pay)
    early = (0, 1, 2)
    grad_q = query_grads(info, early, pay, probs, span)
    before = key_grads(info, early, own, peer, recv_q, exch_q, pays)

    pay = dout_rows(info, {3: 2}, [mid_second, out_third], out_weight, mixed, stats)
    pays = send(pay)
    grad_q = query_grads(info, (3,), pay, probs, span, grad_q)
    grad_k, grad_v = key_grads(info, (3,), own, peer, recv_q, exch_q, pays, before)
    return (grad_q, grad_k, grad_v)


def solution(mesh):
    in_specs = (
        P("ctx", "tp"),
        P("ctx", "tp"),
        P("ctx", "tp"),
        P(("ctx", "tp"), None),
        P("tp", None),
    )
    out_specs = (P("ctx", "tp"), P("ctx", "tp"), P("ctx", "tp"))
    return jax.shard_map(
        functools.partial(on_device, mesh.shape["ctx"]),
        mesh=mesh,
        in_specs=in_specs,
        out_specs=out_specs,
        check_vma=False,
    )
```

```python
import functools

import jax
import jax.numpy as jnp
from jax import lax
from jax.experimental import pallas as pl
from jax.experimental.pallas import tpu as pltpu
from jax.sharding import PartitionSpec as P

HD = 128
WIN = 1024
SPAN_BLOCKS = 5
SCALE = 168.0 ** (-0.5)
NT = (((1,), (1,)), ((), ()))
NN = (((1,), (0,)), ((), ()))
F32 = jnp.float32
BF16 = jnp.bfloat16
VMEM = pl.BlockSpec(memory_space=pltpu.VMEM)
SMEM = pl.BlockSpec(memory_space=pltpu.SMEM)
ANY = pl.BlockSpec(memory_space=pl.ANY)
COST = pl.CostEstimate(flops=1, bytes_accessed=1, transcendentals=0)


def dot(a, b, dims):
    return lax.dot_general(a, b, dims, preferred_element_type=F32)


def params(limit=20):
    return pltpu.CompilerParams(vmem_limit_bytes=limit * 2**20)


def call(kernel, name, shapes, info, arrays, scratch=(), outs=VMEM, in_place=()):
    return pl.pallas_call(
        kernel,
        out_shape=shapes,
        in_specs=[SMEM] + [VMEM] * len(arrays) + [ANY] * len(in_place),
        out_specs=outs if isinstance(outs, tuple) else jax.tree.map(lambda _: outs, shapes),
        scratch_shapes=list(scratch),
        input_output_aliases={1 + len(arrays) + n: n for n in range(len(in_place))},
        compiler_params=params(),
        cost_estimate=COST,
        name=name,
    )(info, *arrays, *in_place)


TOKEN = jax.ShapeDtypeStruct((8, HD), F32)


def pack_kernel(places, *refs):
    sources, outs, sems = refs[: len(places)], refs[len(places) : -1], refs[-1]
    copies = []
    for n, (source, (out, row, col)) in enumerate(zip(sources, places)):
        first, last, at = (0, source.shape[1], col) if isinstance(col, int) else (*col, 0)
        target = outs[out].at[row : row + source.shape[0], at : at + last - first]
        copies.append(pltpu.make_async_copy(source.at[:, first:last], target, sems.at[n]))
    for copy in copies:
        copy.start()
    for copy in copies:
        copy.wait()


def pack(arrays, places, shapes, limit=20, outs=ANY):
    return pl.pallas_call(
        functools.partial(pack_kernel, places),
        out_shape=tuple(jax.ShapeDtypeStruct(shape, BF16) for shape in shapes),
        in_specs=[ANY] * len(arrays),
        out_specs=(outs,) * len(shapes),
        scratch_shapes=[pltpu.SemaphoreType.DMA((len(arrays),))],
        compiler_params=params(limit),
        cost_estimate=COST,
        name="pack",
    )(*arrays)


def pair_kernel(nearer, count, info, *refs):
    own, near, far = (refs[n * count : (n + 1) * count] for n in range(3))
    pair = refs[-1]
    total = pair.shape[0] // 2

    def put(at, blocks):
        for block in blocks:
            pair[at : at + block.shape[0], :] = block[...]
            at += block.shape[0]

    @pl.when(info[0] == nearer)
    def _():
        put(0, own)
        put(total, near)

    @pl.when(info[0] != nearer)
    def _():
        put(0, near)
        put(total, far)


def pair_for_peer(info, nearer, own, near, far, after=()):
    total = sum(block.shape[0] for block in own)
    shape = jax.ShapeDtypeStruct((2 * total, own[0].shape[1]), BF16)
    kernel = functools.partial(pair_kernel, nearer, len(own))
    return call(kernel, "pair", shape, info, (*own, *near, *far, *after))


def pieces(x):
    hi = x.astype(BF16)
    rest = x - hi.astype(F32)
    mid = rest.astype(BF16)
    low = (rest - mid.astype(F32)).astype(BF16)
    return hi.astype(F32), mid.astype(F32), low.astype(F32)


def spread(x, first, into):
    lane = lax.broadcasted_iota(jnp.int32, into.shape, 1)
    for n, piece in enumerate(pieces(x)):
        into = jnp.where(lane == first + n, piece, into)
    return into


def minus_ones(rows, first):
    lane = lax.broadcasted_iota(jnp.int32, (rows, HD), 1)
    return jnp.where((lane >= first) & (lane < first + 3), -1.0, 0.0).astype(BF16)


def stacked(refs):
    blocks = [ref[...] for ref in refs]
    return blocks[0] if len(blocks) == 1 else jnp.concatenate(blocks, axis=0)


def head_cols(head):
    return slice(head * HD, (head + 1) * HD)


def probs_kernel(info, kv, query, near, far, odd, *refs):
    probs, mixed, stats, span = refs[-4:]
    rows, kv_width = kv.shape[0], kv.shape[1] // 2
    heads = query.shape[1] // HD
    shard = info[1]

    span[:rows, :] = far[...]
    span[rows : 2 * rows, :] = odd[rows:, :]
    span[2 * rows : 3 * rows, :] = near[...]
    span[3 * rows : 4 * rows, :] = odd[:rows, :]
    span[4 * rows :, :] = kv[...]

    span_rows = span.shape[0]
    row = lax.broadcasted_iota(jnp.int32, (rows, 1), 0)
    col = lax.broadcasted_iota(jnp.int32, (rows, span_rows), 1)
    first = jnp.maximum(row + 1, (SPAN_BLOCKS - 1 - shard) * rows)
    allowed = (col >= first) & (col <= row + WIN)
    row_stats = jnp.zeros((rows, HD), F32)
    for head in range(heads):
        group = head // 2
        scores = dot(query[:, head_cols(head)], span[:, head_cols(group)], NT) * SCALE
        scores = jnp.where(allowed, scores, -1e30)
        top = jnp.max(scores, axis=1, keepdims=True)
        weights = jnp.exp(scores - top)
        total = jnp.sum(weights, axis=1, keepdims=True)
        probability = (weights * (1.0 / total)).astype(BF16)
        probs[head] = probability
        value_span = span[:, kv_width + group * HD : kv_width + (group + 1) * HD]
        mixed[:, head_cols(head)] = dot(probability, value_span, NN)
        level = (top + jnp.log(total)) * (1.0 / SCALE)
        row_stats = spread(level, 8 * head, row_stats)
    stats[...] = row_stats.astype(BF16)


def attention_probs(info, kv, query, near, far, odd, after):
    rows, width = query.shape
    span_rows = SPAN_BLOCKS * rows
    shapes = (
        jax.ShapeDtypeStruct((width // HD, rows, span_rows), BF16),
        jax.ShapeDtypeStruct((rows, width), F32),
        jax.ShapeDtypeStruct((rows, HD), BF16),
        jax.ShapeDtypeStruct((span_rows, kv.shape[1]), BF16),
    )
    arrays = (kv, query, near, far, odd, *after)
    return call(probs_kernel, "attention_probs", shapes, info, arrays)


def finish_rows(info, slot, product, mixed, stats, pay, at):
    rows, width = product.shape
    start = pl.multiple_of(info[2 + slot], 16)
    dout = product.astype(BF16)
    row_stats = stats[pl.ds(start, rows), :].astype(F32)
    out_rows = mixed[pl.ds(start, rows), :]
    for head in range(width // HD):
        cols = head_cols(head)
        delta = jnp.sum(dout[:, cols].astype(F32) * out_rows[:, cols], axis=1, keepdims=True)
        row_stats = spread(delta, 8 * head + 3, row_stats)
    pay[at : at + rows, :width] = dout
    pay[at : at + rows, width:] = row_stats.astype(BF16)


def dout_kernel(slots, info, *refs):
    sources = refs[: sum(slots.values())]
    weight, mixed, stats = refs[len(sources) : len(sources) + 3]
    pay = refs[-1]
    rows = sources[0].shape[0]
    parts = []
    at = 0
    for n in slots.values():
        part = sources[at][...]
        for other in sources[at + 1 : at + n]:
            part = part + other[...]
        parts.append(part)
        at += n
    product = dot(jnp.concatenate(parts, axis=0), weight[...], NT)
    for n, slot in enumerate(slots):
        finish_rows(info, slot, product[n * rows : (n + 1) * rows], mixed, stats, pay, n * rows)


def dout_rows(info, slots, sources, weight, mixed, stats, after=()):
    total = sources[0].shape[0] * len(slots)
    shape = jax.ShapeDtypeStruct((total, weight.shape[0] + HD), BF16)
    arrays = (*sources, weight, mixed, stats, *after)
    return call(functools.partial(dout_kernel, slots), "dout_rows", shape, info, arrays)


def query_kernel(slots, count, info, probs, span, *refs):
    out, done, held, sems = refs[-4:]
    done[...] = jnp.zeros_like(done)
    pay = stacked(refs[:count])
    heads, rows, _ = probs.shape
    kv_width = span.shape[1] // 2
    total = pay.shape[0]
    part_rows = total // len(slots)
    starts = [pl.multiple_of(info[2 + slot], 16) for slot in slots]
    extra = pay[:, heads * HD :].astype(F32)
    lane = lax.broadcasted_iota(jnp.int32, extra.shape, 1)
    for group in range(heads // 2):
        key = span[:, head_cols(group)]
        value = span[:, kv_width + group * HD : kv_width + (group + 1) * HD]
        pair = (2 * group, 2 * group + 1)
        dprobs = dot(jnp.concatenate([pay[:, head_cols(head)] for head in pair], axis=0), value, NT)
        parts = []
        for m, head in enumerate(pair):
            first = 8 * head + 3
            delta = jnp.sum(
                jnp.where((lane >= first) & (lane < first + 3), extra, 0.0), axis=1, keepdims=True
            )
            for n, start in enumerate(starts):
                at = m * total + n * part_rows
                weights = probs[head, pl.ds(start, part_rows), :].astype(F32)
                centred = dprobs[at : at + part_rows, :] - delta[n * part_rows : (n + 1) * part_rows]
                parts.append((weights * centred).astype(BF16))
        grads = dot(jnp.concatenate(parts, axis=0), key, NN) * SCALE
        for m, head in enumerate(pair):
            held[:, head_cols(head)] = grads[m * total : (m + 1) * total, :]
    copies = [
        pltpu.make_async_copy(
            held.at[n * part_rows : (n + 1) * part_rows, :],
            out.at[pl.ds(start, part_rows), :],
            sems.at[n],
        )
        for n, start in enumerate(starts)
    ]
    for copy in copies:
        copy.start()
    for copy in copies:
        copy.wait()


def query_grads(info, slots, pays, probs, span, before=()):
    heads, rows, _ = probs.shape
    total = sum(pay.shape[0] for pay in pays)
    return call(
        functools.partial(query_kernel, slots, len(pays)),
        "query_grads",
        (
            jax.ShapeDtypeStruct((rows, heads * HD), F32),
            TOKEN,
        ),
        info,
        (probs, span, *pays),
        [pltpu.VMEM((total, heads * HD), F32), pltpu.SemaphoreType.DMA((len(slots),))],
        outs=(ANY, VMEM),
        in_place=before,
    )


def key_kernel(slots, blocks, q_count, d_count, info, kv, *refs):
    q_refs, d_refs = refs[:q_count], refs[q_count : q_count + d_count]
    before = refs[q_count + d_count : -7]
    grad_k, grad_v, q_cat, d_cat, held_k, held_v, sems = refs[-7:]
    rows, kv_width = kv.shape[0], kv.shape[1] // 2
    width = q_cat.shape[1]
    lanes = q_cat.shape[0]
    total = lanes // len(blocks)
    part_rows = total // len(slots)
    lane = lax.broadcasted_iota(jnp.int32, (1, lanes), 1)
    low = jnp.zeros((1, lanes), jnp.int32)
    high = jnp.full((1, lanes), rows, jnp.int32)
    for m, (distance, q_at, q_row, d_at, d_row) in enumerate(blocks):
        at = m * total
        for slot in slots:
            start = pl.multiple_of(info[2 + slot], 16)
            q_cat[at : at + part_rows, :] = q_refs[q_at][pl.ds(start + q_row, part_rows), :]
            inside = (lane >= at) & (lane < at + part_rows)
            if distance == 0:
                high = jnp.where(inside, lane - at + start, high)
            if distance == SPAN_BLOCKS - 1:
                low = jnp.where(inside, lane - at + start + 1, low)
            at += part_rows
        at = m * total
        for n in d_at:
            size = min(d_refs[n].shape[0], total)
            d_cat[at : at + size, :] = d_refs[n][d_row : d_row + size, :]
            at += size

    masked = any(block[0] in (0, SPAN_BLOCKS - 1) for block in blocks)
    key_row = lax.broadcasted_iota(jnp.int32, (rows, lanes), 0)
    allowed = (key_row >= low) & (key_row <= high)
    extra = d_cat[:, width:]
    copies = []
    for group in range(kv_width // HD):
        cols = head_cols(group)
        key = kv[:, cols]
        value = kv[:, kv_width + group * HD : kv_width + (group + 1) * HD]
        sum_k = None
        sum_v = None
        for head in (2 * group, 2 * group + 1):
            queries = q_cat[:, head_cols(head)]
            dout = d_cat[:, head_cols(head)]
            scores = dot(
                jnp.concatenate([key, minus_ones(rows, 8 * head)], axis=1),
                jnp.concatenate([queries, extra], axis=1),
                NT,
            )
            probability = jnp.exp(scores * SCALE)
            if masked:
                probability = jnp.where(allowed, probability, 0.0)
            centred = dot(
                jnp.concatenate([value, minus_ones(rows, 8 * head + 3)], axis=1),
                jnp.concatenate([dout, extra], axis=1),
                NT,
            )
            dscores = (probability * centred).astype(BF16)
            term_v = dot(probability.astype(BF16), dout, NN)
            term_k = dot(dscores, queries, NN)
            sum_v = term_v if sum_v is None else sum_v + term_v
            sum_k = term_k if sum_k is None else sum_k + term_k
        sum_k = sum_k * SCALE
        if before:
            sum_k = sum_k + before[0][:, cols]
            sum_v = sum_v + before[1][:, cols]
        held_k[:, cols] = sum_k
        held_v[:, cols] = sum_v
        for n, (held, out) in enumerate(((held_k, grad_k), (held_v, grad_v))):
            copy = pltpu.make_async_copy(held.at[:, cols], out.at[:, cols], sems.at[2 * group + n])
            copy.start()
            copies.append(copy)
    for copy in copies:
        copy.wait()


def key_grads(info, slots, blocks, kv, q_arrays, d_arrays, total, before=()):
    lanes = len(blocks) * total
    width = q_arrays[0].shape[1]
    kv_width = kv.shape[1] // 2
    shape = jax.ShapeDtypeStruct((kv.shape[0], kv_width), F32)
    held = pltpu.VMEM(shape.shape, F32)
    return call(
        functools.partial(key_kernel, slots, blocks, len(q_arrays), len(d_arrays)),
        "key_grads",
        (shape, shape),
        info,
        (kv, *q_arrays, *d_arrays, *before),
        [
            pltpu.VMEM((lanes, width), BF16),
            pltpu.VMEM((lanes, width + HD), BF16),
            held,
            held,
            pltpu.SemaphoreType.DMA((2 * (kv_width // HD),)),
        ],
        outs=ANY,
    )


def on_device(ctx, queries, keys, values, grad_out, out_weight):
    rows, width = queries.shape
    kv_width = 2 * keys.shape[1]
    slot_rows = grad_out.shape[0]
    swap = [(i, i ^ 1) for i in range(ctx)]

    def along(x, pairs, name):
        with jax.named_scope(name):
            return lax.ppermute(x, "ctx", pairs)

    def over(x, pairs, name):
        with jax.named_scope(name):
            return lax.ppermute(x, "tp", pairs)

    def moved(distance):
        return [(i, i + distance) for i in range(ctx) if 0 <= i + distance < ctx]

    shard = lax.axis_index("ctx")
    tp = lax.axis_index("tp")
    low_side = tp < 2
    slot_at = [tp, tp ^ 1, jnp.where(low_side, 2, 1), jnp.where(low_side, 3, 0)]
    info = jnp.stack([shard % 2, shard] + [s * slot_rows for s in slot_at]).astype(jnp.int32)

    middle = [(1, 2), (2, 1)]
    ends = [(0, 1), (1, 0), (2, 3), (3, 2)]
    outward = [(1, 0), (2, 3)]
    mid_first = over(grad_out, middle, "mid_first")
    end_first = over(grad_out, ends, "end_first")
    mid_second = over(end_first, middle, "mid_second")
    out_second = over(mid_first, outward, "out_second")

    kv, query = pack(
        [keys, values, queries],
        [(0, 0, 0), (0, 0, kv_width // 2), (1, 0, 0)],
        [(rows, kv_width), (rows, width)],
        limit=56,
        outs=VMEM,
    )
    near_kv = along(kv, moved(2), "kv_near")
    far_kv = along(kv, moved(4), "kv_far")
    near_q = along(query, moved(-2), "q_near")
    far_q = along(query, moved(-4), "q_far")
    odd_kv = along(pair_for_peer(info, 0, [kv], [near_kv], [far_kv]), swap, "kv_swap")
    odd_q = along(pair_for_peer(info, 1, [query], [near_q], [far_q]), swap, "q_swap")


    probs, mixed, stats, span = attention_probs(
        info, kv, query, near_kv, far_kv, odd_kv, (odd_q,)
    )

    def sent(pay, name):
        near = along(pay, moved(-2), name + "_near")
        far = along(pay, moved(-4), name + "_far")
        return near, far

    mid_second, out_second, stats = lax.optimization_barrier((mid_second, out_second, stats))
    out_third = over(mid_second, outward, "out_third")
    statistics = (out_weight, mixed, stats)
    early, late = {0: 1, 1: 1, 2: 2}, {3: 2}
    pay_a = dout_rows(info, early, (grad_out, end_first, mid_first, out_second), *statistics)
    near_a, far_a = sent(pay_a, "early")
    grad_q, queries_done = query_grads(info, early, (pay_a,), probs, span)

    pay_b = dout_rows(info, late, (mid_second, out_third), *statistics, (queries_done,))
    near_b, far_b = sent(pay_b, "late")
    grad_q, queries_done = query_grads(info, late, (pay_b,), probs, span, (grad_q,))
    pays = ((pay_a, pay_b), (near_a, near_b), (far_a, far_b))
    pair = pair_for_peer(info, 1, *pays, (queries_done,))
    odd = along(pair, swap, "pay_swap")
    slots = (0, 1, 2, 3)
    even_blocks = ((0, 0, 0, (0, 1), 0), (2, 1, 0, (2, 3), 0), (4, 2, 0, (4, 5), 0))
    even = key_grads(
        info, slots, even_blocks, kv, (query, near_q, far_q), sum(pays, ()), rows
    )
    odd_blocks = ((1, 0, 0, (0,), 0), (3, 0, rows, (0,), rows))
    grad_k, grad_v = key_grads(info, slots, odd_blocks, kv, (odd_q,), (odd,), rows, even)
    return (grad_q, grad_k, grad_v)


def solution(mesh):
    in_specs = (
        P("ctx", "tp"),
        P("ctx", "tp"),
        P("ctx", "tp"),
        P(("ctx", "tp"), None),
        P("tp", None),
    )
    out_specs = (P("ctx", "tp"), P("ctx", "tp"), P("ctx", "tp"))
    return jax.shard_map(
        functools.partial(on_device, mesh.shape["ctx"]),
        mesh=mesh,
        in_specs=in_specs,
        out_specs=out_specs,
        check_vma=False,
    )
```

```python
import functools

import jax
import jax.numpy as jnp
from jax import lax
from jax.experimental import pallas as pl
from jax.experimental.pallas import tpu as pltpu
from jax.sharding import PartitionSpec as P

HD = 128
WIN = 1024
SPAN_BLOCKS = 5
SCALE = 168.0 ** (-0.5)
NT = (((1,), (1,)), ((), ()))
NN = (((1,), (0,)), ((), ()))
F32 = jnp.float32
BF16 = jnp.bfloat16
VMEM = pl.BlockSpec(memory_space=pltpu.VMEM)
SMEM = pl.BlockSpec(memory_space=pltpu.SMEM)
ANY = pl.BlockSpec(memory_space=pl.ANY)
COST = pl.CostEstimate(flops=1, bytes_accessed=1, transcendentals=0)


def dot(a, b, dims):
    return lax.dot_general(a, b, dims, preferred_element_type=F32)


def params(limit=20):
    return pltpu.CompilerParams(vmem_limit_bytes=limit * 2**20)


def call(kernel, name, shapes, info, arrays, scratch=(), outs=VMEM, in_place=()):
    return pl.pallas_call(
        kernel,
        out_shape=shapes,
        in_specs=[SMEM] + [VMEM] * len(arrays) + [ANY] * len(in_place),
        out_specs=outs if isinstance(outs, tuple) else jax.tree.map(lambda _: outs, shapes),
        scratch_shapes=list(scratch),
        input_output_aliases={1 + len(arrays) + n: n for n in range(len(in_place))},
        compiler_params=params(),
        cost_estimate=COST,
        name=name,
    )(info, *arrays, *in_place)


TOKEN = jax.ShapeDtypeStruct((8, HD), F32)


def token_kernel(*refs):
    refs[-1][...] = jnp.zeros_like(refs[-1])


def token_of(*arrays):
    return pl.pallas_call(
        token_kernel,
        out_shape=TOKEN,
        in_specs=[ANY] * len(arrays),
        out_specs=VMEM,
        compiler_params=params(),
        cost_estimate=pl.CostEstimate(flops=2 * 10**9, bytes_accessed=1, transcendentals=0),
        name="token",
    )(*arrays)


def pack_kernel(places, *refs):
    sources, outs, sems = refs[: len(places)], refs[len(places) : -1], refs[-1]
    copies = []
    for n, (source, (out, row, col)) in enumerate(zip(sources, places)):
        first, last, at = (0, source.shape[1], col) if isinstance(col, int) else (*col, 0)
        target = outs[out].at[row : row + source.shape[0], at : at + last - first]
        copies.append(pltpu.make_async_copy(source.at[:, first:last], target, sems.at[n]))
    for copy in copies:
        copy.start()
    for copy in copies:
        copy.wait()


def pack(arrays, places, shapes, limit=20, outs=ANY):
    return pl.pallas_call(
        functools.partial(pack_kernel, places),
        out_shape=tuple(jax.ShapeDtypeStruct(shape, BF16) for shape in shapes),
        in_specs=[ANY] * len(arrays),
        out_specs=(outs,) * len(shapes),
        scratch_shapes=[pltpu.SemaphoreType.DMA((len(arrays),))],
        compiler_params=params(limit),
        cost_estimate=COST,
        name="pack",
    )(*arrays)


def pair_kernel(nearer, count, info, *refs):
    own, near, far = (refs[n * count : (n + 1) * count] for n in range(3))
    pair = refs[-1]
    total = pair.shape[0] // 2

    def put(at, blocks):
        for block in blocks:
            pair[at : at + block.shape[0], :] = block[...]
            at += block.shape[0]

    @pl.when(info[0] == nearer)
    def _():
        put(0, own)
        put(total, near)

    @pl.when(info[0] != nearer)
    def _():
        put(0, near)
        put(total, far)


def pair_for_peer(info, nearer, own, near, far, after=()):
    total = sum(block.shape[0] for block in own)
    shape = jax.ShapeDtypeStruct((2 * total, own[0].shape[1]), BF16)
    kernel = functools.partial(pair_kernel, nearer, len(own))
    return call(kernel, "pair", shape, info, (*own, *near, *far, *after))


def pieces(x):
    hi = x.astype(BF16)
    rest = x - hi.astype(F32)
    mid = rest.astype(BF16)
    low = (rest - mid.astype(F32)).astype(BF16)
    return hi.astype(F32), mid.astype(F32), low.astype(F32)


def spread(x, first, into):
    lane = lax.broadcasted_iota(jnp.int32, into.shape, 1)
    for n, piece in enumerate(pieces(x)):
        into = jnp.where(lane == first + n, piece, into)
    return into


def minus_ones(rows, first):
    lane = lax.broadcasted_iota(jnp.int32, (rows, HD), 1)
    return jnp.where((lane >= first) & (lane < first + 3), -1.0, 0.0).astype(BF16)


def stacked(refs):
    blocks = [ref[...] for ref in refs]
    return blocks[0] if len(blocks) == 1 else jnp.concatenate(blocks, axis=0)


def head_cols(head):
    return slice(head * HD, (head + 1) * HD)


def probs_kernel(info, kv, query, near, far, odd, *refs):
    probs, mixed, stats, span = refs[-4:]
    rows, kv_width = kv.shape[0], kv.shape[1] // 2
    heads = query.shape[1] // HD
    shard = info[1]

    span[:rows, :] = far[...]
    span[rows : 2 * rows, :] = odd[rows:, :]
    span[2 * rows : 3 * rows, :] = near[...]
    span[3 * rows : 4 * rows, :] = odd[:rows, :]
    span[4 * rows :, :] = kv[...]

    span_rows = span.shape[0]
    row = lax.broadcasted_iota(jnp.int32, (rows, 1), 0)
    col = lax.broadcasted_iota(jnp.int32, (rows, span_rows), 1)
    first = jnp.maximum(row + 1, (SPAN_BLOCKS - 1 - shard) * rows)
    allowed = (col >= first) & (col <= row + WIN)
    row_stats = jnp.zeros((rows, HD), F32)
    for head in range(heads):
        group = head // 2
        scores = dot(query[:, head_cols(head)], span[:, head_cols(group)], NT) * SCALE
        scores = jnp.where(allowed, scores, -1e30)
        top = jnp.max(scores, axis=1, keepdims=True)
        weights = jnp.exp(scores - top)
        total = jnp.sum(weights, axis=1, keepdims=True)
        probability = (weights * (1.0 / total)).astype(BF16)
        probs[head] = probability
        value_span = span[:, kv_width + group * HD : kv_width + (group + 1) * HD]
        mixed[:, head_cols(head)] = dot(probability, value_span, NN)
        level = (top + jnp.log(total)) * (1.0 / SCALE)
        row_stats = spread(level, 8 * head, row_stats)
    stats[...] = row_stats.astype(BF16)


def attention_probs(info, kv, query, near, far, odd, after):
    rows, width = query.shape
    span_rows = SPAN_BLOCKS * rows
    shapes = (
        jax.ShapeDtypeStruct((width // HD, rows, span_rows), BF16),
        jax.ShapeDtypeStruct((rows, width), F32),
        jax.ShapeDtypeStruct((rows, HD), BF16),
        jax.ShapeDtypeStruct((span_rows, kv.shape[1]), BF16),
    )
    arrays = (kv, query, near, far, odd, *after)
    return call(probs_kernel, "attention_probs", shapes, info, arrays)


def finish_rows(info, slot, product, mixed, stats, pay, at):
    rows, width = product.shape
    start = pl.multiple_of(info[2 + slot], 16)
    dout = product.astype(BF16)
    row_stats = stats[pl.ds(start, rows), :].astype(F32)
    out_rows = mixed[pl.ds(start, rows), :]
    for head in range(width // HD):
        cols = head_cols(head)
        delta = jnp.sum(dout[:, cols].astype(F32) * out_rows[:, cols], axis=1, keepdims=True)
        row_stats = spread(delta, 8 * head + 3, row_stats)
    pay[at : at + rows, :width] = dout
    pay[at : at + rows, width:] = row_stats.astype(BF16)


def dout_kernel(slots, info, *refs):
    sources = refs[: sum(slots.values())]
    weight, mixed, stats = refs[len(sources) : len(sources) + 3]
    pay = refs[-1]
    rows = sources[0].shape[0]
    parts = []
    at = 0
    for n in slots.values():
        part = sources[at][...]
        for other in sources[at + 1 : at + n]:
            part = part + other[...]
        parts.append(part)
        at += n
    product = dot(jnp.concatenate(parts, axis=0), weight[...], NT)
    for n, slot in enumerate(slots):
        finish_rows(info, slot, product[n * rows : (n + 1) * rows], mixed, stats, pay, n * rows)


def dout_rows(info, slots, sources, weight, mixed, stats, after=()):
    total = sources[0].shape[0] * len(slots)
    shape = jax.ShapeDtypeStruct((total, weight.shape[0] + HD), BF16)
    arrays = (*sources, weight, mixed, stats, *after)
    return call(functools.partial(dout_kernel, slots), "dout_rows", shape, info, arrays)


def query_kernel(slots, count, info, probs, span, *refs):
    out, done, held, sems = refs[-4:]
    done[...] = jnp.zeros_like(done)
    pay = stacked(refs[:count])
    heads, rows, _ = probs.shape
    kv_width = span.shape[1] // 2
    total = pay.shape[0]
    part_rows = total // len(slots)
    starts = [pl.multiple_of(info[2 + slot], 16) for slot in slots]
    extra = pay[:, heads * HD :].astype(F32)
    lane = lax.broadcasted_iota(jnp.int32, extra.shape, 1)
    for group in range(heads // 2):
        key = span[:, head_cols(group)]
        value = span[:, kv_width + group * HD : kv_width + (group + 1) * HD]
        pair = (2 * group, 2 * group + 1)
        dprobs = dot(jnp.concatenate([pay[:, head_cols(head)] for head in pair], axis=0), value, NT)
        parts = []
        for m, head in enumerate(pair):
            first = 8 * head + 3
            delta = jnp.sum(
                jnp.where((lane >= first) & (lane < first + 3), extra, 0.0), axis=1, keepdims=True
            )
            for n, start in enumerate(starts):
                at = m * total + n * part_rows
                weights = probs[head, pl.ds(start, part_rows), :].astype(F32)
                centred = dprobs[at : at + part_rows, :] - delta[n * part_rows : (n + 1) * part_rows]
                parts.append((weights * centred).astype(BF16))
        grads = dot(jnp.concatenate(parts, axis=0), key, NN) * SCALE
        for m, head in enumerate(pair):
            held[:, head_cols(head)] = grads[m * total : (m + 1) * total, :]
    copies = [
        pltpu.make_async_copy(
            held.at[n * part_rows : (n + 1) * part_rows, :],
            out.at[pl.ds(start, part_rows), :],
            sems.at[n],
        )
        for n, start in enumerate(starts)
    ]
    for copy in copies:
        copy.start()
    for copy in copies:
        copy.wait()


def query_grads(info, slots, pays, probs, span, before=()):
    heads, rows, _ = probs.shape
    total = sum(pay.shape[0] for pay in pays)
    return call(
        functools.partial(query_kernel, slots, len(pays)),
        "query_grads",
        (
            jax.ShapeDtypeStruct((rows, heads * HD), F32),
            TOKEN,
        ),
        info,
        (probs, span, *pays),
        [pltpu.VMEM((total, heads * HD), F32), pltpu.SemaphoreType.DMA((len(slots),))],
        outs=(ANY, VMEM),
        in_place=before,
    )


def key_kernel(blocks, q_count, d_count, info, kv, *refs):
    q_refs, d_refs = refs[:q_count], refs[q_count : q_count + d_count]
    before = refs[q_count + d_count : -7]
    grad_k, grad_v, q_cat, d_cat, held_k, held_v, sems = refs[-7:]
    rows, kv_width = kv.shape[0], kv.shape[1] // 2
    width = q_cat.shape[1]
    lanes = q_cat.shape[0]
    part_rows = lanes // sum(len(block[1]) for block in blocks)
    lane = lax.broadcasted_iota(jnp.int32, (1, lanes), 1)
    low = jnp.zeros((1, lanes), jnp.int32)
    high = jnp.full((1, lanes), rows, jnp.int32)
    at = 0
    for distance, slots, q_at, q_row, d_at, d_row in blocks:
        size = len(slots) * part_rows
        d_cat[at : at + size, :] = d_refs[d_at][d_row : d_row + size, :]
        for slot in slots:
            start = pl.multiple_of(info[2 + slot], 16)
            q_cat[at : at + part_rows, :] = q_refs[q_at][pl.ds(start + q_row, part_rows), :]
            inside = (lane >= at) & (lane < at + part_rows)
            if distance == 0:
                high = jnp.where(inside, lane - at + start, high)
            if distance == SPAN_BLOCKS - 1:
                low = jnp.where(inside, lane - at + start + 1, low)
            at += part_rows

    masked = any(block[0] in (0, SPAN_BLOCKS - 1) for block in blocks)
    key_row = lax.broadcasted_iota(jnp.int32, (rows, lanes), 0)
    allowed = (key_row >= low) & (key_row <= high)
    extra = d_cat[:, width:]
    copies = []
    for group in range(kv_width // HD):
        cols = head_cols(group)
        key = kv[:, cols]
        value = kv[:, kv_width + group * HD : kv_width + (group + 1) * HD]
        sum_k = None
        sum_v = None
        for head in (2 * group, 2 * group + 1):
            queries = q_cat[:, head_cols(head)]
            dout = d_cat[:, head_cols(head)]
            scores = dot(
                jnp.concatenate([key, minus_ones(rows, 8 * head)], axis=1),
                jnp.concatenate([queries, extra], axis=1),
                NT,
            )
            probability = jnp.exp(scores * SCALE)
            if masked:
                probability = jnp.where(allowed, probability, 0.0)
            centred = dot(
                jnp.concatenate([value, minus_ones(rows, 8 * head + 3)], axis=1),
                jnp.concatenate([dout, extra], axis=1),
                NT,
            )
            dscores = (probability * centred).astype(BF16)
            term_v = dot(probability.astype(BF16), dout, NN)
            term_k = dot(dscores, queries, NN)
            sum_v = term_v if sum_v is None else sum_v + term_v
            sum_k = term_k if sum_k is None else sum_k + term_k
        sum_k = sum_k * SCALE
        if before:
            sum_k = sum_k + before[0][:, cols]
            sum_v = sum_v + before[1][:, cols]
        held_k[:, cols] = sum_k
        held_v[:, cols] = sum_v
        for n, (held, out) in enumerate(((held_k, grad_k), (held_v, grad_v))):
            copy = pltpu.make_async_copy(held.at[:, cols], out.at[:, cols], sems.at[2 * group + n])
            copy.start()
            copies.append(copy)
    for copy in copies:
        copy.wait()


def key_grads(info, blocks, kv, q_arrays, d_arrays, slot_rows, before=()):
    lanes = sum(len(block[1]) for block in blocks) * slot_rows
    width = q_arrays[0].shape[1]
    kv_width = kv.shape[1] // 2
    shape = jax.ShapeDtypeStruct((kv.shape[0], kv_width), F32)
    held = pltpu.VMEM(shape.shape, F32)
    return call(
        functools.partial(key_kernel, blocks, len(q_arrays), len(d_arrays)),
        "key_grads",
        (shape, shape),
        info,
        (kv, *q_arrays, *d_arrays, *before),
        [
            pltpu.VMEM((lanes, width), BF16),
            pltpu.VMEM((lanes, width + HD), BF16),
            held,
            held,
            pltpu.SemaphoreType.DMA((2 * (kv_width // HD),)),
        ],
        outs=ANY,
    )


def on_device(ctx, queries, keys, values, grad_out, out_weight):
    rows, width = queries.shape
    kv_width = 2 * keys.shape[1]
    slot_rows = grad_out.shape[0]
    swap = [(i, i ^ 1) for i in range(ctx)]

    def along(x, pairs, name):
        with jax.named_scope(name):
            return lax.ppermute(x, "ctx", pairs)

    def over(x, pairs, name):
        with jax.named_scope(name):
            return lax.ppermute(x, "tp", pairs)

    def moved(distance):
        return [(i, i + distance) for i in range(ctx) if 0 <= i + distance < ctx]

    shard = lax.axis_index("ctx")
    tp = lax.axis_index("tp")
    low_side = tp < 2
    slot_at = [tp, tp ^ 1, jnp.where(low_side, 2, 1), jnp.where(low_side, 3, 0)]
    info = jnp.stack([shard % 2, shard] + [s * slot_rows for s in slot_at]).astype(jnp.int32)

    middle = [(1, 2), (2, 1)]
    ends = [(0, 1), (1, 0), (2, 3), (3, 2)]
    outward = [(1, 0), (2, 3)]
    mid_first = over(grad_out, middle, "mid_first")
    end_first = over(grad_out, ends, "end_first")
    mid_second = over(end_first, middle, "mid_second")
    out_second = over(mid_first, outward, "out_second")

    kv, query = pack(
        [keys, values, queries],
        [(0, 0, 0), (0, 0, kv_width // 2), (1, 0, 0)],
        [(rows, kv_width), (rows, width)],
        limit=56,
        outs=VMEM,
    )
    near_kv = along(kv, moved(2), "kv_near")
    far_kv = along(kv, moved(4), "kv_far")
    near_q = along(query, moved(-2), "q_near")
    far_q = along(query, moved(-4), "q_far")
    odd_kv = along(pair_for_peer(info, 0, [kv], [near_kv], [far_kv]), swap, "kv_swap")
    odd_q = along(pair_for_peer(info, 1, [query], [near_q], [far_q]), swap, "q_swap")


    probs, mixed, stats, span = attention_probs(
        info, kv, query, near_kv, far_kv, odd_kv, (odd_q,)
    )

    def sent(pay, name):
        near = along(pay, moved(-2), name + "_near")
        far = along(pay, moved(-4), name + "_far")
        return near, far

    second_came = token_of(out_second, mid_second)
    mid_second, second_came, stats = lax.optimization_barrier((mid_second, second_came, stats))
    out_third = over(mid_second, outward, "out_third")
    statistics = (out_weight, mixed, stats)
    early, late = {0: 1, 1: 1, 2: 2}, {3: 2}
    pay_a = dout_rows(info, early, (grad_out, end_first, mid_first, out_second), *statistics, (second_came,))
    near_a, far_a = sent(pay_a, "early")
    grad_q, queries_done = query_grads(info, early, (pay_a,), probs, span)

    pay_b = dout_rows(info, late, (mid_second, out_third), *statistics, (queries_done,))
    near_b, far_b = sent(pay_b, "late")
    grad_q, queries_done = query_grads(info, late, (pay_b,), probs, span, (grad_q,))
    a, b = (0, 1, 2), (3,)
    evens = (query, near_q, far_q)
    blocks = ((0, a, 0, 0, 0, 0), (2, a, 1, 0, 1, 0), (4, a, 2, 0, 2, 0), (0, b, 0, 0, 3, 0))
    grads = key_grads(info, blocks, kv, evens, (pay_a, near_a, far_a, pay_b), slot_rows)
    pays = ((pay_a, pay_b), (near_a, near_b), (far_a, far_b))
    pair = pair_for_peer(info, 1, *pays, (queries_done, grads[0]))
    odd = along(pair, swap, "pay_swap")
    blocks = ((2, b, 0, 0, 0, 0), (4, b, 1, 0, 1, 0))
    grads = key_grads(info, blocks, kv, evens[1:], (near_b, far_b), slot_rows, grads)
    blocks = ((1, a + b, 0, 0, 0, 0), (3, a + b, 0, rows, 0, rows))
    grad_k, grad_v = key_grads(info, blocks, kv, (odd_q,), (odd,), slot_rows, grads)
    return (grad_q, grad_k, grad_v)


def solution(mesh):
    in_specs = (
        P("ctx", "tp"),
        P("ctx", "tp"),
        P("ctx", "tp"),
        P(("ctx", "tp"), None),
        P("tp", None),
    )
    out_specs = (P("ctx", "tp"), P("ctx", "tp"), P("ctx", "tp"))
    return jax.shard_map(
        functools.partial(on_device, mesh.shape["ctx"]),
        mesh=mesh,
        in_specs=in_specs,
        out_specs=out_specs,
        check_vma=False,
    )
```

```python
import functools

import jax
import jax.numpy as jnp
from jax import lax
from jax.experimental import pallas as pl
from jax.experimental.pallas import tpu as pltpu
from jax.sharding import PartitionSpec as P

HD = 128
WIN = 1024
SPAN_BLOCKS = 5
SCALE = 168.0 ** (-0.5)
NT = (((1,), (1,)), ((), ()))
NN = (((1,), (0,)), ((), ()))
F32 = jnp.float32
BF16 = jnp.bfloat16
VMEM = pl.BlockSpec(memory_space=pltpu.VMEM)
ANY = pl.BlockSpec(memory_space=pl.ANY)
COST = pl.CostEstimate(flops=1, bytes_accessed=1, transcendentals=0)


def dot(a, b, dims):
    return lax.dot_general(a, b, dims, preferred_element_type=F32)


def params(limit=20):
    return pltpu.CompilerParams(vmem_limit_bytes=limit * 2**20)


def device_info(slot_rows):
    shard = lax.axis_index("ctx")
    tp = lax.axis_index("tp")
    near_side = jnp.where(tp < 2, 1, 0)
    slot_at = [tp, tp + 1 - 2 * lax.rem(tp, 2), 1 + near_side, 3 * near_side]
    return [lax.rem(shard, 2), shard] + [slot * slot_rows for slot in slot_at]


def call(kernel, name, shapes, info, arrays, scratch=(), outs=VMEM, in_place=()):
    return pl.pallas_call(
        lambda *refs: kernel(device_info(info), *refs),
        out_shape=shapes,
        in_specs=[VMEM] * len(arrays) + [ANY] * len(in_place),
        out_specs=outs if isinstance(outs, tuple) else jax.tree.map(lambda _: outs, shapes),
        scratch_shapes=list(scratch),
        input_output_aliases={len(arrays) + n: n for n in range(len(in_place))},
        compiler_params=params(),
        cost_estimate=COST,
        name=name,
    )(*arrays, *in_place)


TOKEN = jax.ShapeDtypeStruct((8, HD), F32)


def token_kernel(*refs):
    refs[-1][...] = jnp.zeros_like(refs[-1])


def token_of(*arrays):
    return pl.pallas_call(
        token_kernel,
        out_shape=TOKEN,
        in_specs=[ANY] * len(arrays),
        out_specs=VMEM,
        compiler_params=params(),
        cost_estimate=pl.CostEstimate(flops=2 * 10**9, bytes_accessed=1, transcendentals=0),
        name="token",
    )(*arrays)


def pack_kernel(places, *refs):
    sources, outs, sems = refs[: len(places)], refs[len(places) : -1], refs[-1]
    copies = []
    for n, (source, (out, row, col)) in enumerate(zip(sources, places)):
        first, last, at = (0, source.shape[1], col) if isinstance(col, int) else (*col, 0)
        target = outs[out].at[row : row + source.shape[0], at : at + last - first]
        copies.append(pltpu.make_async_copy(source.at[:, first:last], target, sems.at[n]))
    for copy in copies:
        copy.start()
    for copy in copies:
        copy.wait()


def pack(arrays, places, shapes, limit=20, outs=ANY):
    return pl.pallas_call(
        functools.partial(pack_kernel, places),
        out_shape=tuple(jax.ShapeDtypeStruct(shape, BF16) for shape in shapes),
        in_specs=[ANY] * len(arrays),
        out_specs=(outs,) * len(shapes),
        scratch_shapes=[pltpu.SemaphoreType.DMA((len(arrays),))],
        compiler_params=params(limit),
        cost_estimate=COST,
        name="pack",
    )(*arrays)


def pair_kernel(nearer, count, info, *refs):
    own, near, far = (refs[n * count : (n + 1) * count] for n in range(3))
    pair = refs[-1]
    total = pair.shape[0] // 2

    def put(at, blocks):
        for block in blocks:
            pair[at : at + block.shape[0], :] = block[...]
            at += block.shape[0]

    @pl.when(info[0] == nearer)
    def _():
        put(0, own)
        put(total, near)

    @pl.when(info[0] != nearer)
    def _():
        put(0, near)
        put(total, far)


def pair_for_peer(info, nearer, own, near, far, after=()):
    total = sum(block.shape[0] for block in own)
    shape = jax.ShapeDtypeStruct((2 * total, own[0].shape[1]), BF16)
    kernel = functools.partial(pair_kernel, nearer, len(own))
    return call(kernel, "pair", shape, info, (*own, *near, *far, *after))


def pieces(x):
    hi = x.astype(BF16)
    rest = x - hi.astype(F32)
    mid = rest.astype(BF16)
    low = (rest - mid.astype(F32)).astype(BF16)
    return hi.astype(F32), mid.astype(F32), low.astype(F32)


def spread(x, first, into):
    lane = lax.broadcasted_iota(jnp.int32, into.shape, 1)
    for n, piece in enumerate(pieces(x)):
        into = jnp.where(lane == first + n, piece, into)
    return into


def minus_ones(rows, first):
    lane = lax.broadcasted_iota(jnp.int32, (rows, HD), 1)
    return jnp.where((lane >= first) & (lane < first + 3), -1.0, 0.0).astype(BF16)


def stacked(refs):
    blocks = [ref[...] for ref in refs]
    return blocks[0] if len(blocks) == 1 else jnp.concatenate(blocks, axis=0)


def head_cols(head):
    return slice(head * HD, (head + 1) * HD)


def probs_kernel(info, kv, query, near, far, odd, *refs):
    probs, mixed, stats, span = refs[-4:]
    rows, kv_width = kv.shape[0], kv.shape[1] // 2
    heads = query.shape[1] // HD
    shard = info[1]

    span[:rows, :] = far[...]
    span[rows : 2 * rows, :] = odd[rows:, :]
    span[2 * rows : 3 * rows, :] = near[...]
    span[3 * rows : 4 * rows, :] = odd[:rows, :]
    span[4 * rows :, :] = kv[...]

    span_rows = span.shape[0]
    row = lax.broadcasted_iota(jnp.int32, (rows, 1), 0)
    col = lax.broadcasted_iota(jnp.int32, (rows, span_rows), 1)
    first = jnp.maximum(row + 1, (SPAN_BLOCKS - 1 - shard) * rows)
    allowed = (col >= first) & (col <= row + WIN)
    row_stats = jnp.zeros((rows, HD), F32)
    for head in range(heads):
        group = head // 2
        scores = dot(query[:, head_cols(head)], span[:, head_cols(group)], NT) * SCALE
        scores = jnp.where(allowed, scores, -1e30)
        top = jnp.max(scores, axis=1, keepdims=True)
        weights = jnp.exp(scores - top)
        total = jnp.sum(weights, axis=1, keepdims=True)
        probability = (weights * (1.0 / total)).astype(BF16)
        probs[head] = probability
        value_span = span[:, kv_width + group * HD : kv_width + (group + 1) * HD]
        mixed[:, head_cols(head)] = dot(probability, value_span, NN)
        level = (top + jnp.log(total)) * (1.0 / SCALE)
        row_stats = spread(level, 8 * head, row_stats)
    stats[...] = row_stats.astype(BF16)


def attention_probs(info, kv, query, near, far, odd, after):
    rows, width = query.shape
    span_rows = SPAN_BLOCKS * rows
    shapes = (
        jax.ShapeDtypeStruct((width // HD, rows, span_rows), BF16),
        jax.ShapeDtypeStruct((rows, width), F32),
        jax.ShapeDtypeStruct((rows, HD), BF16),
        jax.ShapeDtypeStruct((span_rows, kv.shape[1]), BF16),
    )
    arrays = (kv, query, near, far, odd, *after)
    return call(probs_kernel, "attention_probs", shapes, info, arrays)


def finish_rows(info, slot, product, mixed, stats, pay, at):
    rows, width = product.shape
    start = pl.multiple_of(info[2 + slot], 16)
    dout = product.astype(BF16)
    row_stats = stats[pl.ds(start, rows), :].astype(F32)
    out_rows = mixed[pl.ds(start, rows), :]
    for head in range(width // HD):
        cols = head_cols(head)
        delta = jnp.sum(dout[:, cols].astype(F32) * out_rows[:, cols], axis=1, keepdims=True)
        row_stats = spread(delta, 8 * head + 3, row_stats)
    pay[at : at + rows, :width] = dout
    pay[at : at + rows, width:] = row_stats.astype(BF16)


def dout_kernel(slots, info, *refs):
    sources = refs[: sum(slots.values())]
    weight, mixed, stats = refs[len(sources) : len(sources) + 3]
    pay = refs[-1]
    rows = sources[0].shape[0]
    parts = []
    at = 0
    for n in slots.values():
        part = sources[at][...]
        for other in sources[at + 1 : at + n]:
            part = part + other[...]
        parts.append(part)
        at += n
    product = dot(jnp.concatenate(parts, axis=0), weight[...], NT)
    for n, slot in enumerate(slots):
        finish_rows(info, slot, product[n * rows : (n + 1) * rows], mixed, stats, pay, n * rows)


def dout_rows(info, slots, sources, weight, mixed, stats, after=()):
    total = sources[0].shape[0] * len(slots)
    shape = jax.ShapeDtypeStruct((total, weight.shape[0] + HD), BF16)
    arrays = (*sources, weight, mixed, stats, *after)
    return call(functools.partial(dout_kernel, slots), "dout_rows", shape, info, arrays)


def query_kernel(slots, count, info, probs, span, *refs):
    out, done, held, sems = refs[-4:]
    done[...] = jnp.zeros_like(done)
    pay = stacked(refs[:count])
    heads, rows, _ = probs.shape
    kv_width = span.shape[1] // 2
    total = pay.shape[0]
    part_rows = total // len(slots)
    starts = [pl.multiple_of(info[2 + slot], 16) for slot in slots]
    extra = pay[:, heads * HD :].astype(F32)
    lane = lax.broadcasted_iota(jnp.int32, extra.shape, 1)
    for group in range(heads // 2):
        key = span[:, head_cols(group)]
        value = span[:, kv_width + group * HD : kv_width + (group + 1) * HD]
        pair = (2 * group, 2 * group + 1)
        dprobs = dot(jnp.concatenate([pay[:, head_cols(head)] for head in pair], axis=0), value, NT)
        parts = []
        for m, head in enumerate(pair):
            first = 8 * head + 3
            delta = jnp.sum(
                jnp.where((lane >= first) & (lane < first + 3), extra, 0.0), axis=1, keepdims=True
            )
            for n, start in enumerate(starts):
                at = m * total + n * part_rows
                weights = probs[head, pl.ds(start, part_rows), :].astype(F32)
                centred = dprobs[at : at + part_rows, :] - delta[n * part_rows : (n + 1) * part_rows]
                parts.append((weights * centred).astype(BF16))
        grads = dot(jnp.concatenate(parts, axis=0), key, NN) * SCALE
        for m, head in enumerate(pair):
            held[:, head_cols(head)] = grads[m * total : (m + 1) * total, :]
    copies = [
        pltpu.make_async_copy(
            held.at[n * part_rows : (n + 1) * part_rows, :],
            out.at[pl.ds(start, part_rows), :],
            sems.at[n],
        )
        for n, start in enumerate(starts)
    ]
    for copy in copies:
        copy.start()
    for copy in copies:
        copy.wait()


def query_grads(info, slots, pays, probs, span, before=()):
    heads, rows, _ = probs.shape
    total = sum(pay.shape[0] for pay in pays)
    return call(
        functools.partial(query_kernel, slots, len(pays)),
        "query_grads",
        (
            jax.ShapeDtypeStruct((rows, heads * HD), F32),
            TOKEN,
        ),
        info,
        (probs, span, *pays),
        [pltpu.VMEM((total, heads * HD), F32), pltpu.SemaphoreType.DMA((len(slots),))],
        outs=(ANY, VMEM),
        in_place=before,
    )


def key_kernel(blocks, q_count, d_count, info, kv, *refs):
    q_refs, d_refs = refs[:q_count], refs[q_count : q_count + d_count]
    before = refs[q_count + d_count : -7]
    grad_k, grad_v, q_cat, d_cat, held_k, held_v, sems = refs[-7:]
    rows, kv_width = kv.shape[0], kv.shape[1] // 2
    width = q_cat.shape[1]
    lanes = q_cat.shape[0]
    part_rows = lanes // sum(len(block[1]) for block in blocks)
    lane = lax.broadcasted_iota(jnp.int32, (1, lanes), 1)
    low = jnp.zeros((1, lanes), jnp.int32)
    high = jnp.full((1, lanes), rows, jnp.int32)
    at = 0
    for distance, slots, q_at, q_row, d_at, d_row in blocks:
        size = len(slots) * part_rows
        d_cat[at : at + size, :] = d_refs[d_at][d_row : d_row + size, :]
        for slot in slots:
            start = pl.multiple_of(info[2 + slot], 16)
            q_cat[at : at + part_rows, :] = q_refs[q_at][pl.ds(start + q_row, part_rows), :]
            inside = (lane >= at) & (lane < at + part_rows)
            if distance == 0:
                high = jnp.where(inside, lane - at + start, high)
            if distance == SPAN_BLOCKS - 1:
                low = jnp.where(inside, lane - at + start + 1, low)
            at += part_rows

    masked = any(block[0] in (0, SPAN_BLOCKS - 1) for block in blocks)
    key_row = lax.broadcasted_iota(jnp.int32, (rows, lanes), 0)
    allowed = (key_row >= low) & (key_row <= high)
    extra = d_cat[:, width:]
    copies = []
    for group in range(kv_width // HD):
        cols = head_cols(group)
        key = kv[:, cols]
        value = kv[:, kv_width + group * HD : kv_width + (group + 1) * HD]
        sum_k = None
        sum_v = None
        for head in (2 * group, 2 * group + 1):
            queries = q_cat[:, head_cols(head)]
            dout = d_cat[:, head_cols(head)]
            scores = dot(
                jnp.concatenate([key, minus_ones(rows, 8 * head)], axis=1),
                jnp.concatenate([queries, extra], axis=1),
                NT,
            )
            probability = jnp.exp(scores * SCALE)
            if masked:
                probability = jnp.where(allowed, probability, 0.0)
            centred = dot(
                jnp.concatenate([value, minus_ones(rows, 8 * head + 3)], axis=1),
                jnp.concatenate([dout, extra], axis=1),
                NT,
            )
            dscores = (probability * centred).astype(BF16)
            term_v = dot(probability.astype(BF16), dout, NN)
            term_k = dot(dscores, queries, NN)
            sum_v = term_v if sum_v is None else sum_v + term_v
            sum_k = term_k if sum_k is None else sum_k + term_k
        sum_k = sum_k * SCALE
        if before:
            sum_k = sum_k + before[0][:, cols]
            sum_v = sum_v + before[1][:, cols]
        held_k[:, cols] = sum_k
        held_v[:, cols] = sum_v
        for n, (held, out) in enumerate(((held_k, grad_k), (held_v, grad_v))):
            copy = pltpu.make_async_copy(held.at[:, cols], out.at[:, cols], sems.at[2 * group + n])
            copy.start()
            copies.append(copy)
    for copy in copies:
        copy.wait()


def key_grads(info, blocks, kv, q_arrays, d_arrays, slot_rows, before=()):
    lanes = sum(len(block[1]) for block in blocks) * slot_rows
    width = q_arrays[0].shape[1]
    kv_width = kv.shape[1] // 2
    shape = jax.ShapeDtypeStruct((kv.shape[0], kv_width), F32)
    held = pltpu.VMEM(shape.shape, F32)
    return call(
        functools.partial(key_kernel, blocks, len(q_arrays), len(d_arrays)),
        "key_grads",
        (shape, shape),
        info,
        (kv, *q_arrays, *d_arrays, *before),
        [
            pltpu.VMEM((lanes, width), BF16),
            pltpu.VMEM((lanes, width + HD), BF16),
            held,
            held,
            pltpu.SemaphoreType.DMA((2 * (kv_width // HD),)),
        ],
        outs=ANY,
    )


def on_device(ctx, queries, keys, values, grad_out, out_weight):
    rows, width = queries.shape
    kv_width = 2 * keys.shape[1]
    slot_rows = grad_out.shape[0]
    swap = [(i, i ^ 1) for i in range(ctx)]

    def along(x, pairs, name):
        with jax.named_scope(name):
            return lax.ppermute(x, "ctx", pairs)

    def over(x, pairs, name):
        with jax.named_scope(name):
            return lax.ppermute(x, "tp", pairs)

    def moved(distance):
        return [(i, i + distance) for i in range(ctx) if 0 <= i + distance < ctx]

    info = slot_rows

    middle = [(1, 2), (2, 1)]
    ends = [(0, 1), (1, 0), (2, 3), (3, 2)]
    outward = [(1, 0), (2, 3)]
    mid_first = over(grad_out, middle, "mid_first")
    end_first = over(grad_out, ends, "end_first")
    mid_second = over(end_first, middle, "mid_second")
    out_second = over(mid_first, outward, "out_second")

    kv, query = pack(
        [keys, values, queries],
        [(0, 0, 0), (0, 0, kv_width // 2), (1, 0, 0)],
        [(rows, kv_width), (rows, width)],
        limit=56,
        outs=VMEM,
    )
    near_kv = along(kv, moved(2), "kv_near")
    far_kv = along(kv, moved(4), "kv_far")
    near_q = along(query, moved(-2), "q_near")
    far_q = along(query, moved(-4), "q_far")
    odd_kv = along(pair_for_peer(info, 0, [kv], [near_kv], [far_kv]), swap, "kv_swap")
    odd_q = along(pair_for_peer(info, 1, [query], [near_q], [far_q]), swap, "q_swap")


    probs, mixed, stats, span = attention_probs(
        info, kv, query, near_kv, far_kv, odd_kv, (odd_q,)
    )

    def sent(pay, name):
        near = along(pay, moved(-2), name + "_near")
        far = along(pay, moved(-4), name + "_far")
        return near, far

    second_came = token_of(out_second, mid_second)
    mid_second, second_came, stats = lax.optimization_barrier((mid_second, second_came, stats))
    out_third = over(mid_second, outward, "out_third")
    statistics = (out_weight, mixed, stats)
    early, late = {0: 1, 1: 1, 2: 2}, {3: 2}
    pay_a = dout_rows(info, early, (grad_out, end_first, mid_first, out_second), *statistics, (second_came,))
    near_a, far_a = sent(pay_a, "early")
    grad_q, queries_done = query_grads(info, early, (pay_a,), probs, span)

    pay_b = dout_rows(info, late, (mid_second, out_third), *statistics, (queries_done,))
    near_b, far_b = sent(pay_b, "late")
    grad_q, queries_done = query_grads(info, late, (pay_b,), probs, span, (grad_q,))
    a, b = (0, 1, 2), (3,)
    evens = (query, near_q, far_q)
    blocks = ((0, a, 0, 0, 0, 0), (2, a, 1, 0, 1, 0), (4, a, 2, 0, 2, 0), (0, b, 0, 0, 3, 0))
    grads = key_grads(info, blocks, kv, evens, (pay_a, near_a, far_a, pay_b), slot_rows)
    pays = ((pay_a, pay_b), (near_a, near_b), (far_a, far_b))
    pair = pair_for_peer(info, 1, *pays, (queries_done, grads[0]))
    odd = along(pair, swap, "pay_swap")
    blocks = ((2, b, 0, 0, 0, 0), (4, b, 1, 0, 1, 0))
    grads = key_grads(info, blocks, kv, evens[1:], (near_b, far_b), slot_rows, grads)
    blocks = ((1, a + b, 0, 0, 0, 0), (3, a + b, 0, rows, 0, rows))
    grad_k, grad_v = key_grads(info, blocks, kv, (odd_q,), (odd,), slot_rows, grads)
    return (grad_q, grad_k, grad_v)


def solution(mesh):
    in_specs = (
        P("ctx", "tp"),
        P("ctx", "tp"),
        P("ctx", "tp"),
        P(("ctx", "tp"), None),
        P("tp", None),
    )
    out_specs = (P("ctx", "tp"), P("ctx", "tp"), P("ctx", "tp"))
    return jax.shard_map(
        functools.partial(on_device, mesh.shape["ctx"]),
        mesh=mesh,
        in_specs=in_specs,
        out_specs=out_specs,
        check_vma=False,
    )
```

```python
import functools

import jax
import jax.numpy as jnp
from jax import lax
from jax.experimental import pallas as pl
from jax.experimental.pallas import tpu as pltpu
from jax.sharding import PartitionSpec as P

HD = 128
WIN = 1024
SPAN_BLOCKS = 5
SCALE = 168.0 ** (-0.5)
NT = (((1,), (1,)), ((), ()))
NN = (((1,), (0,)), ((), ()))
F32 = jnp.float32
BF16 = jnp.bfloat16
VMEM = pl.BlockSpec(memory_space=pltpu.VMEM)
ANY = pl.BlockSpec(memory_space=pl.ANY)
COST = pl.CostEstimate(flops=1, bytes_accessed=1, transcendentals=0)


def dot(a, b, dims):
    return lax.dot_general(a, b, dims, preferred_element_type=F32)


def params(limit=20):
    return pltpu.CompilerParams(vmem_limit_bytes=limit * 2**20)


def device_info(slot_rows):
    shard = lax.axis_index("ctx")
    tp = lax.axis_index("tp")
    near_side = jnp.where(tp < 2, 1, 0)
    slot_at = [tp, tp + 1 - 2 * lax.rem(tp, 2), 1 + near_side, 3 * near_side]
    return [lax.rem(shard, 2), shard] + [slot * slot_rows for slot in slot_at]


def call(kernel, name, shapes, info, arrays, scratch=(), outs=VMEM, in_place=()):
    return pl.pallas_call(
        lambda *refs: kernel(device_info(info), *refs),
        out_shape=shapes,
        in_specs=[VMEM] * len(arrays) + [ANY] * len(in_place),
        out_specs=outs if isinstance(outs, tuple) else jax.tree.map(lambda _: outs, shapes),
        scratch_shapes=list(scratch),
        input_output_aliases={len(arrays) + n: n for n in range(len(in_place))},
        compiler_params=params(),
        cost_estimate=COST,
        name=name,
    )(*arrays, *in_place)


TOKEN = jax.ShapeDtypeStruct((8, HD), F32)


def token_kernel(*refs):
    refs[-1][...] = jnp.zeros_like(refs[-1])


def token_of(*arrays):
    return pl.pallas_call(
        token_kernel,
        out_shape=TOKEN,
        in_specs=[ANY] * len(arrays),
        out_specs=VMEM,
        compiler_params=params(),
        cost_estimate=pl.CostEstimate(flops=2 * 10**9, bytes_accessed=1, transcendentals=0),
        name="token",
    )(*arrays)


def pack_kernel(places, *refs):
    sources, outs, sems = refs[: len(places)], refs[len(places) : -1], refs[-1]
    copies = []
    for n, (source, (out, row, col)) in enumerate(zip(sources, places)):
        first, last, at = (0, source.shape[1], col) if isinstance(col, int) else (*col, 0)
        target = outs[out].at[row : row + source.shape[0], at : at + last - first]
        copies.append(pltpu.make_async_copy(source.at[:, first:last], target, sems.at[n]))
    for copy in copies:
        copy.start()
    for copy in copies:
        copy.wait()


def pack(arrays, places, shapes, limit=20, outs=ANY):
    return pl.pallas_call(
        functools.partial(pack_kernel, places),
        out_shape=tuple(jax.ShapeDtypeStruct(shape, BF16) for shape in shapes),
        in_specs=[ANY] * len(arrays),
        out_specs=(outs,) * len(shapes),
        scratch_shapes=[pltpu.SemaphoreType.DMA((len(arrays),))],
        compiler_params=params(limit),
        cost_estimate=COST,
        name="pack",
    )(*arrays)


def pair_kernel(nearer, count, info, *refs):
    own, far, near = (refs[n * count : (n + 1) * count] for n in range(3))
    pair = refs[-1]
    total = pair.shape[0] // 2

    def put(at, blocks):
        for block in blocks:
            pair[at : at + block.shape[0], :] = block[...]
            at += block.shape[0]

    @pl.when(info[0] == nearer)
    def _():
        put(0, own)
        put(total, near)

    @pl.when(info[0] != nearer)
    def _():
        put(0, near)
        put(total, far)


def pair_for_peer(info, nearer, own, near, far, after=()):
    total = sum(block.shape[0] for block in own)
    shape = jax.ShapeDtypeStruct((2 * total, own[0].shape[1]), BF16)
    kernel = functools.partial(pair_kernel, nearer, len(own))
    return call(kernel, "pair", shape, info, (*own, *far, *near, *after))


def pieces(x):
    hi = x.astype(BF16)
    rest = x - hi.astype(F32)
    mid = rest.astype(BF16)
    low = (rest - mid.astype(F32)).astype(BF16)
    return hi.astype(F32), mid.astype(F32), low.astype(F32)


def spread(x, first, into):
    lane = lax.broadcasted_iota(jnp.int32, into.shape, 1)
    for n, piece in enumerate(pieces(x)):
        into = jnp.where(lane == first + n, piece, into)
    return into


def minus_ones(rows, first):
    lane = lax.broadcasted_iota(jnp.int32, (rows, HD), 1)
    return jnp.where((lane >= first) & (lane < first + 3), -1.0, 0.0).astype(BF16)


def stacked(refs):
    blocks = [ref[...] for ref in refs]
    return blocks[0] if len(blocks) == 1 else jnp.concatenate(blocks, axis=0)


def head_cols(head):
    return slice(head * HD, (head + 1) * HD)


def probs_kernel(info, kv, query, near, far, odd, *refs):
    probs, mixed, stats, span = refs[-4:]
    rows, kv_width = kv.shape[0], kv.shape[1] // 2
    heads = query.shape[1] // HD
    shard = info[1]

    span[:rows, :] = far[...]
    span[rows : 2 * rows, :] = odd[rows:, :]
    span[2 * rows : 3 * rows, :] = near[...]
    span[3 * rows : 4 * rows, :] = odd[:rows, :]
    span[4 * rows :, :] = kv[...]

    span_rows = span.shape[0]
    row = lax.broadcasted_iota(jnp.int32, (rows, 1), 0)
    col = lax.broadcasted_iota(jnp.int32, (rows, span_rows), 1)
    first = jnp.maximum(row + 1, (SPAN_BLOCKS - 1 - shard) * rows)
    allowed = (col >= first) & (col <= row + WIN)
    row_stats = jnp.zeros((rows, HD), F32)
    for head in range(heads):
        group = head // 2
        scores = dot(query[:, head_cols(head)], span[:, head_cols(group)], NT) * SCALE
        scores = jnp.where(allowed, scores, -1e30)
        top = jnp.max(scores, axis=1, keepdims=True)
        weights = jnp.exp(scores - top)
        total = jnp.sum(weights, axis=1, keepdims=True)
        probability = (weights * (1.0 / total)).astype(BF16)
        probs[head] = probability
        value_span = span[:, kv_width + group * HD : kv_width + (group + 1) * HD]
        mixed[:, head_cols(head)] = dot(probability, value_span, NN)
        level = (top + jnp.log(total)) * (1.0 / SCALE)
        row_stats = spread(level, 8 * head, row_stats)
    stats[...] = row_stats.astype(BF16)


def attention_probs(info, kv, query, near, far, odd, after):
    rows, width = query.shape
    span_rows = SPAN_BLOCKS * rows
    shapes = (
        jax.ShapeDtypeStruct((width // HD, rows, span_rows), BF16),
        jax.ShapeDtypeStruct((rows, width), F32),
        jax.ShapeDtypeStruct((rows, HD), BF16),
        jax.ShapeDtypeStruct((span_rows, kv.shape[1]), BF16),
    )
    arrays = (kv, query, near, far, odd, *after)
    return call(probs_kernel, "attention_probs", shapes, info, arrays)


def finish_rows(info, slot, product, mixed, stats, pay, at):
    rows, width = product.shape
    start = pl.multiple_of(info[2 + slot], 16)
    dout = product.astype(BF16)
    row_stats = stats[pl.ds(start, rows), :].astype(F32)
    out_rows = mixed[pl.ds(start, rows), :]
    for head in range(width // HD):
        cols = head_cols(head)
        delta = jnp.sum(dout[:, cols].astype(F32) * out_rows[:, cols], axis=1, keepdims=True)
        row_stats = spread(delta, 8 * head + 3, row_stats)
    pay[at : at + rows, :width] = dout
    pay[at : at + rows, width:] = row_stats.astype(BF16)


def dout_kernel(slots, info, *refs):
    sources = refs[: sum(slots.values())]
    weight, mixed, stats = refs[len(sources) : len(sources) + 3]
    pay = refs[-1]
    rows = sources[0].shape[0]
    parts = []
    at = 0
    for n in slots.values():
        part = sources[at][...]
        for other in sources[at + 1 : at + n]:
            part = part + other[...]
        parts.append(part)
        at += n
    product = dot(jnp.concatenate(parts, axis=0), weight[...], NT)
    for n, slot in enumerate(slots):
        finish_rows(info, slot, product[n * rows : (n + 1) * rows], mixed, stats, pay, n * rows)


def dout_rows(info, slots, sources, weight, mixed, stats, after=()):
    total = sources[0].shape[0] * len(slots)
    shape = jax.ShapeDtypeStruct((total, weight.shape[0] + HD), BF16)
    arrays = (*sources, weight, mixed, stats, *after)
    return call(functools.partial(dout_kernel, slots), "dout_rows", shape, info, arrays)


def query_kernel(slots, count, info, probs, span, *refs):
    out, done, held, sems = refs[-4:]
    done[...] = jnp.zeros_like(done)
    pay = stacked(refs[:count])
    heads, rows, _ = probs.shape
    kv_width = span.shape[1] // 2
    total = pay.shape[0]
    part_rows = total // len(slots)
    starts = [pl.multiple_of(info[2 + slot], 16) for slot in slots]
    extra = pay[:, heads * HD :].astype(F32)
    lane = lax.broadcasted_iota(jnp.int32, extra.shape, 1)
    for group in range(heads // 2):
        key = span[:, head_cols(group)]
        value = span[:, kv_width + group * HD : kv_width + (group + 1) * HD]
        pair = (2 * group, 2 * group + 1)
        dprobs = dot(jnp.concatenate([pay[:, head_cols(head)] for head in pair], axis=0), value, NT)
        parts = []
        for m, head in enumerate(pair):
            first = 8 * head + 3
            delta = jnp.sum(
                jnp.where((lane >= first) & (lane < first + 3), extra, 0.0), axis=1, keepdims=True
            )
            for n, start in enumerate(starts):
                at = m * total + n * part_rows
                weights = probs[head, pl.ds(start, part_rows), :].astype(F32)
                centred = dprobs[at : at + part_rows, :] - delta[n * part_rows : (n + 1) * part_rows]
                parts.append((weights * centred).astype(BF16))
        grads = dot(jnp.concatenate(parts, axis=0), key, NN) * SCALE
        for m, head in enumerate(pair):
            held[:, head_cols(head)] = grads[m * total : (m + 1) * total, :]
    copies = [
        pltpu.make_async_copy(
            held.at[n * part_rows : (n + 1) * part_rows, :],
            out.at[pl.ds(start, part_rows), :],
            sems.at[n],
        )
        for n, start in enumerate(starts)
    ]
    for copy in copies:
        copy.start()
    for copy in copies:
        copy.wait()


def query_grads(info, slots, pays, probs, span, before=()):
    heads, rows, _ = probs.shape
    total = sum(pay.shape[0] for pay in pays)
    return call(
        functools.partial(query_kernel, slots, len(pays)),
        "query_grads",
        (
            jax.ShapeDtypeStruct((rows, heads * HD), F32),
            TOKEN,
        ),
        info,
        (probs, span, *pays),
        [pltpu.VMEM((total, heads * HD), F32), pltpu.SemaphoreType.DMA((len(slots),))],
        outs=(ANY, VMEM),
        in_place=before,
    )


def key_kernel(blocks, q_count, d_count, info, kv, *refs):
    q_refs, d_refs = refs[:q_count], refs[q_count : q_count + d_count]
    before = refs[q_count + d_count : -7]
    grad_k, grad_v, q_cat, d_cat, held_k, held_v, sems = refs[-7:]
    rows, kv_width = kv.shape[0], kv.shape[1] // 2
    width = q_cat.shape[1]
    lanes = q_cat.shape[0]
    part_rows = lanes // sum(len(block[1]) for block in blocks)
    lane = lax.broadcasted_iota(jnp.int32, (1, lanes), 1)
    low = jnp.zeros((1, lanes), jnp.int32)
    high = jnp.full((1, lanes), rows, jnp.int32)
    at = 0
    for distance, slots, q_at, q_row, d_at, d_row in blocks:
        size = len(slots) * part_rows
        d_cat[at : at + size, :] = d_refs[d_at][d_row : d_row + size, :]
        for slot in slots:
            start = pl.multiple_of(info[2 + slot], 16)
            q_cat[at : at + part_rows, :] = q_refs[q_at][pl.ds(start + q_row, part_rows), :]
            inside = (lane >= at) & (lane < at + part_rows)
            if distance == 0:
                high = jnp.where(inside, lane - at + start, high)
            if distance == SPAN_BLOCKS - 1:
                low = jnp.where(inside, lane - at + start + 1, low)
            at += part_rows

    masked = any(block[0] in (0, SPAN_BLOCKS - 1) for block in blocks)
    key_row = lax.broadcasted_iota(jnp.int32, (rows, lanes), 0)
    allowed = (key_row >= low) & (key_row <= high)
    extra = d_cat[:, width:]
    copies = []
    for group in range(kv_width // HD):
        cols = head_cols(group)
        key = kv[:, cols]
        value = kv[:, kv_width + group * HD : kv_width + (group + 1) * HD]
        sum_k = None
        sum_v = None
        for head in (2 * group, 2 * group + 1):
            queries = q_cat[:, head_cols(head)]
            dout = d_cat[:, head_cols(head)]
            scores = dot(
                jnp.concatenate([key, minus_ones(rows, 8 * head)], axis=1),
                jnp.concatenate([queries, extra], axis=1),
                NT,
            )
            probability = jnp.exp(scores * SCALE)
            if masked:
                probability = jnp.where(allowed, probability, 0.0)
            centred = dot(
                jnp.concatenate([value, minus_ones(rows, 8 * head + 3)], axis=1),
                jnp.concatenate([dout, extra], axis=1),
                NT,
            )
            dscores = (probability * centred).astype(BF16)
            term_v = dot(probability.astype(BF16), dout, NN)
            term_k = dot(dscores, queries, NN)
            sum_v = term_v if sum_v is None else sum_v + term_v
            sum_k = term_k if sum_k is None else sum_k + term_k
        sum_k = sum_k * SCALE
        if before:
            sum_k = sum_k + before[0][:, cols]
            sum_v = sum_v + before[1][:, cols]
        held_k[:, cols] = sum_k
        held_v[:, cols] = sum_v
        for n, (held, out) in enumerate(((held_k, grad_k), (held_v, grad_v))):
            copy = pltpu.make_async_copy(held.at[:, cols], out.at[:, cols], sems.at[2 * group + n])
            copy.start()
            copies.append(copy)
    for copy in copies:
        copy.wait()


def key_grads(info, blocks, kv, q_arrays, d_arrays, slot_rows, before=()):
    lanes = sum(len(block[1]) for block in blocks) * slot_rows
    width = q_arrays[0].shape[1]
    kv_width = kv.shape[1] // 2
    shape = jax.ShapeDtypeStruct((kv.shape[0], kv_width), F32)
    held = pltpu.VMEM(shape.shape, F32)
    return call(
        functools.partial(key_kernel, blocks, len(q_arrays), len(d_arrays)),
        "key_grads",
        (shape, shape),
        info,
        (kv, *q_arrays, *d_arrays, *before),
        [
            pltpu.VMEM((lanes, width), BF16),
            pltpu.VMEM((lanes, width + HD), BF16),
            held,
            held,
            pltpu.SemaphoreType.DMA((2 * (kv_width // HD),)),
        ],
        outs=ANY,
    )


def on_device(ctx, queries, keys, values, grad_out, out_weight):
    rows, width = queries.shape
    kv_width = 2 * keys.shape[1]
    slot_rows = grad_out.shape[0]
    swap = [(i, i ^ 1) for i in range(ctx)]

    def along(x, pairs, name):
        with jax.named_scope(name):
            return lax.ppermute(x, "ctx", pairs)

    def over(x, pairs, name):
        with jax.named_scope(name):
            return lax.ppermute(x, "tp", pairs)

    def moved(distance):
        return [(i, i + distance) for i in range(ctx) if 0 <= i + distance < ctx]

    info = slot_rows

    middle = [(1, 2), (2, 1)]
    ends = [(0, 1), (1, 0), (2, 3), (3, 2)]
    outward = [(1, 0), (2, 3)]
    mid_first = over(grad_out, middle, "mid_first")
    end_first = over(grad_out, ends, "end_first")
    mid_second = over(end_first, middle, "mid_second")
    out_second = over(mid_first, outward, "out_second")

    kv, query = pack(
        [keys, values, queries],
        [(0, 0, 0), (0, 0, kv_width // 2), (1, 0, 0)],
        [(rows, kv_width), (rows, width)],
        limit=56,
        outs=VMEM,
    )
    near_kv = along(kv, moved(2), "kv_near")
    far_kv = along(kv, moved(4), "kv_far")
    near_q = along(query, moved(-2), "q_near")
    far_q = along(query, moved(-4), "q_far")
    odd_kv = along(pair_for_peer(info, 0, [kv], [near_kv], [far_kv]), swap, "kv_swap")
    odd_q = along(pair_for_peer(info, 1, [query], [near_q], [far_q]), swap, "q_swap")


    probs, mixed, stats, span = attention_probs(
        info, kv, query, near_kv, far_kv, odd_kv, (odd_q,)
    )

    def sent(pay, name):
        far = along(pay, moved(-4), name + "_far")
        near = along(pay, moved(-2), name + "_near")
        return near, far

    second_came = token_of(out_second, mid_second)
    mid_second, second_came, stats = lax.optimization_barrier((mid_second, second_came, stats))
    out_third = over(mid_second, outward, "out_third")
    statistics = (out_weight, mixed, stats)
    early, late = {0: 1, 1: 1, 2: 2}, {3: 2}
    pay_a = dout_rows(info, early, (grad_out, end_first, mid_first, out_second), *statistics, (second_came,))
    near_a, far_a = sent(pay_a, "early")
    grad_q, queries_done = query_grads(info, early, (pay_a,), probs, span)

    pay_b = dout_rows(info, late, (mid_second, out_third), *statistics, (queries_done,))
    near_b, far_b = sent(pay_b, "late")
    grad_q, queries_done = query_grads(info, late, (pay_b,), probs, span, (grad_q,))
    a, b = (0, 1, 2), (3,)
    evens = (query, near_q, far_q)
    blocks = ((0, a, 0, 0, 0, 0), (2, a, 1, 0, 1, 0), (4, a, 2, 0, 2, 0), (0, b, 0, 0, 3, 0))
    grads = key_grads(info, blocks, kv, evens, (pay_a, near_a, far_a, pay_b), slot_rows)
    pays = ((pay_a, pay_b), (near_a, near_b), (far_a, far_b))
    pair = pair_for_peer(info, 1, *pays, (queries_done, grads[0]))
    odd = along(pair, swap, "pay_swap")
    blocks = ((2, b, 0, 0, 1, 0), (4, b, 1, 0, 0, 0))
    grads = key_grads(info, blocks, kv, evens[1:], (far_b, near_b), slot_rows, grads)
    blocks = ((1, a + b, 0, 0, 0, 0), (3, a + b, 0, rows, 0, rows))
    grad_k, grad_v = key_grads(info, blocks, kv, (odd_q,), (odd,), slot_rows, grads)
    return (grad_q, grad_k, grad_v)


def solution(mesh):
    in_specs = (
        P("ctx", "tp"),
        P("ctx", "tp"),
        P("ctx", "tp"),
        P(("ctx", "tp"), None),
        P("tp", None),
    )
    out_specs = (P("ctx", "tp"), P("ctx", "tp"), P("ctx", "tp"))
    return jax.shard_map(
        functools.partial(on_device, mesh.shape["ctx"]),
        mesh=mesh,
        in_specs=in_specs,
        out_specs=out_specs,
        check_vma=False,
    )
```

```python
import functools

import jax
import jax.numpy as jnp
from jax import lax
from jax.experimental import pallas as pl
from jax.experimental.pallas import tpu as pltpu
from jax.sharding import PartitionSpec as P

HD = 128
WIN = 1024
SPAN_BLOCKS = 5
SCALE = 168.0 ** (-0.5)
NT = (((1,), (1,)), ((), ()))
NN = (((1,), (0,)), ((), ()))
F32 = jnp.float32
BF16 = jnp.bfloat16
FETCH = pl.CostEstimate(flops=2 * 10**9, bytes_accessed=1, transcendentals=0)
VMEM = pl.BlockSpec(memory_space=pltpu.VMEM)
ANY = pl.BlockSpec(memory_space=pl.ANY)
COST = pl.CostEstimate(flops=1, bytes_accessed=1, transcendentals=0)


def dot(a, b, dims):
    return lax.dot_general(a, b, dims, preferred_element_type=F32)


def params(limit=20):
    return pltpu.CompilerParams(vmem_limit_bytes=limit * 2**20)


def device_info(slot_rows):
    shard = lax.axis_index("ctx")
    tp = lax.axis_index("tp")
    near_side = jnp.where(tp < 2, 1, 0)
    slot_at = [tp, tp + 1 - 2 * lax.rem(tp, 2), 1 + near_side, 3 * near_side]
    return [lax.rem(shard, 2), shard] + [slot * slot_rows for slot in slot_at]


def call(kernel, name, shapes, info, arrays, scratch=(), outs=VMEM, in_place=()):
    return pl.pallas_call(
        lambda *refs: kernel(device_info(info), *refs),
        out_shape=shapes,
        in_specs=[VMEM] * len(arrays) + [ANY] * len(in_place),
        out_specs=outs if isinstance(outs, tuple) else jax.tree.map(lambda _: outs, shapes),
        scratch_shapes=list(scratch),
        input_output_aliases={len(arrays) + n: n for n in range(len(in_place))},
        compiler_params=params(),
        cost_estimate=COST,
        name=name,
    )(*arrays, *in_place)


TOKEN = jax.ShapeDtypeStruct((8, HD), F32)


def token_kernel(*refs):
    refs[-1][...] = jnp.zeros_like(refs[-1])


def token_of(*arrays, cost=COST):
    return pl.pallas_call(
        token_kernel,
        out_shape=TOKEN,
        in_specs=[ANY] * len(arrays),
        out_specs=VMEM,
        compiler_params=params(),
        cost_estimate=cost,
        name="token",
    )(*arrays)


def pack_kernel(places, *refs):
    sources, outs, sems = refs[: len(places)], refs[len(places) : -1], refs[-1]
    copies = []
    for n, (source, (out, row, col)) in enumerate(zip(sources, places)):
        first, last, at = (0, source.shape[1], col) if isinstance(col, int) else (*col, 0)
        target = outs[out].at[row : row + source.shape[0], at : at + last - first]
        copies.append(pltpu.make_async_copy(source.at[:, first:last], target, sems.at[n]))
    for copy in copies:
        copy.start()
    for copy in copies:
        copy.wait()


def pack(arrays, places, shapes, limit=20, outs=ANY):
    return pl.pallas_call(
        functools.partial(pack_kernel, places),
        out_shape=tuple(jax.ShapeDtypeStruct(shape, BF16) for shape in shapes),
        in_specs=[ANY] * len(arrays),
        out_specs=(outs,) * len(shapes),
        scratch_shapes=[pltpu.SemaphoreType.DMA((len(arrays),))],
        compiler_params=params(limit),
        cost_estimate=COST,
        name="pack",
    )(*arrays)


def pair_kernel(nearer, count, info, *refs):
    own, far, near = (refs[n * count : (n + 1) * count] for n in range(3))
    pair = refs[-1]
    total = pair.shape[0] // 2

    def put(at, blocks):
        for block in blocks:
            pair[at : at + block.shape[0], :] = block[...]
            at += block.shape[0]

    @pl.when(info[0] == nearer)
    def _():
        put(0, own)
        put(total, near)

    @pl.when(info[0] != nearer)
    def _():
        put(0, near)
        put(total, far)


def pair_for_peer(info, nearer, own, near, far, after=()):
    total = sum(block.shape[0] for block in own)
    shape = jax.ShapeDtypeStruct((2 * total, own[0].shape[1]), BF16)
    kernel = functools.partial(pair_kernel, nearer, len(own))
    return call(kernel, "pair", shape, info, (*own, *far, *near, *after))


def pieces(x):
    hi = x.astype(BF16)
    rest = x - hi.astype(F32)
    mid = rest.astype(BF16)
    low = (rest - mid.astype(F32)).astype(BF16)
    return hi.astype(F32), mid.astype(F32), low.astype(F32)


def spread(x, first, into):
    lane = lax.broadcasted_iota(jnp.int32, into.shape, 1)
    for n, piece in enumerate(pieces(x)):
        into = jnp.where(lane == first + n, piece, into)
    return into


def minus_ones(rows, first):
    lane = lax.broadcasted_iota(jnp.int32, (rows, HD), 1)
    return jnp.where((lane >= first) & (lane < first + 3), -1.0, 0.0).astype(BF16)


def stacked(refs):
    blocks = [ref[...] for ref in refs]
    return blocks[0] if len(blocks) == 1 else jnp.concatenate(blocks, axis=0)


def head_cols(head):
    return slice(head * HD, (head + 1) * HD)


def probs_kernel(info, kv, query, near, far, odd, *refs):
    probs, mixed, stats, span = refs[-4:]
    rows, kv_width = kv.shape[0], kv.shape[1] // 2
    heads = query.shape[1] // HD
    shard = info[1]

    span[:rows, :] = far[...]
    span[rows : 2 * rows, :] = odd[rows:, :]
    span[2 * rows : 3 * rows, :] = near[...]
    span[3 * rows : 4 * rows, :] = odd[:rows, :]
    span[4 * rows :, :] = kv[...]

    span_rows = span.shape[0]
    row = lax.broadcasted_iota(jnp.int32, (rows, 1), 0)
    col = lax.broadcasted_iota(jnp.int32, (rows, span_rows), 1)
    first = jnp.maximum(row + 1, (SPAN_BLOCKS - 1 - shard) * rows)
    allowed = (col >= first) & (col <= row + WIN)
    row_stats = jnp.zeros((rows, HD), F32)
    for head in range(heads):
        group = head // 2
        scores = dot(query[:, head_cols(head)], span[:, head_cols(group)], NT) * SCALE
        scores = jnp.where(allowed, scores, -1e30)
        top = jnp.max(scores, axis=1, keepdims=True)
        weights = jnp.exp(scores - top)
        total = jnp.sum(weights, axis=1, keepdims=True)
        probability = (weights * (1.0 / total)).astype(BF16)
        probs[head] = probability
        value_span = span[:, kv_width + group * HD : kv_width + (group + 1) * HD]
        mixed[:, head_cols(head)] = dot(probability, value_span, NN)
        level = (top + jnp.log(total)) * (1.0 / SCALE)
        row_stats = spread(level, 8 * head, row_stats)
    stats[...] = row_stats.astype(BF16)


def attention_probs(info, kv, query, near, far, odd, after):
    rows, width = query.shape
    span_rows = SPAN_BLOCKS * rows
    shapes = (
        jax.ShapeDtypeStruct((width // HD, rows, span_rows), BF16),
        jax.ShapeDtypeStruct((rows, width), F32),
        jax.ShapeDtypeStruct((rows, HD), BF16),
        jax.ShapeDtypeStruct((span_rows, kv.shape[1]), BF16),
    )
    arrays = (kv, query, near, far, odd, *after)
    return call(probs_kernel, "attention_probs", shapes, info, arrays)


def finish_rows(info, slot, product, mixed, stats, pay, at):
    rows, width = product.shape
    start = pl.multiple_of(info[2 + slot], 16)
    dout = product.astype(BF16)
    row_stats = stats[pl.ds(start, rows), :].astype(F32)
    out_rows = mixed[pl.ds(start, rows), :]
    for head in range(width // HD):
        cols = head_cols(head)
        delta = jnp.sum(dout[:, cols].astype(F32) * out_rows[:, cols], axis=1, keepdims=True)
        row_stats = spread(delta, 8 * head + 3, row_stats)
    pay[at : at + rows, :width] = dout
    pay[at : at + rows, width:] = row_stats.astype(BF16)


def dout_kernel(slots, info, *refs):
    sources = refs[: sum(slots.values())]
    weight, mixed, stats = refs[len(sources) : len(sources) + 3]
    pay = refs[-1]
    rows = sources[0].shape[0]
    parts = []
    at = 0
    for n in slots.values():
        part = sources[at][...]
        for other in sources[at + 1 : at + n]:
            part = part + other[...]
        parts.append(part)
        at += n
    product = dot(jnp.concatenate(parts, axis=0), weight[...], NT)
    for n, slot in enumerate(slots):
        finish_rows(info, slot, product[n * rows : (n + 1) * rows], mixed, stats, pay, n * rows)


def dout_rows(info, slots, sources, weight, mixed, stats, after=()):
    total = sources[0].shape[0] * len(slots)
    shape = jax.ShapeDtypeStruct((total, weight.shape[0] + HD), BF16)
    arrays = (*sources, weight, mixed, stats, *after)
    return call(functools.partial(dout_kernel, slots), "dout_rows", shape, info, arrays)


def query_kernel(slots, count, info, probs, span, *refs):
    out, done, held, sems = refs[-4:]
    done[...] = jnp.zeros_like(done)
    pay = stacked(refs[:count])
    heads, rows, _ = probs.shape
    kv_width = span.shape[1] // 2
    total = pay.shape[0]
    part_rows = total // len(slots)
    starts = [pl.multiple_of(info[2 + slot], 16) for slot in slots]
    extra = pay[:, heads * HD :].astype(F32)
    lane = lax.broadcasted_iota(jnp.int32, extra.shape, 1)
    for group in range(heads // 2):
        key = span[:, head_cols(group)]
        value = span[:, kv_width + group * HD : kv_width + (group + 1) * HD]
        pair = (2 * group, 2 * group + 1)
        dprobs = dot(jnp.concatenate([pay[:, head_cols(head)] for head in pair], axis=0), value, NT)
        parts = []
        for m, head in enumerate(pair):
            first = 8 * head + 3
            delta = jnp.sum(
                jnp.where((lane >= first) & (lane < first + 3), extra, 0.0), axis=1, keepdims=True
            )
            for n, start in enumerate(starts):
                at = m * total + n * part_rows
                weights = probs[head, pl.ds(start, part_rows), :].astype(F32)
                centred = dprobs[at : at + part_rows, :] - delta[n * part_rows : (n + 1) * part_rows]
                parts.append((weights * centred).astype(BF16))
        grads = dot(jnp.concatenate(parts, axis=0), key, NN) * SCALE
        for m, head in enumerate(pair):
            held[:, head_cols(head)] = grads[m * total : (m + 1) * total, :]
    copies = [
        pltpu.make_async_copy(
            held.at[n * part_rows : (n + 1) * part_rows, :],
            out.at[pl.ds(start, part_rows), :],
            sems.at[n],
        )
        for n, start in enumerate(starts)
    ]
    for copy in copies:
        copy.start()
    for copy in copies:
        copy.wait()


def query_grads(info, slots, pays, probs, span, before=()):
    heads, rows, _ = probs.shape
    total = sum(pay.shape[0] for pay in pays)
    return call(
        functools.partial(query_kernel, slots, len(pays)),
        "query_grads",
        (
            jax.ShapeDtypeStruct((rows, heads * HD), F32),
            TOKEN,
        ),
        info,
        (probs, span, *pays),
        [pltpu.VMEM((total, heads * HD), F32), pltpu.SemaphoreType.DMA((len(slots),))],
        outs=(ANY, VMEM),
        in_place=before,
    )


def key_kernel(blocks, q_count, d_count, before_count, last, info, kv, *refs):
    q_refs, d_refs = refs[:q_count], refs[q_count : q_count + d_count]
    before = refs[q_count + d_count : q_count + d_count + before_count]
    if last:
        grad_k, grad_v, q_cat, d_cat, held_k, held_v, sems = refs[-7:]
    else:
        held_k, held_v, q_cat, d_cat = refs[-4:]
    rows, kv_width = kv.shape[0], kv.shape[1] // 2
    width = q_cat.shape[1]
    lanes = q_cat.shape[0]
    part_rows = lanes // sum(len(block[1]) for block in blocks)
    lane = lax.broadcasted_iota(jnp.int32, (1, lanes), 1)
    low = jnp.zeros((1, lanes), jnp.int32)
    high = jnp.full((1, lanes), rows, jnp.int32)
    at = 0
    for distance, slots, q_at, q_row, d_at, d_row in blocks:
        size = len(slots) * part_rows
        d_cat[at : at + size, :] = d_refs[d_at][d_row : d_row + size, :]
        for slot in slots:
            start = pl.multiple_of(info[2 + slot], 16)
            q_cat[at : at + part_rows, :] = q_refs[q_at][pl.ds(start + q_row, part_rows), :]
            inside = (lane >= at) & (lane < at + part_rows)
            if distance == 0:
                high = jnp.where(inside, lane - at + start, high)
            if distance == SPAN_BLOCKS - 1:
                low = jnp.where(inside, lane - at + start + 1, low)
            at += part_rows

    masked = any(block[0] in (0, SPAN_BLOCKS - 1) for block in blocks)
    key_row = lax.broadcasted_iota(jnp.int32, (rows, lanes), 0)
    allowed = (key_row >= low) & (key_row <= high)
    extra = d_cat[:, width:]
    copies = []
    for group in range(kv_width // HD):
        cols = head_cols(group)
        key = kv[:, cols]
        value = kv[:, kv_width + group * HD : kv_width + (group + 1) * HD]
        sum_k = None
        sum_v = None
        for head in (2 * group, 2 * group + 1):
            queries = q_cat[:, head_cols(head)]
            dout = d_cat[:, head_cols(head)]
            scores = dot(
                jnp.concatenate([key, minus_ones(rows, 8 * head)], axis=1),
                jnp.concatenate([queries, extra], axis=1),
                NT,
            )
            probability = jnp.exp(scores * SCALE)
            if masked:
                probability = jnp.where(allowed, probability, 0.0)
            centred = dot(
                jnp.concatenate([value, minus_ones(rows, 8 * head + 3)], axis=1),
                jnp.concatenate([dout, extra], axis=1),
                NT,
            )
            dscores = (probability * centred).astype(BF16)
            term_v = dot(probability.astype(BF16), dout, NN)
            term_k = dot(dscores, queries, NN)
            sum_v = term_v if sum_v is None else sum_v + term_v
            sum_k = term_k if sum_k is None else sum_k + term_k
        sum_k = sum_k * SCALE
        if before:
            sum_k = sum_k + before[0][:, cols]
            sum_v = sum_v + before[1][:, cols]
        held_k[:, cols] = sum_k
        held_v[:, cols] = sum_v
        for n, (held, out) in enumerate(((held_k, grad_k), (held_v, grad_v)) if last else ()):
            copy = pltpu.make_async_copy(held.at[:, cols], out.at[:, cols], sems.at[2 * group + n])
            copy.start()
            copies.append(copy)
    for copy in copies:
        copy.wait()


def key_grads(info, blocks, kv, q_arrays, d_arrays, slot_rows, before=(), after=(), last=False):
    lanes = sum(len(block[1]) for block in blocks) * slot_rows
    width = q_arrays[0].shape[1]
    kv_width = kv.shape[1] // 2
    shape = jax.ShapeDtypeStruct((kv.shape[0], kv_width), F32)
    held = pltpu.VMEM(shape.shape, F32)
    return call(
        functools.partial(key_kernel, blocks, len(q_arrays), len(d_arrays), len(before), last),
        "key_grads",
        (shape, shape),
        info,
        (kv, *q_arrays, *d_arrays, *before, *after),
        [
            pltpu.VMEM((lanes, width), BF16),
            pltpu.VMEM((lanes, width + HD), BF16),
        ]
        + ([held, held, pltpu.SemaphoreType.DMA((2 * (kv_width // HD),))] if last else []),
        outs=ANY if last else VMEM,
    )


def on_device(ctx, queries, keys, values, grad_out, out_weight):
    rows, width = queries.shape
    kv_width = 2 * keys.shape[1]
    slot_rows = grad_out.shape[0]
    swap = [(i, i ^ 1) for i in range(ctx)]

    def along(x, pairs, name):
        with jax.named_scope(name):
            return lax.ppermute(x, "ctx", pairs)

    def over(x, pairs, name):
        with jax.named_scope(name):
            return lax.ppermute(x, "tp", pairs)

    def moved(distance):
        return [(i, i + distance) for i in range(ctx) if 0 <= i + distance < ctx]

    info = slot_rows

    middle = [(1, 2), (2, 1)]
    ends = [(0, 1), (1, 0), (2, 3), (3, 2)]
    outward = [(1, 0), (2, 3)]
    mid_first = over(grad_out, middle, "mid_first")
    end_first = over(grad_out, ends, "end_first")
    mid_second = over(end_first, middle, "mid_second")
    out_second = over(mid_first, outward, "out_second")

    kv, query = pack(
        [keys, values, queries],
        [(0, 0, 0), (0, 0, kv_width // 2), (1, 0, 0)],
        [(rows, kv_width), (rows, width)],
        limit=56,
        outs=VMEM,
    )
    near_kv = along(kv, moved(2), "kv_near")
    far_kv = along(kv, moved(4), "kv_far")
    near_q = along(query, moved(-2), "q_near")
    far_q = along(query, moved(-4), "q_far")
    odd_kv = along(pair_for_peer(info, 0, [kv], [near_kv], [far_kv]), swap, "kv_swap")
    odd_q = along(pair_for_peer(info, 1, [query], [near_q], [far_q]), swap, "q_swap")


    probs, mixed, stats, span = attention_probs(
        info, kv, query, near_kv, far_kv, odd_kv, (odd_q,)
    )

    def sent(pay, name):
        far = along(pay, moved(-4), name + "_far")
        near = along(pay, moved(-2), name + "_near")
        return near, far

    second_came = token_of(token_of(out_second), mid_second, cost=FETCH)
    mid_second, second_came, stats = lax.optimization_barrier((mid_second, second_came, stats))
    out_third = over(mid_second, outward, "out_third")
    statistics = (out_weight, mixed, stats)
    early, late = {0: 1, 1: 1, 2: 2}, {3: 2}
    pay_a = dout_rows(info, early, (grad_out, end_first, mid_first, out_second), *statistics, (second_came,))
    near_a, far_a = sent(pay_a, "early")
    grad_q, queries_done = query_grads(info, early, (pay_a,), probs, span)

    a, b = (0, 1, 2), (3,)
    pair = pair_for_peer(info, 1, (pay_a,), (near_a,), (far_a,), (queries_done,))
    odd_a = along(pair, swap, "early_swap")

    pay_b = dout_rows(info, late, (mid_second, out_third), *statistics, (queries_done,))
    near_b, far_b = sent(pay_b, "late")
    grad_q, queries_done = query_grads(info, late, (pay_b,), probs, span, (grad_q,))
    blocks = (
        (0, a, 0, 0, 0, 0),
        (2, a, 1, 0, 2, 0),
        (4, a, 2, 0, 1, 0),
        (1, a, 3, 0, 3, 0),
        (3, a, 3, rows, 3, len(a) * slot_rows),
        (0, b, 0, 0, 4, 0),
    )
    q_arrays = (query, near_q, far_q, odd_q)
    d_arrays = (pay_a, far_a, near_a, odd_a, pay_b)
    grads = key_grads(info, blocks, kv, q_arrays, d_arrays, slot_rows)
    after = (queries_done, grads[0])
    pair = pair_for_peer(info, 1, (pay_b,), (near_b,), (far_b,), after)
    odd_b = along(pair, swap, "late_swap")
    blocks = ((2, b, 0, 0, 1, 0), (4, b, 1, 0, 0, 0))
    grads = key_grads(info, blocks, kv, (near_q, far_q), (far_b, near_b), slot_rows, grads)
    blocks = ((1, b, 0, 0, 0, 0), (3, b, 0, rows, 0, slot_rows))
    grad_k, grad_v = key_grads(info, blocks, kv, (odd_q,), (odd_b,), slot_rows, grads, last=True)
    return (grad_q, grad_k, grad_v)


def solution(mesh):
    in_specs = (
        P("ctx", "tp"),
        P("ctx", "tp"),
        P("ctx", "tp"),
        P(("ctx", "tp"), None),
        P("tp", None),
    )
    out_specs = (P("ctx", "tp"), P("ctx", "tp"), P("ctx", "tp"))
    return jax.shard_map(
        functools.partial(on_device, mesh.shape["ctx"]),
        mesh=mesh,
        in_specs=in_specs,
        out_specs=out_specs,
        check_vma=False,
    )
```

```python
import functools

import jax
import jax.numpy as jnp
from jax import lax
from jax.experimental import pallas as pl
from jax.experimental.pallas import tpu as pltpu
from jax.sharding import PartitionSpec as P

HD = 128
WIN = 1024
SPAN_BLOCKS = 5
SCALE = 168.0 ** (-0.5)
NT = (((1,), (1,)), ((), ()))
NN = (((1,), (0,)), ((), ()))
F32 = jnp.float32
BF16 = jnp.bfloat16
FETCH = pl.CostEstimate(flops=10**9, bytes_accessed=1, transcendentals=0)
VMEM = pl.BlockSpec(memory_space=pltpu.VMEM)
ANY = pl.BlockSpec(memory_space=pl.ANY)
COST = pl.CostEstimate(flops=1, bytes_accessed=1, transcendentals=0)


def dot(a, b, dims):
    return lax.dot_general(a, b, dims, preferred_element_type=F32)


def params(limit=20):
    return pltpu.CompilerParams(vmem_limit_bytes=limit * 2**20)


def device_info(slot_rows):
    shard = lax.axis_index("ctx")
    tp = lax.axis_index("tp")
    near_side = jnp.where(tp < 2, 1, 0)
    slot_at = [tp, tp + 1 - 2 * lax.rem(tp, 2), 1 + near_side, 3 * near_side]
    return [lax.rem(shard, 2), shard] + [slot * slot_rows for slot in slot_at]


def call(kernel, name, shapes, info, arrays, scratch=(), outs=VMEM, in_place=()):
    return pl.pallas_call(
        lambda *refs: kernel(device_info(info), *refs),
        out_shape=shapes,
        in_specs=[VMEM] * len(arrays) + [ANY] * len(in_place),
        out_specs=outs if isinstance(outs, tuple) else jax.tree.map(lambda _: outs, shapes),
        scratch_shapes=list(scratch),
        input_output_aliases={len(arrays) + n: n for n in range(len(in_place))},
        compiler_params=params(),
        cost_estimate=COST,
        name=name,
    )(*arrays, *in_place)


TOKEN = jax.ShapeDtypeStruct((8, HD), F32)


def token_kernel(*refs):
    refs[-1][...] = jnp.zeros_like(refs[-1])


def token_of(*arrays, cost=COST):
    return pl.pallas_call(
        token_kernel,
        out_shape=TOKEN,
        in_specs=[ANY] * len(arrays),
        out_specs=VMEM,
        compiler_params=params(),
        cost_estimate=cost,
        name="token",
    )(*arrays)


def pack_kernel(places, *refs):
    sources, outs, sems = refs[: len(places)], refs[len(places) : -1], refs[-1]
    copies = []
    for n, (source, (out, row, col)) in enumerate(zip(sources, places)):
        first, last, at = (0, source.shape[1], col) if isinstance(col, int) else (*col, 0)
        target = outs[out].at[row : row + source.shape[0], at : at + last - first]
        copies.append(pltpu.make_async_copy(source.at[:, first:last], target, sems.at[n]))
    for copy in copies:
        copy.start()
    for copy in copies:
        copy.wait()


def pack(arrays, places, shapes, limit=20, outs=ANY):
    return pl.pallas_call(
        functools.partial(pack_kernel, places),
        out_shape=tuple(jax.ShapeDtypeStruct(shape, BF16) for shape in shapes),
        in_specs=[ANY] * len(arrays),
        out_specs=(outs,) * len(shapes),
        scratch_shapes=[pltpu.SemaphoreType.DMA((len(arrays),))],
        compiler_params=params(limit),
        cost_estimate=COST,
        name="pack",
    )(*arrays)


def pair_kernel(nearer, count, info, *refs):
    own, far, near = (refs[n * count : (n + 1) * count] for n in range(3))
    pair = refs[-1]
    total = pair.shape[0] // 2

    def put(at, blocks):
        for block in blocks:
            pair[at : at + block.shape[0], :] = block[...]
            at += block.shape[0]

    @pl.when(info[0] == nearer)
    def _():
        put(0, own)
        put(total, near)

    @pl.when(info[0] != nearer)
    def _():
        put(0, near)
        put(total, far)


def pair_for_peer(info, nearer, own, near, far, after=()):
    total = sum(block.shape[0] for block in own)
    shape = jax.ShapeDtypeStruct((2 * total, own[0].shape[1]), BF16)
    kernel = functools.partial(pair_kernel, nearer, len(own))
    return call(kernel, "pair", shape, info, (*own, *far, *near, *after))


def pieces(x):
    hi = x.astype(BF16)
    rest = x - hi.astype(F32)
    mid = rest.astype(BF16)
    low = (rest - mid.astype(F32)).astype(BF16)
    return hi.astype(F32), mid.astype(F32), low.astype(F32)


def spread(x, first, into):
    lane = lax.broadcasted_iota(jnp.int32, into.shape, 1)
    for n, piece in enumerate(pieces(x)):
        into = jnp.where(lane == first + n, piece, into)
    return into


def minus_ones(rows, first):
    lane = lax.broadcasted_iota(jnp.int32, (rows, HD), 1)
    return jnp.where((lane >= first) & (lane < first + 3), -1.0, 0.0).astype(BF16)


def stacked(refs):
    blocks = [ref[...] for ref in refs]
    return blocks[0] if len(blocks) == 1 else jnp.concatenate(blocks, axis=0)


def head_cols(head):
    return slice(head * HD, (head + 1) * HD)


def probs_kernel(info, kv, query, near, far, odd, *refs):
    probs, mixed, stats, span = refs[-4:]
    rows, kv_width = kv.shape[0], kv.shape[1] // 2
    heads = query.shape[1] // HD
    shard = info[1]

    span[:rows, :] = far[...]
    span[rows : 2 * rows, :] = odd[rows:, :]
    span[2 * rows : 3 * rows, :] = near[...]
    span[3 * rows : 4 * rows, :] = odd[:rows, :]
    span[4 * rows :, :] = kv[...]

    span_rows = span.shape[0]
    row = lax.broadcasted_iota(jnp.int32, (rows, 1), 0)
    col = lax.broadcasted_iota(jnp.int32, (rows, span_rows), 1)
    first = jnp.maximum(row + 1, (SPAN_BLOCKS - 1 - shard) * rows)
    allowed = (col >= first) & (col <= row + WIN)
    row_stats = jnp.zeros((rows, HD), F32)
    for head in range(heads):
        group = head // 2
        scores = dot(query[:, head_cols(head)], span[:, head_cols(group)], NT) * SCALE
        scores = jnp.where(allowed, scores, -1e30)
        top = jnp.max(scores, axis=1, keepdims=True)
        weights = jnp.exp(scores - top)
        total = jnp.sum(weights, axis=1, keepdims=True)
        probability = (weights * (1.0 / total)).astype(BF16)
        probs[head] = probability
        value_span = span[:, kv_width + group * HD : kv_width + (group + 1) * HD]
        mixed[:, head_cols(head)] = dot(probability, value_span, NN)
        level = (top + jnp.log(total)) * (1.0 / SCALE)
        row_stats = spread(level, 8 * head, row_stats)
    stats[...] = row_stats.astype(BF16)


def attention_probs(info, kv, query, near, far, odd, after):
    rows, width = query.shape
    span_rows = SPAN_BLOCKS * rows
    shapes = (
        jax.ShapeDtypeStruct((width // HD, rows, span_rows), BF16),
        jax.ShapeDtypeStruct((rows, width), F32),
        jax.ShapeDtypeStruct((rows, HD), BF16),
        jax.ShapeDtypeStruct((span_rows, kv.shape[1]), BF16),
    )
    arrays = (kv, query, near, far, odd, *after)
    return call(probs_kernel, "attention_probs", shapes, info, arrays)


def finish_rows(info, slot, product, mixed, stats, pay, at):
    rows, width = product.shape
    start = pl.multiple_of(info[2 + slot], 16)
    dout = product.astype(BF16)
    row_stats = stats[pl.ds(start, rows), :].astype(F32)
    out_rows = mixed[pl.ds(start, rows), :]
    for head in range(width // HD):
        cols = head_cols(head)
        delta = jnp.sum(dout[:, cols].astype(F32) * out_rows[:, cols], axis=1, keepdims=True)
        row_stats = spread(delta, 8 * head + 3, row_stats)
    pay[at : at + rows, :width] = dout
    pay[at : at + rows, width:] = row_stats.astype(BF16)


def dout_kernel(slots, info, *refs):
    sources = refs[: sum(slots.values())]
    weight, mixed, stats = refs[len(sources) : len(sources) + 3]
    pay = refs[-1]
    rows = sources[0].shape[0]
    parts = []
    at = 0
    for n in slots.values():
        part = sources[at][...]
        for other in sources[at + 1 : at + n]:
            part = part + other[...]
        parts.append(part)
        at += n
    product = dot(jnp.concatenate(parts, axis=0), weight[...], NT)
    for n, slot in enumerate(slots):
        finish_rows(info, slot, product[n * rows : (n + 1) * rows], mixed, stats, pay, n * rows)


def dout_rows(info, slots, sources, weight, mixed, stats, after=()):
    total = sources[0].shape[0] * len(slots)
    shape = jax.ShapeDtypeStruct((total, weight.shape[0] + HD), BF16)
    arrays = (*sources, weight, mixed, stats, *after)
    return call(functools.partial(dout_kernel, slots), "dout_rows", shape, info, arrays)


def query_kernel(slots, count, info, probs, span, *refs):
    out, done, held, sems = refs[-4:]
    done[...] = jnp.zeros_like(done)
    pay = stacked(refs[:count])
    heads, rows, _ = probs.shape
    kv_width = span.shape[1] // 2
    total = pay.shape[0]
    part_rows = total // len(slots)
    starts = [pl.multiple_of(info[2 + slot], 16) for slot in slots]
    extra = pay[:, heads * HD :].astype(F32)
    lane = lax.broadcasted_iota(jnp.int32, extra.shape, 1)
    for group in range(heads // 2):
        key = span[:, head_cols(group)]
        value = span[:, kv_width + group * HD : kv_width + (group + 1) * HD]
        pair = (2 * group, 2 * group + 1)
        dprobs = dot(jnp.concatenate([pay[:, head_cols(head)] for head in pair], axis=0), value, NT)
        parts = []
        for m, head in enumerate(pair):
            first = 8 * head + 3
            delta = jnp.sum(
                jnp.where((lane >= first) & (lane < first + 3), extra, 0.0), axis=1, keepdims=True
            )
            for n, start in enumerate(starts):
                at = m * total + n * part_rows
                weights = probs[head, pl.ds(start, part_rows), :].astype(F32)
                centred = dprobs[at : at + part_rows, :] - delta[n * part_rows : (n + 1) * part_rows]
                parts.append((weights * centred).astype(BF16))
        grads = dot(jnp.concatenate(parts, axis=0), key, NN) * SCALE
        for m, head in enumerate(pair):
            held[:, head_cols(head)] = grads[m * total : (m + 1) * total, :]
    copies = [
        pltpu.make_async_copy(
            held.at[n * part_rows : (n + 1) * part_rows, :],
            out.at[pl.ds(start, part_rows), :],
            sems.at[n],
        )
        for n, start in enumerate(starts)
    ]
    for copy in copies:
        copy.start()
    for copy in copies:
        copy.wait()


def query_grads(info, slots, pays, probs, span, before=()):
    heads, rows, _ = probs.shape
    total = sum(pay.shape[0] for pay in pays)
    return call(
        functools.partial(query_kernel, slots, len(pays)),
        "query_grads",
        (
            jax.ShapeDtypeStruct((rows, heads * HD), F32),
            TOKEN,
        ),
        info,
        (probs, span, *pays),
        [pltpu.VMEM((total, heads * HD), F32), pltpu.SemaphoreType.DMA((len(slots),))],
        outs=(ANY, VMEM),
        in_place=before,
    )


def key_kernel(blocks, q_count, d_count, before_count, last, info, kv, *refs):
    q_refs, d_refs = refs[:q_count], refs[q_count : q_count + d_count]
    before = refs[q_count + d_count : q_count + d_count + before_count]
    if last:
        grad_k, grad_v, q_cat, d_cat, held_k, held_v, sems = refs[-7:]
    else:
        held_k, held_v, q_cat, d_cat = refs[-4:]
    rows, kv_width = kv.shape[0], kv.shape[1] // 2
    width = q_cat.shape[1]
    lanes = q_cat.shape[0]
    part_rows = lanes // sum(len(block[1]) for block in blocks)
    lane = lax.broadcasted_iota(jnp.int32, (1, lanes), 1)
    low = jnp.zeros((1, lanes), jnp.int32)
    high = jnp.full((1, lanes), rows, jnp.int32)
    at = 0
    for distance, slots, q_at, q_row, d_at, d_row in blocks:
        size = len(slots) * part_rows
        d_cat[at : at + size, :] = d_refs[d_at][d_row : d_row + size, :]
        for slot in slots:
            start = pl.multiple_of(info[2 + slot], 16)
            q_cat[at : at + part_rows, :] = q_refs[q_at][pl.ds(start + q_row, part_rows), :]
            inside = (lane >= at) & (lane < at + part_rows)
            if distance == 0:
                high = jnp.where(inside, lane - at + start, high)
            if distance == SPAN_BLOCKS - 1:
                low = jnp.where(inside, lane - at + start + 1, low)
            at += part_rows

    masked = any(block[0] in (0, SPAN_BLOCKS - 1) for block in blocks)
    key_row = lax.broadcasted_iota(jnp.int32, (rows, lanes), 0)
    allowed = (key_row >= low) & (key_row <= high)
    extra = d_cat[:, width:]
    copies = []
    for group in range(kv_width // HD):
        cols = head_cols(group)
        key = kv[:, cols]
        value = kv[:, kv_width + group * HD : kv_width + (group + 1) * HD]
        sum_k = None
        sum_v = None
        for head in (2 * group, 2 * group + 1):
            queries = q_cat[:, head_cols(head)]
            dout = d_cat[:, head_cols(head)]
            scores = dot(
                jnp.concatenate([key, minus_ones(rows, 8 * head)], axis=1),
                jnp.concatenate([queries, extra], axis=1),
                NT,
            )
            probability = jnp.exp(scores * SCALE)
            if masked:
                probability = jnp.where(allowed, probability, 0.0)
            centred = dot(
                jnp.concatenate([value, minus_ones(rows, 8 * head + 3)], axis=1),
                jnp.concatenate([dout, extra], axis=1),
                NT,
            )
            dscores = (probability * centred).astype(BF16)
            term_v = dot(probability.astype(BF16), dout, NN)
            term_k = dot(dscores, queries, NN)
            sum_v = term_v if sum_v is None else sum_v + term_v
            sum_k = term_k if sum_k is None else sum_k + term_k
        sum_k = sum_k * SCALE
        if before:
            sum_k = sum_k + before[0][:, cols]
            sum_v = sum_v + before[1][:, cols]
        held_k[:, cols] = sum_k
        held_v[:, cols] = sum_v
        for n, (held, out) in enumerate(((held_k, grad_k), (held_v, grad_v)) if last else ()):
            copy = pltpu.make_async_copy(held.at[:, cols], out.at[:, cols], sems.at[2 * group + n])
            copy.start()
            copies.append(copy)
    for copy in copies:
        copy.wait()


def key_grads(info, blocks, kv, q_arrays, d_arrays, slot_rows, before=(), after=(), last=False):
    lanes = sum(len(block[1]) for block in blocks) * slot_rows
    width = q_arrays[0].shape[1]
    kv_width = kv.shape[1] // 2
    shape = jax.ShapeDtypeStruct((kv.shape[0], kv_width), F32)
    held = pltpu.VMEM(shape.shape, F32)
    return call(
        functools.partial(key_kernel, blocks, len(q_arrays), len(d_arrays), len(before), last),
        "key_grads",
        (shape, shape),
        info,
        (kv, *q_arrays, *d_arrays, *before, *after),
        [
            pltpu.VMEM((lanes, width), BF16),
            pltpu.VMEM((lanes, width + HD), BF16),
        ]
        + ([held, held, pltpu.SemaphoreType.DMA((2 * (kv_width // HD),))] if last else []),
        outs=ANY if last else VMEM,
    )


def on_device(ctx, queries, keys, values, grad_out, out_weight):
    rows, width = queries.shape
    kv_width = 2 * keys.shape[1]
    slot_rows = grad_out.shape[0]
    swap = [(i, i ^ 1) for i in range(ctx)]

    def along(x, pairs, name):
        with jax.named_scope(name):
            return lax.ppermute(x, "ctx", pairs)

    def over(x, pairs, name):
        with jax.named_scope(name):
            return lax.ppermute(x, "tp", pairs)

    def moved(distance):
        return [(i, i + distance) for i in range(ctx) if 0 <= i + distance < ctx]

    info = slot_rows

    middle = [(1, 2), (2, 1)]
    ends = [(0, 1), (1, 0), (2, 3), (3, 2)]
    outward = [(1, 0), (2, 3)]
    mid_first = over(grad_out, middle, "mid_first")
    end_first = over(grad_out, ends, "end_first")
    mid_second = over(end_first, middle, "mid_second")
    out_second = over(mid_first, outward, "out_second")

    kv, query = pack(
        [keys, values, queries],
        [(0, 0, 0), (0, 0, kv_width // 2), (1, 0, 0)],
        [(rows, kv_width), (rows, width)],
        limit=56,
        outs=VMEM,
    )
    near_kv = along(kv, moved(2), "kv_near")
    far_kv = along(kv, moved(4), "kv_far")
    near_q = along(query, moved(-2), "q_near")
    far_q = along(query, moved(-4), "q_far")
    odd_kv = along(pair_for_peer(info, 0, [kv], [near_kv], [far_kv]), swap, "kv_swap")
    odd_q = along(pair_for_peer(info, 1, [query], [near_q], [far_q]), swap, "q_swap")


    probs, mixed, stats, span = attention_probs(
        info, kv, query, near_kv, far_kv, odd_kv, (odd_q,)
    )

    def sent(pay, name):
        far = along(pay, moved(-4), name + "_far")
        near = along(pay, moved(-2), name + "_near")
        return near, far

    second_came = token_of(token_of(out_second), mid_second, cost=FETCH)
    mid_second, second_came, stats = lax.optimization_barrier((mid_second, second_came, stats))
    out_third = over(mid_second, outward, "out_third")
    statistics = (out_weight, mixed, stats)
    early, late = {0: 1, 1: 1, 2: 2}, {3: 2}
    pay_a = dout_rows(info, early, (grad_out, end_first, mid_first, out_second), *statistics, (second_came,))
    near_a, far_a = sent(pay_a, "early")
    grad_q, queries_done = query_grads(info, early, (pay_a,), probs, span)

    a, b = (0, 1, 2), (3,)
    grads = key_grads(info, ((0, a, 0, 0, 0, 0),), kv, (query,), (pay_a,), slot_rows)
    pair = pair_for_peer(info, 1, (pay_a,), (near_a,), (far_a,), (queries_done, grads[0]))
    odd_a = along(pair, swap, "early_swap")

    pay_b = dout_rows(info, late, (mid_second, out_third), *statistics, (queries_done,))
    near_b, far_b = sent(pay_b, "late")
    grad_q, queries_done = query_grads(info, late, (pay_b,), probs, span, (grad_q,))
    blocks = (
        (2, a, 1, 0, 2, 0),
        (4, a, 2, 0, 1, 0),
        (1, a, 3, 0, 3, 0),
        (3, a, 3, rows, 3, len(a) * slot_rows),
        (0, b, 0, 0, 4, 0),
    )
    q_arrays = (query, near_q, far_q, odd_q)
    d_arrays = (pay_a, far_a, near_a, odd_a, pay_b)
    grads = key_grads(info, blocks, kv, q_arrays, d_arrays, slot_rows, grads)
    after = (queries_done, grads[0])
    pair = pair_for_peer(info, 1, (pay_b,), (near_b,), (far_b,), after)
    odd_b = along(pair, swap, "late_swap")
    blocks = ((2, b, 0, 0, 1, 0), (4, b, 1, 0, 0, 0))
    grads = key_grads(info, blocks, kv, (near_q, far_q), (far_b, near_b), slot_rows, grads)
    blocks = ((1, b, 0, 0, 0, 0), (3, b, 0, rows, 0, slot_rows))
    grad_k, grad_v = key_grads(info, blocks, kv, (odd_q,), (odd_b,), slot_rows, grads, last=True)
    return (grad_q, grad_k, grad_v)


def solution(mesh):
    in_specs = (
        P("ctx", "tp"),
        P("ctx", "tp"),
        P("ctx", "tp"),
        P(("ctx", "tp"), None),
        P("tp", None),
    )
    out_specs = (P("ctx", "tp"), P("ctx", "tp"), P("ctx", "tp"))
    return jax.shard_map(
        functools.partial(on_device, mesh.shape["ctx"]),
        mesh=mesh,
        in_specs=in_specs,
        out_specs=out_specs,
        check_vma=False,
    )
```

```python
import functools

import jax
import jax.numpy as jnp
from jax import lax
from jax.experimental import pallas as pl
from jax.experimental.pallas import tpu as pltpu
from jax.sharding import PartitionSpec as P

HD = 128
WIN = 1024
SPAN_BLOCKS = 5
SCALE = 168.0 ** (-0.5)
NT = (((1,), (1,)), ((), ()))
NN = (((1,), (0,)), ((), ()))
F32 = jnp.float32
BF16 = jnp.bfloat16
FETCH = pl.CostEstimate(flops=10**9, bytes_accessed=1, transcendentals=0)
VMEM = pl.BlockSpec(memory_space=pltpu.VMEM)
ANY = pl.BlockSpec(memory_space=pl.ANY)
COST = pl.CostEstimate(flops=1, bytes_accessed=1, transcendentals=0)


def dot(a, b, dims):
    return lax.dot_general(a, b, dims, preferred_element_type=F32)


def params(limit=20):
    return pltpu.CompilerParams(vmem_limit_bytes=limit * 2**20)


def device_info(slot_rows):
    shard = lax.axis_index("ctx")
    tp = lax.axis_index("tp")
    near_side = jnp.where(tp < 2, 1, 0)
    slot_at = [tp, tp + 1 - 2 * lax.rem(tp, 2), 1 + near_side, 3 * near_side]
    return [lax.rem(shard, 2), shard] + [slot * slot_rows for slot in slot_at]


def call(kernel, name, shapes, info, arrays, scratch=(), outs=VMEM, in_place=()):
    return pl.pallas_call(
        lambda *refs: kernel(device_info(info), *refs),
        out_shape=shapes,
        in_specs=[VMEM] * len(arrays) + [ANY] * len(in_place),
        out_specs=outs if isinstance(outs, tuple) else jax.tree.map(lambda _: outs, shapes),
        scratch_shapes=list(scratch),
        input_output_aliases={len(arrays) + n: n for n in range(len(in_place))},
        compiler_params=params(),
        cost_estimate=COST,
        name=name,
    )(*arrays, *in_place)


TOKEN = jax.ShapeDtypeStruct((8, HD), F32)


def token_kernel(*refs):
    refs[-1][...] = jnp.zeros_like(refs[-1])


def token_of(*arrays, cost=COST):
    return pl.pallas_call(
        token_kernel,
        out_shape=TOKEN,
        in_specs=[ANY] * len(arrays),
        out_specs=VMEM,
        compiler_params=params(),
        cost_estimate=cost,
        name="token",
    )(*arrays)


def pack_kernel(places, *refs):
    sources, outs, sems = refs[: len(places)], refs[len(places) : -1], refs[-1]
    copies = []
    for n, (source, (out, row, col)) in enumerate(zip(sources, places)):
        first, last, at = (0, source.shape[1], col) if isinstance(col, int) else (*col, 0)
        target = outs[out].at[row : row + source.shape[0], at : at + last - first]
        copies.append(pltpu.make_async_copy(source.at[:, first:last], target, sems.at[n]))
    for copy in copies:
        copy.start()
    for copy in copies:
        copy.wait()


def pack(arrays, places, shapes, limit=20, outs=ANY):
    return pl.pallas_call(
        functools.partial(pack_kernel, places),
        out_shape=tuple(jax.ShapeDtypeStruct(shape, BF16) for shape in shapes),
        in_specs=[ANY] * len(arrays),
        out_specs=(outs,) * len(shapes),
        scratch_shapes=[pltpu.SemaphoreType.DMA((len(arrays),))],
        compiler_params=params(limit),
        cost_estimate=COST,
        name="pack",
    )(*arrays)


def pair_kernel(nearer, count, info, *refs):
    own, far, near = (refs[n * count : (n + 1) * count] for n in range(3))
    pair = refs[-1]
    total = pair.shape[0] // 2

    def put(at, blocks):
        for block in blocks:
            pair[at : at + block.shape[0], :] = block[...]
            at += block.shape[0]

    @pl.when(info[0] == nearer)
    def _():
        put(0, own)
        put(total, near)

    @pl.when(info[0] != nearer)
    def _():
        put(0, near)
        put(total, far)


def pair_for_peer(info, nearer, own, near, far, after=()):
    total = sum(block.shape[0] for block in own)
    shape = jax.ShapeDtypeStruct((2 * total, own[0].shape[1]), BF16)
    kernel = functools.partial(pair_kernel, nearer, len(own))
    return call(kernel, "pair", shape, info, (*own, *far, *near, *after))


def pieces(x):
    hi = x.astype(BF16)
    rest = x - hi.astype(F32)
    mid = rest.astype(BF16)
    low = (rest - mid.astype(F32)).astype(BF16)
    return hi.astype(F32), mid.astype(F32), low.astype(F32)


def spread(x, first, into):
    lane = lax.broadcasted_iota(jnp.int32, into.shape, 1)
    for n, piece in enumerate(pieces(x)):
        into = jnp.where(lane == first + n, piece, into)
    return into


def minus_ones(rows, first):
    lane = lax.broadcasted_iota(jnp.int32, (rows, HD), 1)
    return jnp.where((lane >= first) & (lane < first + 3), -1.0, 0.0).astype(BF16)


def stacked(refs):
    blocks = [ref[...] for ref in refs]
    return blocks[0] if len(blocks) == 1 else jnp.concatenate(blocks, axis=0)


def head_cols(head):
    return slice(head * HD, (head + 1) * HD)


def probs_kernel(info, kv, query, near, far, odd, *refs):
    probs, mixed, stats, span = refs[-4:]
    rows, kv_width = kv.shape[0], kv.shape[1] // 2
    heads = query.shape[1] // HD
    shard = info[1]

    span[:rows, :] = far[...]
    span[rows : 2 * rows, :] = odd[rows:, :]
    span[2 * rows : 3 * rows, :] = near[...]
    span[3 * rows : 4 * rows, :] = odd[:rows, :]
    span[4 * rows :, :] = kv[...]

    span_rows = span.shape[0]
    row = lax.broadcasted_iota(jnp.int32, (rows, 1), 0)
    col = lax.broadcasted_iota(jnp.int32, (rows, span_rows), 1)
    first = jnp.maximum(row + 1, (SPAN_BLOCKS - 1 - shard) * rows)
    allowed = (col >= first) & (col <= row + WIN)
    row_stats = jnp.zeros((rows, HD), F32)
    for head in range(heads):
        group = head // 2
        scores = dot(query[:, head_cols(head)], span[:, head_cols(group)], NT) * SCALE
        scores = jnp.where(allowed, scores, -1e30)
        top = jnp.max(scores, axis=1, keepdims=True)
        weights = jnp.exp(scores - top)
        total = jnp.sum(weights, axis=1, keepdims=True)
        probability = (weights * (1.0 / total)).astype(BF16)
        probs[head] = probability
        value_span = span[:, kv_width + group * HD : kv_width + (group + 1) * HD]
        mixed[:, head_cols(head)] = dot(probability, value_span, NN)
        level = (top + jnp.log(total)) * (1.0 / SCALE)
        row_stats = spread(level, 8 * head, row_stats)
    stats[...] = row_stats.astype(BF16)


def attention_probs(info, kv, query, near, far, odd, after):
    rows, width = query.shape
    span_rows = SPAN_BLOCKS * rows
    shapes = (
        jax.ShapeDtypeStruct((width // HD, rows, span_rows), BF16),
        jax.ShapeDtypeStruct((rows, width), F32),
        jax.ShapeDtypeStruct((rows, HD), BF16),
        jax.ShapeDtypeStruct((span_rows, kv.shape[1]), BF16),
    )
    arrays = (kv, query, near, far, odd, *after)
    return call(probs_kernel, "attention_probs", shapes, info, arrays)


def finish_rows(info, slot, product, mixed, stats, pay, at):
    rows, width = product.shape
    start = pl.multiple_of(info[2 + slot], 16)
    dout = product.astype(BF16)
    row_stats = stats[pl.ds(start, rows), :].astype(F32)
    out_rows = mixed[pl.ds(start, rows), :]
    for head in range(width // HD):
        cols = head_cols(head)
        delta = jnp.sum(dout[:, cols].astype(F32) * out_rows[:, cols], axis=1, keepdims=True)
        row_stats = spread(delta, 8 * head + 3, row_stats)
    pay[at : at + rows, :width] = dout
    pay[at : at + rows, width:] = row_stats.astype(BF16)


def dout_kernel(slots, info, *refs):
    sources = refs[: sum(slots.values())]
    weight, mixed, stats = refs[len(sources) : len(sources) + 3]
    pay = refs[-1]
    rows = sources[0].shape[0]
    parts = []
    at = 0
    for n in slots.values():
        part = sources[at][...]
        for other in sources[at + 1 : at + n]:
            part = part + other[...]
        parts.append(part)
        at += n
    if len(parts) == 1:
        product = dot(weight[...], parts[0], NT).T
    else:
        product = dot(jnp.concatenate(parts, axis=0), weight[...], NT)
    for n, slot in enumerate(slots):
        finish_rows(info, slot, product[n * rows : (n + 1) * rows], mixed, stats, pay, n * rows)


def dout_rows(info, slots, sources, weight, mixed, stats, after=()):
    total = sources[0].shape[0] * len(slots)
    shape = jax.ShapeDtypeStruct((total, weight.shape[0] + HD), BF16)
    arrays = (*sources, weight, mixed, stats, *after)
    return call(functools.partial(dout_kernel, slots), "dout_rows", shape, info, arrays)


def query_kernel(slots, count, info, probs, span, *refs):
    out, done, held, sems = refs[-4:]
    done[...] = jnp.zeros_like(done)
    pay = stacked(refs[:count])
    heads, rows, _ = probs.shape
    kv_width = span.shape[1] // 2
    total = pay.shape[0]
    part_rows = total // len(slots)
    starts = [pl.multiple_of(info[2 + slot], 16) for slot in slots]
    extra = pay[:, heads * HD :].astype(F32)
    lane = lax.broadcasted_iota(jnp.int32, extra.shape, 1)
    for group in range(heads // 2):
        key = span[:, head_cols(group)]
        value = span[:, kv_width + group * HD : kv_width + (group + 1) * HD]
        pair = (2 * group, 2 * group + 1)
        dprobs = dot(jnp.concatenate([pay[:, head_cols(head)] for head in pair], axis=0), value, NT)
        parts = []
        for m, head in enumerate(pair):
            first = 8 * head + 3
            delta = jnp.sum(
                jnp.where((lane >= first) & (lane < first + 3), extra, 0.0), axis=1, keepdims=True
            )
            for n, start in enumerate(starts):
                at = m * total + n * part_rows
                weights = probs[head, pl.ds(start, part_rows), :].astype(F32)
                centred = dprobs[at : at + part_rows, :] - delta[n * part_rows : (n + 1) * part_rows]
                parts.append((weights * centred).astype(BF16))
        grads = dot(jnp.concatenate(parts, axis=0), key, NN) * SCALE
        for m, head in enumerate(pair):
            held[:, head_cols(head)] = grads[m * total : (m + 1) * total, :]
    copies = [
        pltpu.make_async_copy(
            held.at[n * part_rows : (n + 1) * part_rows, :],
            out.at[pl.ds(start, part_rows), :],
            sems.at[n],
        )
        for n, start in enumerate(starts)
    ]
    for copy in copies:
        copy.start()
    for copy in copies:
        copy.wait()


def query_grads(info, slots, pays, probs, span, before=()):
    heads, rows, _ = probs.shape
    total = sum(pay.shape[0] for pay in pays)
    return call(
        functools.partial(query_kernel, slots, len(pays)),
        "query_grads",
        (
            jax.ShapeDtypeStruct((rows, heads * HD), F32),
            TOKEN,
        ),
        info,
        (probs, span, *pays),
        [pltpu.VMEM((total, heads * HD), F32), pltpu.SemaphoreType.DMA((len(slots),))],
        outs=(ANY, VMEM),
        in_place=before,
    )


def key_kernel(blocks, q_count, d_count, before_count, last, info, kv, *refs):
    q_refs, d_refs = refs[:q_count], refs[q_count : q_count + d_count]
    before = refs[q_count + d_count : q_count + d_count + before_count]
    if last:
        grad_k, grad_v, q_cat, d_cat, held_k, held_v, sems = refs[-7:]
    else:
        held_k, held_v, q_cat, d_cat = refs[-4:]
    rows, kv_width = kv.shape[0], kv.shape[1] // 2
    width = q_cat.shape[1]
    lanes = q_cat.shape[0]
    part_rows = lanes // sum(len(block[1]) for block in blocks)
    lane = lax.broadcasted_iota(jnp.int32, (1, lanes), 1)
    low = jnp.zeros((1, lanes), jnp.int32)
    high = jnp.full((1, lanes), rows, jnp.int32)
    at = 0
    for distance, slots, q_at, q_row, d_at, d_row in blocks:
        size = len(slots) * part_rows
        d_cat[at : at + size, :] = d_refs[d_at][d_row : d_row + size, :]
        for slot in slots:
            start = pl.multiple_of(info[2 + slot], 16)
            q_cat[at : at + part_rows, :] = q_refs[q_at][pl.ds(start + q_row, part_rows), :]
            inside = (lane >= at) & (lane < at + part_rows)
            if distance == 0:
                high = jnp.where(inside, lane - at + start, high)
            if distance == SPAN_BLOCKS - 1:
                low = jnp.where(inside, lane - at + start + 1, low)
            at += part_rows

    masked = any(block[0] in (0, SPAN_BLOCKS - 1) for block in blocks)
    key_row = lax.broadcasted_iota(jnp.int32, (rows, lanes), 0)
    allowed = (key_row >= low) & (key_row <= high)
    extra = d_cat[:, width:]
    copies = []
    for group in range(kv_width // HD):
        cols = head_cols(group)
        key = kv[:, cols]
        value = kv[:, kv_width + group * HD : kv_width + (group + 1) * HD]
        sum_k = None
        sum_v = None
        for head in (2 * group, 2 * group + 1):
            queries = q_cat[:, head_cols(head)]
            dout = d_cat[:, head_cols(head)]
            scores = dot(
                jnp.concatenate([key, minus_ones(rows, 8 * head)], axis=1),
                jnp.concatenate([queries, extra], axis=1),
                NT,
            )
            probability = jnp.exp(scores * SCALE)
            if masked:
                probability = jnp.where(allowed, probability, 0.0)
            centred = dot(
                jnp.concatenate([value, minus_ones(rows, 8 * head + 3)], axis=1),
                jnp.concatenate([dout, extra], axis=1),
                NT,
            )
            dscores = (probability * centred).astype(BF16)
            term_v = dot(probability.astype(BF16), dout, NN)
            term_k = dot(dscores, queries, NN)
            sum_v = term_v if sum_v is None else sum_v + term_v
            sum_k = term_k if sum_k is None else sum_k + term_k
        sum_k = sum_k * SCALE
        if before:
            sum_k = sum_k + before[0][:, cols]
            sum_v = sum_v + before[1][:, cols]
        held_k[:, cols] = sum_k
        held_v[:, cols] = sum_v
        for n, (held, out) in enumerate(((held_k, grad_k), (held_v, grad_v)) if last else ()):
            copy = pltpu.make_async_copy(held.at[:, cols], out.at[:, cols], sems.at[2 * group + n])
            copy.start()
            copies.append(copy)
    for copy in copies:
        copy.wait()


def key_grads(info, blocks, kv, q_arrays, d_arrays, slot_rows, before=(), after=(), last=False):
    lanes = sum(len(block[1]) for block in blocks) * slot_rows
    width = q_arrays[0].shape[1]
    kv_width = kv.shape[1] // 2
    shape = jax.ShapeDtypeStruct((kv.shape[0], kv_width), F32)
    held = pltpu.VMEM(shape.shape, F32)
    return call(
        functools.partial(key_kernel, blocks, len(q_arrays), len(d_arrays), len(before), last),
        "key_grads",
        (shape, shape),
        info,
        (kv, *q_arrays, *d_arrays, *before, *after),
        [
            pltpu.VMEM((lanes, width), BF16),
            pltpu.VMEM((lanes, width + HD), BF16),
        ]
        + ([held, held, pltpu.SemaphoreType.DMA((2 * (kv_width // HD),))] if last else []),
        outs=ANY if last else VMEM,
    )


def on_device(ctx, queries, keys, values, grad_out, out_weight):
    rows, width = queries.shape
    kv_width = 2 * keys.shape[1]
    slot_rows = grad_out.shape[0]
    swap = [(i, i ^ 1) for i in range(ctx)]

    def along(x, pairs, name):
        with jax.named_scope(name):
            return lax.ppermute(x, "ctx", pairs)

    def over(x, pairs, name):
        with jax.named_scope(name):
            return lax.ppermute(x, "tp", pairs)

    def moved(distance):
        return [(i, i + distance) for i in range(ctx) if 0 <= i + distance < ctx]

    info = slot_rows

    middle = [(1, 2), (2, 1)]
    ends = [(0, 1), (1, 0), (2, 3), (3, 2)]
    outward = [(1, 0), (2, 3)]
    mid_first = over(grad_out, middle, "mid_first")
    end_first = over(grad_out, ends, "end_first")
    mid_second = over(end_first, middle, "mid_second")
    out_second = over(mid_first, outward, "out_second")

    kv, query = pack(
        [keys, values, queries],
        [(0, 0, 0), (0, 0, kv_width // 2), (1, 0, 0)],
        [(rows, kv_width), (rows, width)],
        limit=56,
        outs=VMEM,
    )
    near_kv = along(kv, moved(2), "kv_near")
    far_kv = along(kv, moved(4), "kv_far")
    near_q = along(query, moved(-2), "q_near")
    far_q = along(query, moved(-4), "q_far")
    odd_kv = along(pair_for_peer(info, 0, [kv], [near_kv], [far_kv]), swap, "kv_swap")
    odd_q = along(pair_for_peer(info, 1, [query], [near_q], [far_q]), swap, "q_swap")


    probs, mixed, stats, span = attention_probs(
        info, kv, query, near_kv, far_kv, odd_kv, (odd_q,)
    )

    def sent(pay, name):
        far = along(pay, moved(-4), name + "_far")
        near = along(pay, moved(-2), name + "_near")
        return near, far

    second_came = token_of(token_of(out_second), mid_second, cost=FETCH)
    mid_second, second_came, stats = lax.optimization_barrier((mid_second, second_came, stats))
    out_third = over(mid_second, outward, "out_third")
    statistics = (out_weight, mixed, stats)
    early, late = {0: 1, 1: 1, 2: 2}, {3: 2}
    pay_a = dout_rows(info, early, (grad_out, end_first, mid_first, out_second), *statistics, (second_came,))
    near_a, far_a = sent(pay_a, "early")
    grad_q, queries_done = query_grads(info, early, (pay_a,), probs, span)

    a, b = (0, 1, 2), (3,)
    grads = key_grads(info, ((0, a, 0, 0, 0, 0),), kv, (query,), (pay_a,), slot_rows)
    pair = pair_for_peer(info, 1, (pay_a,), (near_a,), (far_a,), (queries_done, grads[0]))
    odd_a = along(pair, swap, "early_swap")

    pay_b = dout_rows(info, late, (mid_second, out_third), *statistics, (queries_done,))
    near_b, far_b = sent(pay_b, "late")
    grad_q, queries_done = query_grads(info, late, (pay_b,), probs, span, (grad_q,))
    blocks = (
        (2, a, 1, 0, 2, 0),
        (4, a, 2, 0, 1, 0),
        (1, a, 3, 0, 3, 0),
        (3, a, 3, rows, 3, len(a) * slot_rows),
        (0, b, 0, 0, 4, 0),
    )
    q_arrays = (query, near_q, far_q, odd_q)
    d_arrays = (pay_a, far_a, near_a, odd_a, pay_b)
    grads = key_grads(info, blocks, kv, q_arrays, d_arrays, slot_rows, grads)
    after = (queries_done, grads[0])
    pair = pair_for_peer(info, 1, (pay_b,), (near_b,), (far_b,), after)
    odd_b = along(pair, swap, "late_swap")
    blocks = ((2, b, 0, 0, 1, 0), (4, b, 1, 0, 0, 0))
    grads = key_grads(info, blocks, kv, (near_q, far_q), (far_b, near_b), slot_rows, grads)
    blocks = ((1, b, 0, 0, 0, 0), (3, b, 0, rows, 0, slot_rows))
    grad_k, grad_v = key_grads(info, blocks, kv, (odd_q,), (odd_b,), slot_rows, grads, last=True)
    return (grad_q, grad_k, grad_v)


def solution(mesh):
    in_specs = (
        P("ctx", "tp"),
        P("ctx", "tp"),
        P("ctx", "tp"),
        P(("ctx", "tp"), None),
        P("tp", None),
    )
    out_specs = (P("ctx", "tp"), P("ctx", "tp"), P("ctx", "tp"))
    return jax.shard_map(
        functools.partial(on_device, mesh.shape["ctx"]),
        mesh=mesh,
        in_specs=in_specs,
        out_specs=out_specs,
        check_vma=False,
    )
```

```python
import functools

import jax
import jax.numpy as jnp
from jax import lax
from jax.experimental import pallas as pl
from jax.experimental.pallas import tpu as pltpu
from jax.sharding import PartitionSpec as P

HD = 128
WIN = 1024
SPAN_BLOCKS = 5
SCALE = 168.0 ** (-0.5)
NT = (((1,), (1,)), ((), ()))
NN = (((1,), (0,)), ((), ()))
F32 = jnp.float32
BF16 = jnp.bfloat16
FETCH = pl.CostEstimate(flops=10**9, bytes_accessed=1, transcendentals=0)
VMEM = pl.BlockSpec(memory_space=pltpu.VMEM)
ANY = pl.BlockSpec(memory_space=pl.ANY)
COST = pl.CostEstimate(flops=1, bytes_accessed=1, transcendentals=0)


def dot(a, b, dims):
    return lax.dot_general(a, b, dims, preferred_element_type=F32)


def params(limit=20):
    return pltpu.CompilerParams(vmem_limit_bytes=limit * 2**20)


def device_info(slot_rows):
    shard = lax.axis_index("ctx")
    tp = lax.axis_index("tp")
    near_side = jnp.where(tp < 2, 1, 0)
    slot_at = [tp, tp + 1 - 2 * lax.rem(tp, 2), 1 + near_side, 3 * near_side]
    return [lax.rem(shard, 2), shard] + [slot * slot_rows for slot in slot_at]


def call(kernel, name, shapes, info, arrays, scratch=(), outs=VMEM, in_place=()):
    return pl.pallas_call(
        lambda *refs: kernel(device_info(info), *refs),
        out_shape=shapes,
        in_specs=[VMEM] * len(arrays) + [ANY] * len(in_place),
        out_specs=outs if isinstance(outs, tuple) else jax.tree.map(lambda _: outs, shapes),
        scratch_shapes=list(scratch),
        input_output_aliases={len(arrays) + n: n for n in range(len(in_place))},
        compiler_params=params(),
        cost_estimate=COST,
        name=name,
    )(*arrays, *in_place)


TOKEN = jax.ShapeDtypeStruct((8, HD), F32)


def token_kernel(*refs):
    refs[-1][...] = jnp.zeros_like(refs[-1])


def token_of(*arrays, cost=COST):
    return pl.pallas_call(
        token_kernel,
        out_shape=TOKEN,
        in_specs=[ANY] * len(arrays),
        out_specs=VMEM,
        compiler_params=params(),
        cost_estimate=cost,
        name="token",
    )(*arrays)


def pack_kernel(places, *refs):
    sources, outs, sems = refs[: len(places)], refs[len(places) : -1], refs[-1]
    copies = []
    for n, (source, (out, row, col)) in enumerate(zip(sources, places)):
        first, last, at = (0, source.shape[1], col) if isinstance(col, int) else (*col, 0)
        target = outs[out].at[row : row + source.shape[0], at : at + last - first]
        copies.append(pltpu.make_async_copy(source.at[:, first:last], target, sems.at[n]))
    for copy in copies:
        copy.start()
    for copy in copies:
        copy.wait()


def pack(arrays, places, shapes, limit=20, outs=ANY):
    return pl.pallas_call(
        functools.partial(pack_kernel, places),
        out_shape=tuple(jax.ShapeDtypeStruct(shape, BF16) for shape in shapes),
        in_specs=[ANY] * len(arrays),
        out_specs=(outs,) * len(shapes),
        scratch_shapes=[pltpu.SemaphoreType.DMA((len(arrays),))],
        compiler_params=params(limit),
        cost_estimate=COST,
        name="pack",
    )(*arrays)


def pair_kernel(nearer, count, info, *refs):
    own, far, near = (refs[n * count : (n + 1) * count] for n in range(3))
    pair = refs[-1]
    total = pair.shape[0] // 2

    def put(at, blocks):
        for block in blocks:
            pair[at : at + block.shape[0], :] = block[...]
            at += block.shape[0]

    @pl.when(info[0] == nearer)
    def _():
        put(0, own)
        put(total, near)

    @pl.when(info[0] != nearer)
    def _():
        put(0, near)
        put(total, far)


def pair_for_peer(info, nearer, own, near, far, after=()):
    total = sum(block.shape[0] for block in own)
    shape = jax.ShapeDtypeStruct((2 * total, own[0].shape[1]), BF16)
    kernel = functools.partial(pair_kernel, nearer, len(own))
    return call(kernel, "pair", shape, info, (*own, *far, *near, *after))


def pieces(x):
    hi = x.astype(BF16)
    rest = x - hi.astype(F32)
    mid = rest.astype(BF16)
    low = (rest - mid.astype(F32)).astype(BF16)
    return hi.astype(F32), mid.astype(F32), low.astype(F32)


def spread(x, first, into):
    lane = lax.broadcasted_iota(jnp.int32, into.shape, 1)
    for n, piece in enumerate(pieces(x)):
        into = jnp.where(lane == first + n, piece, into)
    return into


def minus_ones(rows, first):
    lane = lax.broadcasted_iota(jnp.int32, (rows, HD), 1)
    return jnp.where((lane >= first) & (lane < first + 3), -1.0, 0.0).astype(BF16)


def stacked(refs):
    blocks = [ref[...] for ref in refs]
    return blocks[0] if len(blocks) == 1 else jnp.concatenate(blocks, axis=0)


def head_cols(head):
    return slice(head * HD, (head + 1) * HD)


def probs_kernel(info, kv, query, near, far, odd, *refs):
    probs, mixed, stats, span = refs[-4:]
    rows, kv_width = kv.shape[0], kv.shape[1] // 2
    heads = query.shape[1] // HD
    shard = info[1]

    span[:rows, :] = far[...]
    span[rows : 2 * rows, :] = odd[rows:, :]
    span[2 * rows : 3 * rows, :] = near[...]
    span[3 * rows : 4 * rows, :] = odd[:rows, :]
    span[4 * rows :, :] = kv[...]

    span_rows = span.shape[0]
    row = lax.broadcasted_iota(jnp.int32, (rows, 1), 0)
    col = lax.broadcasted_iota(jnp.int32, (rows, span_rows), 1)
    first = jnp.maximum(row + 1, (SPAN_BLOCKS - 1 - shard) * rows)
    allowed = (col >= first) & (col <= row + WIN)
    row_stats = jnp.zeros((rows, HD), F32)
    for head in range(heads):
        group = head // 2
        scores = dot(query[:, head_cols(head)], span[:, head_cols(group)], NT) * SCALE
        scores = jnp.where(allowed, scores, -1e30)
        top = jnp.max(scores, axis=1, keepdims=True)
        weights = jnp.exp(scores - top)
        total = jnp.sum(weights, axis=1, keepdims=True)
        probability = (weights * (1.0 / total)).astype(BF16)
        probs[head] = probability
        value_span = span[:, kv_width + group * HD : kv_width + (group + 1) * HD]
        mixed[:, head_cols(head)] = dot(probability, value_span, NN)
        level = (top + jnp.log(total)) * (1.0 / SCALE)
        row_stats = spread(level, 8 * head, row_stats)
    stats[...] = row_stats.astype(BF16)


def attention_probs(info, kv, query, near, far, odd, after):
    rows, width = query.shape
    span_rows = SPAN_BLOCKS * rows
    shapes = (
        jax.ShapeDtypeStruct((width // HD, rows, span_rows), BF16),
        jax.ShapeDtypeStruct((rows, width), F32),
        jax.ShapeDtypeStruct((rows, HD), BF16),
        jax.ShapeDtypeStruct((span_rows, kv.shape[1]), BF16),
    )
    arrays = (kv, query, near, far, odd, *after)
    return call(probs_kernel, "attention_probs", shapes, info, arrays)


def finish_rows(info, slot, product, mixed, stats, pay, at):
    rows, width = product.shape
    start = pl.multiple_of(info[2 + slot], 16)
    dout = product.astype(BF16)
    row_stats = stats[pl.ds(start, rows), :].astype(F32)
    out_rows = mixed[pl.ds(start, rows), :]
    for head in range(width // HD):
        cols = head_cols(head)
        delta = jnp.sum(dout[:, cols].astype(F32) * out_rows[:, cols], axis=1, keepdims=True)
        row_stats = spread(delta, 8 * head + 3, row_stats)
    pay[at : at + rows, :width] = dout
    pay[at : at + rows, width:] = row_stats.astype(BF16)


def dout_kernel(slots, info, *refs):
    sources = refs[: sum(slots.values())]
    weight, mixed, stats = refs[len(sources) : len(sources) + 3]
    pay = refs[-1]
    rows = sources[0].shape[0]
    parts = []
    at = 0
    for n in slots.values():
        part = sources[at][...]
        for other in sources[at + 1 : at + n]:
            part = part + other[...]
        parts.append(part)
        at += n
    if len(parts) == 1:
        product = dot(weight[...], parts[0], NT).T
    else:
        product = dot(jnp.concatenate(parts, axis=0), weight[...], NT)
    for n, slot in enumerate(slots):
        finish_rows(info, slot, product[n * rows : (n + 1) * rows], mixed, stats, pay, n * rows)


def dout_rows(info, slots, sources, weight, mixed, stats, after=()):
    total = sources[0].shape[0] * len(slots)
    shape = jax.ShapeDtypeStruct((total, weight.shape[0] + HD), BF16)
    arrays = (*sources, weight, mixed, stats, *after)
    return call(functools.partial(dout_kernel, slots), "dout_rows", shape, info, arrays)


def query_kernel(slots, count, info, probs, span, *refs):
    out, done, held, sems = refs[-4:]
    done[...] = jnp.zeros_like(done)
    pay = stacked(refs[:count])
    heads, rows, _ = probs.shape
    kv_width = span.shape[1] // 2
    total = pay.shape[0]
    part_rows = total // len(slots)
    starts = [pl.multiple_of(info[2 + slot], 16) for slot in slots]
    extra = pay[:, heads * HD :].astype(F32)
    lane = lax.broadcasted_iota(jnp.int32, extra.shape, 1)
    for group in range(heads // 2):
        key = span[:, head_cols(group)]
        value = span[:, kv_width + group * HD : kv_width + (group + 1) * HD]
        pair = (2 * group, 2 * group + 1)
        dprobs = dot(jnp.concatenate([pay[:, head_cols(head)] for head in pair], axis=0), value, NT)
        parts = []
        for m, head in enumerate(pair):
            first = 8 * head + 3
            delta = jnp.sum(
                jnp.where((lane >= first) & (lane < first + 3), extra, 0.0), axis=1, keepdims=True
            )
            for n, start in enumerate(starts):
                at = m * total + n * part_rows
                weights = probs[head, pl.ds(start, part_rows), :].astype(F32)
                centred = dprobs[at : at + part_rows, :] - delta[n * part_rows : (n + 1) * part_rows]
                parts.append((weights * centred).astype(BF16))
        grads = dot(jnp.concatenate(parts, axis=0), key, NN) * SCALE
        for m, head in enumerate(pair):
            held[:, head_cols(head)] = grads[m * total : (m + 1) * total, :]
    copies = [
        pltpu.make_async_copy(
            held.at[n * part_rows : (n + 1) * part_rows, :],
            out.at[pl.ds(start, part_rows), :],
            sems.at[n],
        )
        for n, start in enumerate(starts)
    ]
    for copy in copies:
        copy.start()
    for copy in copies:
        copy.wait()


def query_grads(info, slots, pays, probs, span, before=()):
    heads, rows, _ = probs.shape
    total = sum(pay.shape[0] for pay in pays)
    return call(
        functools.partial(query_kernel, slots, len(pays)),
        "query_grads",
        (
            jax.ShapeDtypeStruct((rows, heads * HD), F32),
            TOKEN,
        ),
        info,
        (probs, span, *pays),
        [pltpu.VMEM((total, heads * HD), F32), pltpu.SemaphoreType.DMA((len(slots),))],
        outs=(ANY, VMEM),
        in_place=before,
    )


def key_kernel(blocks, q_count, d_count, before_count, last, info, kv, *refs):
    q_refs, d_refs = refs[:q_count], refs[q_count : q_count + d_count]
    before = refs[q_count + d_count : q_count + d_count + before_count]
    if last:
        grad_k, grad_v, q_cat, d_cat, held_k, held_v, sems = refs[-7:]
    else:
        held_k, held_v, q_cat, d_cat = refs[-4:]
    rows, kv_width = kv.shape[0], kv.shape[1] // 2
    width = q_cat.shape[1]
    lanes = q_cat.shape[0]
    part_rows = lanes // sum(len(block[1]) for block in blocks)
    lane = lax.broadcasted_iota(jnp.int32, (1, lanes), 1)
    low = jnp.zeros((1, lanes), jnp.int32)
    high = jnp.full((1, lanes), rows, jnp.int32)
    at = 0
    for distance, slots, q_at, q_row, d_at, d_row in blocks:
        size = len(slots) * part_rows
        d_cat[at : at + size, :] = d_refs[d_at][d_row : d_row + size, :]
        for slot in slots:
            start = pl.multiple_of(info[2 + slot], 16)
            q_cat[at : at + part_rows, :] = q_refs[q_at][pl.ds(start + q_row, part_rows), :]
            inside = (lane >= at) & (lane < at + part_rows)
            if distance == 0:
                high = jnp.where(inside, lane - at + start, high)
            if distance == SPAN_BLOCKS - 1:
                low = jnp.where(inside, lane - at + start + 1, low)
            at += part_rows

    masked = any(block[0] in (0, SPAN_BLOCKS - 1) for block in blocks)
    key_row = lax.broadcasted_iota(jnp.int32, (rows, lanes), 0)
    allowed = (key_row >= low) & (key_row <= high)
    extra = d_cat[:, width:]
    copies = []
    for group in range(kv_width // HD):
        cols = head_cols(group)
        key = kv[:, cols]
        value = kv[:, kv_width + group * HD : kv_width + (group + 1) * HD]
        sum_k = None
        sum_v = None
        for head in (2 * group, 2 * group + 1):
            queries = q_cat[:, head_cols(head)]
            dout = d_cat[:, head_cols(head)]
            scores = dot(
                jnp.concatenate([key, minus_ones(rows, 8 * head)], axis=1),
                jnp.concatenate([queries, extra], axis=1),
                NT,
            )
            probability = jnp.exp(scores * SCALE)
            if masked:
                probability = jnp.where(allowed, probability, 0.0)
            centred = dot(
                jnp.concatenate([value, minus_ones(rows, 8 * head + 3)], axis=1),
                jnp.concatenate([dout, extra], axis=1),
                NT,
            )
            dscores = (probability * centred).astype(BF16)
            term_v = dot(probability.astype(BF16), dout, NN)
            term_k = dot(dscores, queries, NN)
            sum_v = term_v if sum_v is None else sum_v + term_v
            sum_k = term_k if sum_k is None else sum_k + term_k
        sum_k = sum_k * SCALE
        if before:
            sum_k = sum_k + before[0][:, cols]
            sum_v = sum_v + before[1][:, cols]
        held_k[:, cols] = sum_k
        held_v[:, cols] = sum_v
        for n, (held, out) in enumerate(((held_k, grad_k), (held_v, grad_v)) if last else ()):
            copy = pltpu.make_async_copy(held.at[:, cols], out.at[:, cols], sems.at[2 * group + n])
            copy.start()
            copies.append(copy)
    for copy in copies:
        copy.wait()


def key_grads(info, blocks, kv, q_arrays, d_arrays, slot_rows, before=(), after=(), last=False):
    lanes = sum(len(block[1]) for block in blocks) * slot_rows
    width = q_arrays[0].shape[1]
    kv_width = kv.shape[1] // 2
    shape = jax.ShapeDtypeStruct((kv.shape[0], kv_width), F32)
    held = pltpu.VMEM(shape.shape, F32)
    return call(
        functools.partial(key_kernel, blocks, len(q_arrays), len(d_arrays), len(before), last),
        "key_grads",
        (shape, shape),
        info,
        (kv, *q_arrays, *d_arrays, *before, *after),
        [
            pltpu.VMEM((lanes, width), BF16),
            pltpu.VMEM((lanes, width + HD), BF16),
        ]
        + ([held, held, pltpu.SemaphoreType.DMA((2 * (kv_width // HD),))] if last else []),
        outs=ANY if last else VMEM,
    )


def on_device(ctx, queries, keys, values, grad_out, out_weight):
    rows, width = queries.shape
    kv_width = 2 * keys.shape[1]
    slot_rows = grad_out.shape[0]
    swap = [(i, i ^ 1) for i in range(ctx)]

    def along(x, pairs, name):
        with jax.named_scope(name):
            return lax.ppermute(x, "ctx", pairs)

    def over(x, pairs, name):
        with jax.named_scope(name):
            return lax.ppermute(x, "tp", pairs)

    def moved(distance):
        return [(i, i + distance) for i in range(ctx) if 0 <= i + distance < ctx]

    info = slot_rows

    middle = [(1, 2), (2, 1)]
    ends = [(0, 1), (1, 0), (2, 3), (3, 2)]
    outward = [(1, 0), (2, 3)]
    mid_first = over(grad_out, middle, "mid_first")
    end_first = over(grad_out, ends, "end_first")
    mid_second = over(end_first, middle, "mid_second")
    out_second = over(mid_first, outward, "out_second")

    kv, query = pack(
        [keys, values, queries],
        [(0, 0, 0), (0, 0, kv_width // 2), (1, 0, 0)],
        [(rows, kv_width), (rows, width)],
        limit=56,
        outs=VMEM,
    )
    near_kv = along(kv, moved(2), "kv_near")
    far_kv = along(kv, moved(4), "kv_far")
    near_q = along(query, moved(-2), "q_near")
    far_q = along(query, moved(-4), "q_far")
    odd_kv = along(pair_for_peer(info, 0, [kv], [near_kv], [far_kv]), swap, "kv_swap")
    odd_q = along(pair_for_peer(info, 1, [query], [near_q], [far_q]), swap, "q_swap")


    probs, mixed, stats, span = attention_probs(
        info, kv, query, near_kv, far_kv, odd_kv, (odd_q,)
    )

    def sent(pay, name):
        far = along(pay, moved(-4), name + "_far")
        near = along(pay, moved(-2), name + "_near")
        return near, far

    second_came = token_of(out_second, mid_second, cost=FETCH)
    mid_second, second_came, stats = lax.optimization_barrier((mid_second, second_came, stats))
    out_third = over(mid_second, outward, "out_third")
    statistics = (out_weight, mixed, stats)
    early, late = {0: 1, 1: 1, 2: 2}, {3: 2}
    pay_a = dout_rows(info, early, (grad_out, end_first, mid_first, out_second), *statistics, (second_came,))
    near_a, far_a = sent(pay_a, "early")
    grad_q, queries_done = query_grads(info, early, (pay_a,), probs, span)

    a, b = (0, 1, 2), (3,)
    grads = key_grads(info, ((0, a, 0, 0, 0, 0),), kv, (query,), (pay_a,), slot_rows)
    pair = pair_for_peer(info, 1, (pay_a,), (near_a,), (far_a,), (queries_done, grads[0]))
    odd_a = along(pair, swap, "early_swap")

    pay_b = dout_rows(info, late, (mid_second, out_third), *statistics, (queries_done,))
    near_b, far_b = sent(pay_b, "late")
    grad_q, queries_done = query_grads(info, late, (pay_b,), probs, span, (grad_q,))
    blocks = (
        (2, a, 1, 0, 2, 0),
        (4, a, 2, 0, 1, 0),
        (1, a, 3, 0, 3, 0),
        (3, a, 3, rows, 3, len(a) * slot_rows),
        (0, b, 0, 0, 4, 0),
    )
    q_arrays = (query, near_q, far_q, odd_q)
    d_arrays = (pay_a, far_a, near_a, odd_a, pay_b)
    grads = key_grads(info, blocks, kv, q_arrays, d_arrays, slot_rows, grads)
    after = (queries_done, grads[0])
    pair = pair_for_peer(info, 1, (pay_b,), (near_b,), (far_b,), after)
    odd_b = along(pair, swap, "late_swap")
    blocks = ((2, b, 0, 0, 1, 0), (4, b, 1, 0, 0, 0))
    grads = key_grads(info, blocks, kv, (near_q, far_q), (far_b, near_b), slot_rows, grads)
    blocks = ((1, b, 0, 0, 0, 0), (3, b, 0, rows, 0, slot_rows))
    grad_k, grad_v = key_grads(info, blocks, kv, (odd_q,), (odd_b,), slot_rows, grads, last=True)
    return (grad_q, grad_k, grad_v)


def solution(mesh):
    in_specs = (
        P("ctx", "tp"),
        P("ctx", "tp"),
        P("ctx", "tp"),
        P(("ctx", "tp"), None),
        P("tp", None),
    )
    out_specs = (P("ctx", "tp"), P("ctx", "tp"), P("ctx", "tp"))
    return jax.shard_map(
        functools.partial(on_device, mesh.shape["ctx"]),
        mesh=mesh,
        in_specs=in_specs,
        out_specs=out_specs,
        check_vma=False,
    )
```

```python
import functools

import jax
import jax.numpy as jnp
from jax import lax
from jax.experimental import pallas as pl
from jax.experimental.pallas import tpu as pltpu
from jax.sharding import PartitionSpec as P

HD = 128
WIN = 1024
SPAN_BLOCKS = 5
SCALE = 168.0 ** (-0.5)
NT = (((1,), (1,)), ((), ()))
NN = (((1,), (0,)), ((), ()))
F32 = jnp.float32
BF16 = jnp.bfloat16
FETCH = pl.CostEstimate(flops=10**9, bytes_accessed=1, transcendentals=0)
VMEM = pl.BlockSpec(memory_space=pltpu.VMEM)
ANY = pl.BlockSpec(memory_space=pl.ANY)
COST = pl.CostEstimate(flops=1, bytes_accessed=1, transcendentals=0)


def dot(a, b, dims):
    return lax.dot_general(a, b, dims, preferred_element_type=F32)


def params(limit=20):
    return pltpu.CompilerParams(vmem_limit_bytes=limit * 2**20)


def device_info(slot_rows):
    shard = lax.axis_index("ctx")
    tp = lax.axis_index("tp")
    near_side = jnp.where(tp < 2, 1, 0)
    slot_at = [tp, tp + 1 - 2 * lax.rem(tp, 2), 1 + near_side, 3 * near_side]
    return [lax.rem(shard, 2), shard] + [slot * slot_rows for slot in slot_at]


def call(kernel, name, shapes, info, arrays, scratch=(), outs=VMEM, in_place=()):
    return pl.pallas_call(
        lambda *refs: kernel(device_info(info), *refs),
        out_shape=shapes,
        in_specs=[VMEM] * len(arrays) + [ANY] * len(in_place),
        out_specs=outs if isinstance(outs, tuple) else jax.tree.map(lambda _: outs, shapes),
        scratch_shapes=list(scratch),
        input_output_aliases={len(arrays) + n: n for n in range(len(in_place))},
        compiler_params=params(),
        cost_estimate=COST,
        name=name,
    )(*arrays, *in_place)


TOKEN = jax.ShapeDtypeStruct((8, HD), F32)


def token_kernel(*refs):
    refs[-1][...] = jnp.zeros_like(refs[-1])


def token_of(*arrays, cost=COST):
    return pl.pallas_call(
        token_kernel,
        out_shape=TOKEN,
        in_specs=[ANY] * len(arrays),
        out_specs=VMEM,
        compiler_params=params(),
        cost_estimate=cost,
        name="token",
    )(*arrays)


def pack_kernel(places, *refs):
    sources, outs, sems = refs[: len(places)], refs[len(places) : -1], refs[-1]
    copies = []
    for n, (source, (out, row, col)) in enumerate(zip(sources, places)):
        first, last, at = (0, source.shape[1], col) if isinstance(col, int) else (*col, 0)
        target = outs[out].at[row : row + source.shape[0], at : at + last - first]
        copies.append(pltpu.make_async_copy(source.at[:, first:last], target, sems.at[n]))
    for copy in copies:
        copy.start()
    for copy in copies:
        copy.wait()


def pack(arrays, places, shapes, limit=20, outs=ANY):
    return pl.pallas_call(
        functools.partial(pack_kernel, places),
        out_shape=tuple(jax.ShapeDtypeStruct(shape, BF16) for shape in shapes),
        in_specs=[ANY] * len(arrays),
        out_specs=(outs,) * len(shapes),
        scratch_shapes=[pltpu.SemaphoreType.DMA((len(arrays),))],
        compiler_params=params(limit),
        cost_estimate=COST,
        name="pack",
    )(*arrays)


def pair_kernel(nearer, count, info, *refs):
    own, far, near = (refs[n * count : (n + 1) * count] for n in range(3))
    pair = refs[-1]
    total = pair.shape[0] // 2

    def put(at, blocks):
        for block in blocks:
            pair[at : at + block.shape[0], :] = block[...]
            at += block.shape[0]

    @pl.when(info[0] == nearer)
    def _():
        put(0, own)
        put(total, near)

    @pl.when(info[0] != nearer)
    def _():
        put(0, near)
        put(total, far)


def pair_for_peer(info, nearer, own, near, far, after=()):
    total = sum(block.shape[0] for block in own)
    shape = jax.ShapeDtypeStruct((2 * total, own[0].shape[1]), BF16)
    kernel = functools.partial(pair_kernel, nearer, len(own))
    return call(kernel, "pair", shape, info, (*own, *far, *near, *after))


def pieces(x):
    hi = x.astype(BF16)
    rest = x - hi.astype(F32)
    mid = rest.astype(BF16)
    low = (rest - mid.astype(F32)).astype(BF16)
    return hi.astype(F32), mid.astype(F32), low.astype(F32)


def spread(x, first, into):
    lane = lax.broadcasted_iota(jnp.int32, into.shape, 1)
    for n, piece in enumerate(pieces(x)):
        into = jnp.where(lane == first + n, piece, into)
    return into


def minus_ones(rows, first):
    lane = lax.broadcasted_iota(jnp.int32, (rows, HD), 1)
    return jnp.where((lane >= first) & (lane < first + 3), -1.0, 0.0).astype(BF16)


def stacked(refs):
    blocks = [ref[...] for ref in refs]
    return blocks[0] if len(blocks) == 1 else jnp.concatenate(blocks, axis=0)


def head_cols(head):
    return slice(head * HD, (head + 1) * HD)


def probs_kernel(info, kv, query, near, far, odd, *refs):
    probs, mixed, stats, span = refs[-4:]
    rows, kv_width = kv.shape[0], kv.shape[1] // 2
    heads = query.shape[1] // HD
    shard = info[1]

    span[:rows, :] = far[...]
    span[rows : 2 * rows, :] = odd[rows:, :]
    span[2 * rows : 3 * rows, :] = near[...]
    span[3 * rows : 4 * rows, :] = odd[:rows, :]
    span[4 * rows :, :] = kv[...]

    span_rows = span.shape[0]
    row = lax.broadcasted_iota(jnp.int32, (rows, 1), 0)
    col = lax.broadcasted_iota(jnp.int32, (rows, span_rows), 1)
    first = jnp.maximum(row + 1, (SPAN_BLOCKS - 1 - shard) * rows)
    allowed = (col >= first) & (col <= row + WIN)
    row_stats = jnp.zeros((rows, HD), F32)
    for head in range(heads):
        group = head // 2
        scores = dot(query[:, head_cols(head)], span[:, head_cols(group)], NT) * SCALE
        scores = jnp.where(allowed, scores, -1e30)
        top = jnp.max(scores, axis=1, keepdims=True)
        weights = jnp.exp(scores - top)
        total = jnp.sum(weights, axis=1, keepdims=True)
        probability = (weights * (1.0 / total)).astype(BF16)
        probs[head] = probability
        value_span = span[:, kv_width + group * HD : kv_width + (group + 1) * HD]
        mixed[:, head_cols(head)] = dot(probability, value_span, NN)
        level = (top + jnp.log(total)) * (1.0 / SCALE)
        row_stats = spread(level, 8 * head, row_stats)
    stats[...] = row_stats.astype(BF16)


def attention_probs(info, kv, query, near, far, odd, after):
    rows, width = query.shape
    span_rows = SPAN_BLOCKS * rows
    shapes = (
        jax.ShapeDtypeStruct((width // HD, rows, span_rows), BF16),
        jax.ShapeDtypeStruct((rows, width), F32),
        jax.ShapeDtypeStruct((rows, HD), BF16),
        jax.ShapeDtypeStruct((span_rows, kv.shape[1]), BF16),
    )
    arrays = (kv, query, near, far, odd, *after)
    return call(probs_kernel, "attention_probs", shapes, info, arrays)


def finish_rows(info, slot, product, mixed, stats, pay, at):
    rows, width = product.shape
    start = pl.multiple_of(info[2 + slot], 16)
    dout = product.astype(BF16)
    row_stats = stats[pl.ds(start, rows), :].astype(F32)
    out_rows = mixed[pl.ds(start, rows), :]
    for head in range(width // HD):
        cols = head_cols(head)
        delta = jnp.sum(dout[:, cols].astype(F32) * out_rows[:, cols], axis=1, keepdims=True)
        row_stats = spread(delta, 8 * head + 3, row_stats)
    pay[at : at + rows, :width] = dout
    pay[at : at + rows, width:] = row_stats.astype(BF16)


def dout_kernel(slots, info, *refs):
    sources = refs[: sum(slots.values())]
    weight, mixed, stats = refs[len(sources) : len(sources) + 3]
    pay = refs[-1]
    rows = sources[0].shape[0]
    parts = []
    at = 0
    for n in slots.values():
        part = sources[at][...]
        for other in sources[at + 1 : at + n]:
            part = part + other[...]
        parts.append(part)
        at += n
    block = parts[0] if len(parts) == 1 else jnp.concatenate(parts, axis=0)
    product = dot(weight[...], block, NT).T
    for n, slot in enumerate(slots):
        finish_rows(info, slot, product[n * rows : (n + 1) * rows], mixed, stats, pay, n * rows)


def dout_rows(info, slots, sources, weight, mixed, stats, after=()):
    total = sources[0].shape[0] * len(slots)
    shape = jax.ShapeDtypeStruct((total, weight.shape[0] + HD), BF16)
    arrays = (*sources, weight, mixed, stats, *after)
    return call(functools.partial(dout_kernel, slots), "dout_rows", shape, info, arrays)


def query_kernel(slots, count, info, probs, span, *refs):
    out, done, held, sems = refs[-4:]
    done[...] = jnp.zeros_like(done)
    pay = stacked(refs[:count])
    heads, rows, _ = probs.shape
    kv_width = span.shape[1] // 2
    total = pay.shape[0]
    part_rows = total // len(slots)
    starts = [pl.multiple_of(info[2 + slot], 16) for slot in slots]
    extra = pay[:, heads * HD :].astype(F32)
    lane = lax.broadcasted_iota(jnp.int32, extra.shape, 1)
    for group in range(heads // 2):
        key = span[:, head_cols(group)]
        value = span[:, kv_width + group * HD : kv_width + (group + 1) * HD]
        pair = (2 * group, 2 * group + 1)
        dprobs = dot(jnp.concatenate([pay[:, head_cols(head)] for head in pair], axis=0), value, NT)
        parts = []
        for m, head in enumerate(pair):
            first = 8 * head + 3
            delta = jnp.sum(
                jnp.where((lane >= first) & (lane < first + 3), extra, 0.0), axis=1, keepdims=True
            )
            for n, start in enumerate(starts):
                at = m * total + n * part_rows
                weights = probs[head, pl.ds(start, part_rows), :].astype(F32)
                centred = dprobs[at : at + part_rows, :] - delta[n * part_rows : (n + 1) * part_rows]
                parts.append((weights * centred).astype(BF16))
        grads = dot(jnp.concatenate(parts, axis=0), key, NN) * SCALE
        for m, head in enumerate(pair):
            held[:, head_cols(head)] = grads[m * total : (m + 1) * total, :]
    copies = [
        pltpu.make_async_copy(
            held.at[n * part_rows : (n + 1) * part_rows, :],
            out.at[pl.ds(start, part_rows), :],
            sems.at[n],
        )
        for n, start in enumerate(starts)
    ]
    for copy in copies:
        copy.start()
    for copy in copies:
        copy.wait()


def query_grads(info, slots, pays, probs, span, before=()):
    heads, rows, _ = probs.shape
    total = sum(pay.shape[0] for pay in pays)
    return call(
        functools.partial(query_kernel, slots, len(pays)),
        "query_grads",
        (
            jax.ShapeDtypeStruct((rows, heads * HD), F32),
            TOKEN,
        ),
        info,
        (probs, span, *pays),
        [pltpu.VMEM((total, heads * HD), F32), pltpu.SemaphoreType.DMA((len(slots),))],
        outs=(ANY, VMEM),
        in_place=before,
    )


def key_kernel(blocks, q_count, d_count, before_count, last, info, kv, *refs):
    q_refs, d_refs = refs[:q_count], refs[q_count : q_count + d_count]
    before = refs[q_count + d_count : q_count + d_count + before_count]
    if last:
        grad_k, grad_v, q_cat, d_cat, held_k, held_v, sems = refs[-7:]
    else:
        held_k, held_v, q_cat, d_cat = refs[-4:]
    rows, kv_width = kv.shape[0], kv.shape[1] // 2
    width = q_cat.shape[1]
    lanes = q_cat.shape[0]
    part_rows = lanes // sum(len(block[1]) for block in blocks)
    lane = lax.broadcasted_iota(jnp.int32, (1, lanes), 1)
    low = jnp.zeros((1, lanes), jnp.int32)
    high = jnp.full((1, lanes), rows, jnp.int32)
    at = 0
    for distance, slots, q_at, q_row, d_at, d_row in blocks:
        size = len(slots) * part_rows
        d_cat[at : at + size, :] = d_refs[d_at][d_row : d_row + size, :]
        for slot in slots:
            start = pl.multiple_of(info[2 + slot], 16)
            q_cat[at : at + part_rows, :] = q_refs[q_at][pl.ds(start + q_row, part_rows), :]
            inside = (lane >= at) & (lane < at + part_rows)
            if distance == 0:
                high = jnp.where(inside, lane - at + start, high)
            if distance == SPAN_BLOCKS - 1:
                low = jnp.where(inside, lane - at + start + 1, low)
            at += part_rows

    masked = any(block[0] in (0, SPAN_BLOCKS - 1) for block in blocks)
    key_row = lax.broadcasted_iota(jnp.int32, (rows, lanes), 0)
    allowed = (key_row >= low) & (key_row <= high)
    extra = d_cat[:, width:]
    copies = []
    for group in range(kv_width // HD):
        cols = head_cols(group)
        key = kv[:, cols]
        value = kv[:, kv_width + group * HD : kv_width + (group + 1) * HD]
        sum_k = None
        sum_v = None
        for head in (2 * group, 2 * group + 1):
            queries = q_cat[:, head_cols(head)]
            dout = d_cat[:, head_cols(head)]
            scores = dot(
                jnp.concatenate([key, minus_ones(rows, 8 * head)], axis=1),
                jnp.concatenate([queries, extra], axis=1),
                NT,
            )
            probability = jnp.exp(scores * SCALE)
            if masked:
                probability = jnp.where(allowed, probability, 0.0)
            centred = dot(
                jnp.concatenate([value, minus_ones(rows, 8 * head + 3)], axis=1),
                jnp.concatenate([dout, extra], axis=1),
                NT,
            )
            dscores = (probability * centred).astype(BF16)
            term_v = dot(probability.astype(BF16), dout, NN)
            term_k = dot(dscores, queries, NN)
            sum_v = term_v if sum_v is None else sum_v + term_v
            sum_k = term_k if sum_k is None else sum_k + term_k
        sum_k = sum_k * SCALE
        if before:
            sum_k = sum_k + before[0][:, cols]
            sum_v = sum_v + before[1][:, cols]
        held_k[:, cols] = sum_k
        held_v[:, cols] = sum_v
        for n, (held, out) in enumerate(((held_k, grad_k), (held_v, grad_v)) if last else ()):
            copy = pltpu.make_async_copy(held.at[:, cols], out.at[:, cols], sems.at[2 * group + n])
            copy.start()
            copies.append(copy)
    for copy in copies:
        copy.wait()


def key_grads(info, blocks, kv, q_arrays, d_arrays, slot_rows, before=(), after=(), last=False):
    lanes = sum(len(block[1]) for block in blocks) * slot_rows
    width = q_arrays[0].shape[1]
    kv_width = kv.shape[1] // 2
    shape = jax.ShapeDtypeStruct((kv.shape[0], kv_width), F32)
    held = pltpu.VMEM(shape.shape, F32)
    return call(
        functools.partial(key_kernel, blocks, len(q_arrays), len(d_arrays), len(before), last),
        "key_grads",
        (shape, shape),
        info,
        (kv, *q_arrays, *d_arrays, *before, *after),
        [
            pltpu.VMEM((lanes, width), BF16),
            pltpu.VMEM((lanes, width + HD), BF16),
        ]
        + ([held, held, pltpu.SemaphoreType.DMA((2 * (kv_width // HD),))] if last else []),
        outs=ANY if last else VMEM,
    )


def on_device(ctx, queries, keys, values, grad_out, out_weight):
    rows, width = queries.shape
    kv_width = 2 * keys.shape[1]
    slot_rows = grad_out.shape[0]
    swap = [(i, i ^ 1) for i in range(ctx)]

    def along(x, pairs, name):
        with jax.named_scope(name):
            return lax.ppermute(x, "ctx", pairs)

    def over(x, pairs, name):
        with jax.named_scope(name):
            return lax.ppermute(x, "tp", pairs)

    def moved(distance):
        return [(i, i + distance) for i in range(ctx) if 0 <= i + distance < ctx]

    info = slot_rows

    middle = [(1, 2), (2, 1)]
    ends = [(0, 1), (1, 0), (2, 3), (3, 2)]
    outward = [(1, 0), (2, 3)]
    mid_first = over(grad_out, middle, "mid_first")
    end_first = over(grad_out, ends, "end_first")
    mid_second = over(end_first, middle, "mid_second")
    out_second = over(mid_first, outward, "out_second")

    kv, query = pack(
        [keys, values, queries],
        [(0, 0, 0), (0, 0, kv_width // 2), (1, 0, 0)],
        [(rows, kv_width), (rows, width)],
        limit=56,
        outs=VMEM,
    )
    near_kv = along(kv, moved(2), "kv_near")
    far_kv = along(kv, moved(4), "kv_far")
    near_q = along(query, moved(-2), "q_near")
    far_q = along(query, moved(-4), "q_far")
    odd_kv = along(pair_for_peer(info, 0, [kv], [near_kv], [far_kv]), swap, "kv_swap")
    odd_q = along(pair_for_peer(info, 1, [query], [near_q], [far_q]), swap, "q_swap")


    probs, mixed, stats, span = attention_probs(
        info, kv, query, near_kv, far_kv, odd_kv, (odd_q,)
    )

    def sent(pay, name):
        far = along(pay, moved(-4), name + "_far")
        near = along(pay, moved(-2), name + "_near")
        return near, far

    second_came = token_of(out_second, mid_second, cost=FETCH)
    mid_second, second_came, stats = lax.optimization_barrier((mid_second, second_came, stats))
    out_third = over(mid_second, outward, "out_third")
    statistics = (out_weight, mixed, stats)
    early, late = {0: 1, 1: 1, 2: 2}, {3: 2}
    pay_a = dout_rows(info, early, (grad_out, end_first, mid_first, out_second), *statistics, (second_came,))
    near_a, far_a = sent(pay_a, "early")
    grad_q, queries_done = query_grads(info, early, (pay_a,), probs, span)

    a, b = (0, 1, 2), (3,)
    grads = key_grads(info, ((0, a, 0, 0, 0, 0),), kv, (query,), (pay_a,), slot_rows)
    pair = pair_for_peer(info, 1, (pay_a,), (near_a,), (far_a,), (queries_done, grads[0]))
    odd_a = along(pair, swap, "early_swap")

    pay_b = dout_rows(info, late, (mid_second, out_third), *statistics, (queries_done,))
    near_b, far_b = sent(pay_b, "late")
    grad_q, queries_done = query_grads(info, late, (pay_b,), probs, span, (grad_q,))
    blocks = (
        (2, a, 1, 0, 2, 0),
        (4, a, 2, 0, 1, 0),
        (1, a, 3, 0, 3, 0),
        (3, a, 3, rows, 3, len(a) * slot_rows),
        (0, b, 0, 0, 4, 0),
    )
    q_arrays = (query, near_q, far_q, odd_q)
    d_arrays = (pay_a, far_a, near_a, odd_a, pay_b)
    grads = key_grads(info, blocks, kv, q_arrays, d_arrays, slot_rows, grads)
    after = (queries_done, grads[0])
    pair = pair_for_peer(info, 1, (pay_b,), (near_b,), (far_b,), after)
    odd_b = along(pair, swap, "late_swap")
    blocks = ((2, b, 0, 0, 1, 0), (4, b, 1, 0, 0, 0))
    grads = key_grads(info, blocks, kv, (near_q, far_q), (far_b, near_b), slot_rows, grads)
    blocks = ((1, b, 0, 0, 0, 0), (3, b, 0, rows, 0, slot_rows))
    grad_k, grad_v = key_grads(info, blocks, kv, (odd_q,), (odd_b,), slot_rows, grads, last=True)
    return (grad_q, grad_k, grad_v)


def solution(mesh):
    in_specs = (
        P("ctx", "tp"),
        P("ctx", "tp"),
        P("ctx", "tp"),
        P(("ctx", "tp"), None),
        P("tp", None),
    )
    out_specs = (P("ctx", "tp"), P("ctx", "tp"), P("ctx", "tp"))
    return jax.shard_map(
        functools.partial(on_device, mesh.shape["ctx"]),
        mesh=mesh,
        in_specs=in_specs,
        out_specs=out_specs,
        check_vma=False,
    )
```

```python
import functools

import jax
import jax.numpy as jnp
from jax import lax
from jax.experimental import pallas as pl
from jax.experimental.pallas import tpu as pltpu
from jax.sharding import PartitionSpec as P

HD = 128
WIN = 1024
SPAN_BLOCKS = 5
SCALE = 168.0 ** (-0.5)
NT = (((1,), (1,)), ((), ()))
NN = (((1,), (0,)), ((), ()))
F32 = jnp.float32
BF16 = jnp.bfloat16
FETCH = pl.CostEstimate(flops=10**9, bytes_accessed=1, transcendentals=0)
VMEM = pl.BlockSpec(memory_space=pltpu.VMEM)
ANY = pl.BlockSpec(memory_space=pl.ANY)
COST = pl.CostEstimate(flops=1, bytes_accessed=1, transcendentals=0)


def dot(a, b, dims):
    return lax.dot_general(a, b, dims, preferred_element_type=F32)


def params(limit=20):
    return pltpu.CompilerParams(vmem_limit_bytes=limit * 2**20)


def device_info(slot_rows):
    shard = lax.axis_index("ctx")
    tp = lax.axis_index("tp")
    near_side = jnp.where(tp < 2, 1, 0)
    slot_at = [tp, tp + 1 - 2 * lax.rem(tp, 2), 1 + near_side, 3 * near_side]
    return [lax.rem(shard, 2), shard] + [slot * slot_rows for slot in slot_at]


def call(kernel, name, shapes, info, arrays, scratch=(), outs=VMEM, in_place=()):
    return pl.pallas_call(
        lambda *refs: kernel(device_info(info), *refs),
        out_shape=shapes,
        in_specs=[VMEM] * len(arrays) + [ANY] * len(in_place),
        out_specs=outs if isinstance(outs, tuple) else jax.tree.map(lambda _: outs, shapes),
        scratch_shapes=list(scratch),
        input_output_aliases={len(arrays) + n: n for n in range(len(in_place))},
        compiler_params=params(),
        cost_estimate=COST,
        name=name,
    )(*arrays, *in_place)


TOKEN = jax.ShapeDtypeStruct((8, HD), F32)


def token_kernel(*refs):
    refs[-1][...] = jnp.zeros_like(refs[-1])


def token_of(*arrays, cost=COST):
    return pl.pallas_call(
        token_kernel,
        out_shape=TOKEN,
        in_specs=[ANY] * len(arrays),
        out_specs=VMEM,
        compiler_params=params(),
        cost_estimate=cost,
        name="token",
    )(*arrays)


def pack_kernel(places, *refs):
    sources, outs, sems = refs[: len(places)], refs[len(places) : -1], refs[-1]
    copies = []
    for n, (source, (out, row, col)) in enumerate(zip(sources, places)):
        first, last, at = (0, source.shape[1], col) if isinstance(col, int) else (*col, 0)
        target = outs[out].at[row : row + source.shape[0], at : at + last - first]
        copies.append(pltpu.make_async_copy(source.at[:, first:last], target, sems.at[n]))
    for copy in copies:
        copy.start()
    for copy in copies:
        copy.wait()


def pack(arrays, places, shapes, limit=20, outs=ANY):
    return pl.pallas_call(
        functools.partial(pack_kernel, places),
        out_shape=tuple(jax.ShapeDtypeStruct(shape, BF16) for shape in shapes),
        in_specs=[ANY] * len(arrays),
        out_specs=(outs,) * len(shapes),
        scratch_shapes=[pltpu.SemaphoreType.DMA((len(arrays),))],
        compiler_params=params(limit),
        cost_estimate=COST,
        name="pack",
    )(*arrays)


def pair_kernel(nearer, count, info, *refs):
    own, far, near = (refs[n * count : (n + 1) * count] for n in range(3))
    pair = refs[-1]
    total = pair.shape[0] // 2

    def put(at, blocks):
        for block in blocks:
            pair[at : at + block.shape[0], :] = block[...]
            at += block.shape[0]

    @pl.when(info[0] == nearer)
    def _():
        put(0, own)
        put(total, near)

    @pl.when(info[0] != nearer)
    def _():
        put(0, near)
        put(total, far)


def pair_for_peer(info, nearer, own, near, far, after=()):
    total = sum(block.shape[0] for block in own)
    shape = jax.ShapeDtypeStruct((2 * total, own[0].shape[1]), BF16)
    kernel = functools.partial(pair_kernel, nearer, len(own))
    return call(kernel, "pair", shape, info, (*own, *far, *near, *after))


def pieces(x):
    hi = x.astype(BF16)
    rest = x - hi.astype(F32)
    mid = rest.astype(BF16)
    low = (rest - mid.astype(F32)).astype(BF16)
    return hi.astype(F32), mid.astype(F32), low.astype(F32)


def spread(x, first, into):
    lane = lax.broadcasted_iota(jnp.int32, into.shape, 1)
    for n, piece in enumerate(pieces(x)):
        into = jnp.where(lane == first + n, piece, into)
    return into


def minus_ones(rows, first):
    lane = lax.broadcasted_iota(jnp.int32, (rows, HD), 1)
    return jnp.where((lane >= first) & (lane < first + 3), -1.0, 0.0).astype(BF16)


def stacked(refs):
    blocks = [ref[...] for ref in refs]
    return blocks[0] if len(blocks) == 1 else jnp.concatenate(blocks, axis=0)


def head_cols(head):
    return slice(head * HD, (head + 1) * HD)


def probs_kernel(info, kv, query, near, far, odd, *refs):
    probs, mixed, stats, span = refs[-4:]
    rows, kv_width = kv.shape[0], kv.shape[1] // 2
    heads = query.shape[1] // HD
    shard = info[1]

    span[:rows, :] = far[...]
    span[rows : 2 * rows, :] = odd[rows:, :]
    span[2 * rows : 3 * rows, :] = near[...]
    span[3 * rows : 4 * rows, :] = odd[:rows, :]
    span[4 * rows :, :] = kv[...]

    span_rows = span.shape[0]
    row = lax.broadcasted_iota(jnp.int32, (rows, 1), 0)
    col = lax.broadcasted_iota(jnp.int32, (rows, span_rows), 1)
    first = jnp.maximum(row + 1, (SPAN_BLOCKS - 1 - shard) * rows)
    allowed = (col >= first) & (col <= row + WIN)
    row_stats = jnp.zeros((rows, HD), F32)
    for head in range(heads):
        group = head // 2
        scores = dot(query[:, head_cols(head)], span[:, head_cols(group)], NT) * SCALE
        scores = jnp.where(allowed, scores, -1e30)
        top = jnp.max(scores, axis=1, keepdims=True)
        weights = jnp.exp(scores - top)
        total = jnp.sum(weights, axis=1, keepdims=True)
        probability = (weights * (1.0 / total)).astype(BF16)
        probs[head] = probability
        value_span = span[:, kv_width + group * HD : kv_width + (group + 1) * HD]
        mixed[:, head_cols(head)] = dot(probability, value_span, NN)
        level = (top + jnp.log(total)) * (1.0 / SCALE)
        row_stats = spread(level, 8 * head, row_stats)
    stats[...] = row_stats.astype(BF16)


def attention_probs(info, kv, query, near, far, odd, after):
    rows, width = query.shape
    span_rows = SPAN_BLOCKS * rows
    shapes = (
        jax.ShapeDtypeStruct((width // HD, rows, span_rows), BF16),
        jax.ShapeDtypeStruct((rows, width), F32),
        jax.ShapeDtypeStruct((rows, HD), BF16),
        jax.ShapeDtypeStruct((span_rows, kv.shape[1]), BF16),
    )
    arrays = (kv, query, near, far, odd, *after)
    return call(probs_kernel, "attention_probs", shapes, info, arrays)


def finish_rows(info, slot, product, mixed, stats, pay, at):
    rows, width = product.shape
    start = pl.multiple_of(info[2 + slot], 16)
    dout = product.astype(BF16)
    row_stats = stats[pl.ds(start, rows), :].astype(F32)
    out_rows = mixed[pl.ds(start, rows), :]
    for head in range(width // HD):
        cols = head_cols(head)
        delta = jnp.sum(dout[:, cols].astype(F32) * out_rows[:, cols], axis=1, keepdims=True)
        row_stats = spread(delta, 8 * head + 3, row_stats)
    pay[at : at + rows, :width] = dout
    pay[at : at + rows, width:] = row_stats.astype(BF16)


def dout_kernel(slots, info, *refs):
    sources = refs[: sum(slots.values())]
    weight, mixed, stats = refs[len(sources) : len(sources) + 3]
    pay = refs[-1]
    rows = sources[0].shape[0]
    parts = []
    at = 0
    for n in slots.values():
        part = sources[at][...]
        for other in sources[at + 1 : at + n]:
            part = part + other[...]
        parts.append(part)
        at += n
    block = parts[0] if len(parts) == 1 else jnp.concatenate(parts, axis=0)
    product = dot(weight[...], block, NT).T
    for n, slot in enumerate(slots):
        finish_rows(info, slot, product[n * rows : (n + 1) * rows], mixed, stats, pay, n * rows)


def dout_rows(info, slots, sources, weight, mixed, stats, after=()):
    total = sources[0].shape[0] * len(slots)
    shape = jax.ShapeDtypeStruct((total, weight.shape[0] + HD), BF16)
    arrays = (*sources, weight, mixed, stats, *after)
    return call(functools.partial(dout_kernel, slots), "dout_rows", shape, info, arrays)


def query_kernel(slots, count, info, probs, span, *refs, then=lambda: None):
    out, done, held, sems = refs[-4:]
    done[...] = jnp.zeros_like(done)
    pay = stacked(refs[:count])
    heads, rows, _ = probs.shape
    kv_width = span.shape[1] // 2
    total = pay.shape[0]
    part_rows = total // len(slots)
    starts = [pl.multiple_of(info[2 + slot], 16) for slot in slots]
    extra = pay[:, heads * HD :].astype(F32)
    lane = lax.broadcasted_iota(jnp.int32, extra.shape, 1)
    for group in range(heads // 2):
        key = span[:, head_cols(group)]
        value = span[:, kv_width + group * HD : kv_width + (group + 1) * HD]
        pair = (2 * group, 2 * group + 1)
        dprobs = dot(jnp.concatenate([pay[:, head_cols(head)] for head in pair], axis=0), value, NT)
        parts = []
        for m, head in enumerate(pair):
            first = 8 * head + 3
            delta = jnp.sum(
                jnp.where((lane >= first) & (lane < first + 3), extra, 0.0), axis=1, keepdims=True
            )
            for n, start in enumerate(starts):
                at = m * total + n * part_rows
                weights = probs[head, pl.ds(start, part_rows), :].astype(F32)
                centred = dprobs[at : at + part_rows, :] - delta[n * part_rows : (n + 1) * part_rows]
                parts.append((weights * centred).astype(BF16))
        grads = dot(jnp.concatenate(parts, axis=0), key, NN) * SCALE
        for m, head in enumerate(pair):
            held[:, head_cols(head)] = grads[m * total : (m + 1) * total, :]
    copies = [
        pltpu.make_async_copy(
            held.at[n * part_rows : (n + 1) * part_rows, :],
            out.at[pl.ds(start, part_rows), :],
            sems.at[n],
        )
        for n, start in enumerate(starts)
    ]
    for copy in copies:
        copy.start()
    then()
    for copy in copies:
        copy.wait()


def query_grads(info, slots, pays, probs, span, before=()):
    heads, rows, _ = probs.shape
    total = sum(pay.shape[0] for pay in pays)
    return call(
        functools.partial(query_kernel, slots, len(pays)),
        "query_grads",
        (
            jax.ShapeDtypeStruct((rows, heads * HD), F32),
            TOKEN,
        ),
        info,
        (probs, span, *pays),
        [pltpu.VMEM((total, heads * HD), F32), pltpu.SemaphoreType.DMA((len(slots),))],
        outs=(ANY, VMEM),
        in_place=before,
    )


def key_kernel(blocks, q_count, d_count, before_count, last, info, kv, *refs):
    q_refs, d_refs = refs[:q_count], refs[q_count : q_count + d_count]
    before = refs[q_count + d_count : q_count + d_count + before_count]
    if last:
        grad_k, grad_v, q_cat, d_cat, held_k, held_v, sems = refs[-7:]
    else:
        held_k, held_v, q_cat, d_cat = refs[-4:]
    rows, kv_width = kv.shape[0], kv.shape[1] // 2
    width = q_cat.shape[1]
    lanes = q_cat.shape[0]
    part_rows = lanes // sum(len(block[1]) for block in blocks)
    lane = lax.broadcasted_iota(jnp.int32, (1, lanes), 1)
    low = jnp.zeros((1, lanes), jnp.int32)
    high = jnp.full((1, lanes), rows, jnp.int32)
    at = 0
    for distance, slots, q_at, q_row, d_at, d_row in blocks:
        size = len(slots) * part_rows
        d_cat[at : at + size, :] = d_refs[d_at][d_row : d_row + size, :]
        for slot in slots:
            start = pl.multiple_of(info[2 + slot], 16)
            q_cat[at : at + part_rows, :] = q_refs[q_at][pl.ds(start + q_row, part_rows), :]
            inside = (lane >= at) & (lane < at + part_rows)
            if distance == 0:
                high = jnp.where(inside, lane - at + start, high)
            if distance == SPAN_BLOCKS - 1:
                low = jnp.where(inside, lane - at + start + 1, low)
            at += part_rows

    masked = any(block[0] in (0, SPAN_BLOCKS - 1) for block in blocks)
    key_row = lax.broadcasted_iota(jnp.int32, (rows, lanes), 0)
    allowed = (key_row >= low) & (key_row <= high)
    extra = d_cat[:, width:]
    copies = []
    for group in range(kv_width // HD):
        cols = head_cols(group)
        key = kv[:, cols]
        value = kv[:, kv_width + group * HD : kv_width + (group + 1) * HD]
        sum_k = None
        sum_v = None
        for head in (2 * group, 2 * group + 1):
            queries = q_cat[:, head_cols(head)]
            dout = d_cat[:, head_cols(head)]
            scores = dot(
                jnp.concatenate([key, minus_ones(rows, 8 * head)], axis=1),
                jnp.concatenate([queries, extra], axis=1),
                NT,
            )
            probability = jnp.exp(scores * SCALE)
            if masked:
                probability = jnp.where(allowed, probability, 0.0)
            centred = dot(
                jnp.concatenate([value, minus_ones(rows, 8 * head + 3)], axis=1),
                jnp.concatenate([dout, extra], axis=1),
                NT,
            )
            dscores = (probability * centred).astype(BF16)
            term_v = dot(probability.astype(BF16), dout, NN)
            term_k = dot(dscores, queries, NN)
            sum_v = term_v if sum_v is None else sum_v + term_v
            sum_k = term_k if sum_k is None else sum_k + term_k
        sum_k = sum_k * SCALE
        if before:
            sum_k = sum_k + before[0][:, cols]
            sum_v = sum_v + before[1][:, cols]
        held_k[:, cols] = sum_k
        held_v[:, cols] = sum_v
        for n, (held, out) in enumerate(((held_k, grad_k), (held_v, grad_v)) if last else ()):
            copy = pltpu.make_async_copy(held.at[:, cols], out.at[:, cols], sems.at[2 * group + n])
            copy.start()
            copies.append(copy)
    for copy in copies:
        copy.wait()


def key_grads(info, blocks, kv, q_arrays, d_arrays, slot_rows, before=(), after=(), last=False):
    lanes = sum(len(block[1]) for block in blocks) * slot_rows
    width = q_arrays[0].shape[1]
    kv_width = kv.shape[1] // 2
    shape = jax.ShapeDtypeStruct((kv.shape[0], kv_width), F32)
    held = pltpu.VMEM(shape.shape, F32)
    return call(
        functools.partial(key_kernel, blocks, len(q_arrays), len(d_arrays), len(before), last),
        "key_grads",
        (shape, shape),
        info,
        (kv, *q_arrays, *d_arrays, *before, *after),
        [
            pltpu.VMEM((lanes, width), BF16),
            pltpu.VMEM((lanes, width + HD), BF16),
        ]
        + ([held, held, pltpu.SemaphoreType.DMA((2 * (kv_width // HD),))] if last else []),
        outs=ANY if last else VMEM,
    )


def late_kernel(slots, blocks, counts, info, probs, span, pay, *refs):
    out, done, grad_k, grad_v, held, sems, q_cat, d_cat = refs[-8:]
    arrays = refs[: 1 + sum(counts)]
    query_kernel(
        slots, 1, info, probs, span, pay, out, done, held, sems,
        then=lambda: key_kernel(
            blocks, *counts, False, info, *arrays, grad_k, grad_v, q_cat, d_cat
        ),
    )


def late_grads(info, slots, pay, probs, span, grad_q, blocks, kv, q_arrays, d_arrays, slot_rows, before):
    heads, rows, _ = probs.shape
    lanes = sum(len(block[1]) for block in blocks) * slot_rows
    width = heads * HD
    shape = jax.ShapeDtypeStruct((rows, kv.shape[1] // 2), F32)
    counts = (len(q_arrays), len(d_arrays), len(before))
    return call(
        functools.partial(late_kernel, slots, blocks, counts),
        "late_grads",
        (jax.ShapeDtypeStruct((rows, width), F32), TOKEN, shape, shape),
        info,
        (probs, span, pay, kv, *q_arrays, *d_arrays, *before),
        [
            pltpu.VMEM((pay.shape[0], width), F32),
            pltpu.SemaphoreType.DMA((len(slots),)),
            pltpu.VMEM((lanes, width), BF16),
            pltpu.VMEM((lanes, width + HD), BF16),
        ],
        outs=(ANY, VMEM, VMEM, VMEM),
        in_place=(grad_q,),
    )


def on_device(ctx, queries, keys, values, grad_out, out_weight):
    rows, width = queries.shape
    kv_width = 2 * keys.shape[1]
    slot_rows = grad_out.shape[0]
    swap = [(i, i ^ 1) for i in range(ctx)]

    def along(x, pairs, name):
        with jax.named_scope(name):
            return lax.ppermute(x, "ctx", pairs)

    def over(x, pairs, name):
        with jax.named_scope(name):
            return lax.ppermute(x, "tp", pairs)

    def moved(distance):
        return [(i, i + distance) for i in range(ctx) if 0 <= i + distance < ctx]

    info = slot_rows

    middle = [(1, 2), (2, 1)]
    ends = [(0, 1), (1, 0), (2, 3), (3, 2)]
    outward = [(1, 0), (2, 3)]
    mid_first = over(grad_out, middle, "mid_first")
    end_first = over(grad_out, ends, "end_first")
    mid_second = over(end_first, middle, "mid_second")
    out_second = over(mid_first, outward, "out_second")

    kv, query = pack(
        [keys, values, queries],
        [(0, 0, 0), (0, 0, kv_width // 2), (1, 0, 0)],
        [(rows, kv_width), (rows, width)],
        limit=56,
        outs=VMEM,
    )
    near_kv = along(kv, moved(2), "kv_near")
    far_kv = along(kv, moved(4), "kv_far")
    near_q = along(query, moved(-2), "q_near")
    far_q = along(query, moved(-4), "q_far")
    odd_kv = along(pair_for_peer(info, 0, [kv], [near_kv], [far_kv]), swap, "kv_swap")
    odd_q = along(pair_for_peer(info, 1, [query], [near_q], [far_q]), swap, "q_swap")


    probs, mixed, stats, span = attention_probs(
        info, kv, query, near_kv, far_kv, odd_kv, (odd_q,)
    )

    def sent(pay, name):
        far = along(pay, moved(-4), name + "_far")
        near = along(pay, moved(-2), name + "_near")
        return near, far

    second_came = token_of(out_second, mid_second, cost=FETCH)
    mid_second, second_came, stats = lax.optimization_barrier((mid_second, second_came, stats))
    out_third = over(mid_second, outward, "out_third")
    statistics = (out_weight, mixed, stats)
    early, late = {0: 1, 1: 1, 2: 2}, {3: 2}
    pay_a = dout_rows(info, early, (grad_out, end_first, mid_first, out_second), *statistics, (second_came,))
    near_a, far_a = sent(pay_a, "early")
    grad_q, queries_done = query_grads(info, early, (pay_a,), probs, span)

    a, b = (0, 1, 2), (3,)
    grads = key_grads(info, ((0, a, 0, 0, 0, 0),), kv, (query,), (pay_a,), slot_rows)
    pair = pair_for_peer(info, 1, (pay_a,), (near_a,), (far_a,), (queries_done, grads[0]))
    odd_a = along(pair, swap, "early_swap")

    pay_b = dout_rows(info, late, (mid_second, out_third), *statistics, (queries_done,))
    near_b, far_b = sent(pay_b, "late")
    blocks = (
        (2, a, 1, 0, 2, 0),
        (4, a, 2, 0, 1, 0),
        (1, a, 3, 0, 3, 0),
        (3, a, 3, rows, 3, len(a) * slot_rows),
        (0, b, 0, 0, 4, 0),
    )
    q_arrays = (query, near_q, far_q, odd_q)
    d_arrays = (pay_a, far_a, near_a, odd_a, pay_b)
    grad_q, queries_done, *grads = late_grads(
        info, late, pay_b, probs, span, grad_q, blocks, kv, q_arrays, d_arrays, slot_rows, grads
    )
    after = (queries_done, grads[0])
    pair = pair_for_peer(info, 1, (pay_b,), (near_b,), (far_b,), after)
    odd_b = along(pair, swap, "late_swap")
    blocks = ((2, b, 0, 0, 1, 0), (4, b, 1, 0, 0, 0))
    grads = key_grads(info, blocks, kv, (near_q, far_q), (far_b, near_b), slot_rows, grads)
    blocks = ((1, b, 0, 0, 0, 0), (3, b, 0, rows, 0, slot_rows))
    grad_k, grad_v = key_grads(info, blocks, kv, (odd_q,), (odd_b,), slot_rows, grads, last=True)
    return (grad_q, grad_k, grad_v)


def solution(mesh):
    in_specs = (
        P("ctx", "tp"),
        P("ctx", "tp"),
        P("ctx", "tp"),
        P(("ctx", "tp"), None),
        P("tp", None),
    )
    out_specs = (P("ctx", "tp"), P("ctx", "tp"), P("ctx", "tp"))
    return jax.shard_map(
        functools.partial(on_device, mesh.shape["ctx"]),
        mesh=mesh,
        in_specs=in_specs,
        out_specs=out_specs,
        check_vma=False,
    )
```

```python
import functools

import jax
import jax.numpy as jnp
from jax import lax
from jax.experimental import pallas as pl
from jax.experimental.pallas import tpu as pltpu
from jax.sharding import PartitionSpec as P

HD = 128
WIN = 1024
SPAN_BLOCKS = 5
SCALE = 168.0 ** (-0.5)
NT = (((1,), (1,)), ((), ()))
NN = (((1,), (0,)), ((), ()))
F32 = jnp.float32
BF16 = jnp.bfloat16
FETCH = pl.CostEstimate(flops=10**9, bytes_accessed=1, transcendentals=0)
VMEM = pl.BlockSpec(memory_space=pltpu.VMEM)
ANY = pl.BlockSpec(memory_space=pl.ANY)
COST = pl.CostEstimate(flops=1, bytes_accessed=1, transcendentals=0)


def dot(a, b, dims):
    return lax.dot_general(a, b, dims, preferred_element_type=F32)


def params(limit=20):
    return pltpu.CompilerParams(vmem_limit_bytes=limit * 2**20)


def device_info(slot_rows):
    shard = lax.axis_index("ctx")
    tp = lax.axis_index("tp")
    near_side = jnp.where(tp < 2, 1, 0)
    slot_at = [tp, tp + 1 - 2 * lax.rem(tp, 2), 1 + near_side, 3 * near_side]
    return [lax.rem(shard, 2), shard] + [slot * slot_rows for slot in slot_at]


def call(kernel, name, shapes, info, arrays, scratch=(), outs=VMEM, in_place=()):
    return pl.pallas_call(
        lambda *refs: kernel(device_info(info), *refs),
        out_shape=shapes,
        in_specs=[VMEM] * len(arrays) + [ANY] * len(in_place),
        out_specs=outs if isinstance(outs, tuple) else jax.tree.map(lambda _: outs, shapes),
        scratch_shapes=list(scratch),
        input_output_aliases={len(arrays) + n: n for n in range(len(in_place))},
        compiler_params=params(),
        cost_estimate=COST,
        name=name,
    )(*arrays, *in_place)


TOKEN = jax.ShapeDtypeStruct((8, HD), F32)


def token_kernel(*refs):
    refs[-1][...] = jnp.zeros_like(refs[-1])


def token_of(*arrays, cost=COST):
    return pl.pallas_call(
        token_kernel,
        out_shape=TOKEN,
        in_specs=[ANY] * len(arrays),
        out_specs=VMEM,
        compiler_params=params(),
        cost_estimate=cost,
        name="token",
    )(*arrays)


def pack_kernel(places, *refs):
    sources, outs, sems = refs[: len(places)], refs[len(places) : -1], refs[-1]
    copies = []
    for n, (source, (out, row, col)) in enumerate(zip(sources, places)):
        first, last, at = (0, source.shape[1], col) if isinstance(col, int) else (*col, 0)
        target = outs[out].at[row : row + source.shape[0], at : at + last - first]
        copies.append(pltpu.make_async_copy(source.at[:, first:last], target, sems.at[n]))
    for copy in copies:
        copy.start()
    for copy in copies:
        copy.wait()


def pack(arrays, places, shapes, limit=20, outs=ANY):
    return pl.pallas_call(
        functools.partial(pack_kernel, places),
        out_shape=tuple(jax.ShapeDtypeStruct(shape, BF16) for shape in shapes),
        in_specs=[ANY] * len(arrays),
        out_specs=(outs,) * len(shapes),
        scratch_shapes=[pltpu.SemaphoreType.DMA((len(arrays),))],
        compiler_params=params(limit),
        cost_estimate=COST,
        name="pack",
    )(*arrays)


def pair_kernel(nearer, count, info, *refs):
    own, far, near = (refs[n * count : (n + 1) * count] for n in range(3))
    pair = refs[-1]
    total = pair.shape[0] // 2

    def put(at, blocks):
        for block in blocks:
            pair[at : at + block.shape[0], :] = block[...]
            at += block.shape[0]

    @pl.when(info[0] == nearer)
    def _():
        put(0, own)
        put(total, near)

    @pl.when(info[0] != nearer)
    def _():
        put(0, near)
        put(total, far)


def pair_for_peer(info, nearer, own, near, far, after=()):
    total = sum(block.shape[0] for block in own)
    shape = jax.ShapeDtypeStruct((2 * total, own[0].shape[1]), BF16)
    kernel = functools.partial(pair_kernel, nearer, len(own))
    return call(kernel, "pair", shape, info, (*own, *far, *near, *after))


def pieces(x):
    hi = x.astype(BF16)
    rest = x - hi.astype(F32)
    mid = rest.astype(BF16)
    low = (rest - mid.astype(F32)).astype(BF16)
    return hi.astype(F32), mid.astype(F32), low.astype(F32)


def spread(x, first, into):
    lane = lax.broadcasted_iota(jnp.int32, into.shape, 1)
    for n, piece in enumerate(pieces(x)):
        into = jnp.where(lane == first + n, piece, into)
    return into


def minus_ones(rows, first):
    lane = lax.broadcasted_iota(jnp.int32, (rows, HD), 1)
    return jnp.where((lane >= first) & (lane < first + 3), -1.0, 0.0).astype(BF16)


def stacked(refs):
    blocks = [ref[...] for ref in refs]
    return blocks[0] if len(blocks) == 1 else jnp.concatenate(blocks, axis=0)


def head_cols(head):
    return slice(head * HD, (head + 1) * HD)


def probs_kernel(info, kv, query, near, far, odd, *refs):
    probs, mixed, stats, span = refs[-4:]
    rows, kv_width = kv.shape[0], kv.shape[1] // 2
    heads = query.shape[1] // HD
    shard = info[1]

    span[:rows, :] = far[...]
    span[rows : 2 * rows, :] = odd[rows:, :]
    span[2 * rows : 3 * rows, :] = near[...]
    span[3 * rows : 4 * rows, :] = odd[:rows, :]
    span[4 * rows :, :] = kv[...]

    span_rows = span.shape[0]
    row = lax.broadcasted_iota(jnp.int32, (rows, 1), 0)
    col = lax.broadcasted_iota(jnp.int32, (rows, span_rows), 1)
    first = jnp.maximum(row + 1, (SPAN_BLOCKS - 1 - shard) * rows)
    allowed = (col >= first) & (col <= row + WIN)
    row_stats = jnp.zeros((rows, HD), F32)
    for head in range(heads):
        group = head // 2
        scores = dot(query[:, head_cols(head)], span[:, head_cols(group)], NT) * SCALE
        scores = jnp.where(allowed, scores, -1e30)
        top = jnp.max(scores, axis=1, keepdims=True)
        weights = jnp.exp(scores - top)
        total = jnp.sum(weights, axis=1, keepdims=True)
        probability = (weights * (1.0 / total)).astype(BF16)
        probs[head] = probability
        value_span = span[:, kv_width + group * HD : kv_width + (group + 1) * HD]
        mixed[:, head_cols(head)] = dot(probability, value_span, NN)
        level = (top + jnp.log(total)) * (1.0 / SCALE)
        row_stats = spread(level, 8 * head, row_stats)
    stats[...] = row_stats.astype(BF16)


def attention_probs(info, kv, query, near, far, odd, after):
    rows, width = query.shape
    span_rows = SPAN_BLOCKS * rows
    shapes = (
        jax.ShapeDtypeStruct((width // HD, rows, span_rows), BF16),
        jax.ShapeDtypeStruct((rows, width), F32),
        jax.ShapeDtypeStruct((rows, HD), BF16),
        jax.ShapeDtypeStruct((span_rows, kv.shape[1]), BF16),
    )
    arrays = (kv, query, near, far, odd, *after)
    return call(probs_kernel, "attention_probs", shapes, info, arrays)


def finish_rows(info, slot, product, mixed, stats, pay, at):
    rows, width = product.shape
    start = pl.multiple_of(info[2 + slot], 16)
    dout = product.astype(BF16)
    row_stats = stats[pl.ds(start, rows), :].astype(F32)
    out_rows = mixed[pl.ds(start, rows), :]
    for head in range(width // HD):
        cols = head_cols(head)
        delta = jnp.sum(dout[:, cols].astype(F32) * out_rows[:, cols], axis=1, keepdims=True)
        row_stats = spread(delta, 8 * head + 3, row_stats)
    pay[at : at + rows, :width] = dout
    pay[at : at + rows, width:] = row_stats.astype(BF16)


def dout_kernel(slots, info, *refs):
    sources = refs[: sum(slots.values())]
    weight, mixed, stats = refs[len(sources) : len(sources) + 3]
    pay = refs[-1]
    rows = sources[0].shape[0]
    parts = []
    at = 0
    for n in slots.values():
        part = sources[at][...]
        for other in sources[at + 1 : at + n]:
            part = part + other[...]
        parts.append(part)
        at += n
    block = parts[0] if len(parts) == 1 else jnp.concatenate(parts, axis=0)
    product = dot(weight[...], block, NT).T
    for n, slot in enumerate(slots):
        finish_rows(info, slot, product[n * rows : (n + 1) * rows], mixed, stats, pay, n * rows)


def dout_rows(info, slots, sources, weight, mixed, stats, after=()):
    total = sources[0].shape[0] * len(slots)
    shape = jax.ShapeDtypeStruct((total, weight.shape[0] + HD), BF16)
    arrays = (*sources, weight, mixed, stats, *after)
    return call(functools.partial(dout_kernel, slots), "dout_rows", shape, info, arrays)


def query_kernel(slots, count, info, probs, span, *refs):
    out, done, held, sems = refs[-4:]
    done[...] = jnp.zeros_like(done)
    pay = stacked(refs[:count])
    heads, rows, _ = probs.shape
    kv_width = span.shape[1] // 2
    total = pay.shape[0]
    part_rows = total // len(slots)
    starts = [pl.multiple_of(info[2 + slot], 16) for slot in slots]
    extra = pay[:, heads * HD :].astype(F32)
    lane = lax.broadcasted_iota(jnp.int32, extra.shape, 1)
    for group in range(heads // 2):
        key = span[:, head_cols(group)]
        value = span[:, kv_width + group * HD : kv_width + (group + 1) * HD]
        pair = (2 * group, 2 * group + 1)
        dprobs = dot(jnp.concatenate([pay[:, head_cols(head)] for head in pair], axis=0), value, NT)
        parts = []
        for m, head in enumerate(pair):
            first = 8 * head + 3
            delta = jnp.sum(
                jnp.where((lane >= first) & (lane < first + 3), extra, 0.0), axis=1, keepdims=True
            )
            for n, start in enumerate(starts):
                at = m * total + n * part_rows
                weights = probs[head, pl.ds(start, part_rows), :].astype(F32)
                centred = dprobs[at : at + part_rows, :] - delta[n * part_rows : (n + 1) * part_rows]
                parts.append((weights * centred).astype(BF16))
        grads = dot(jnp.concatenate(parts, axis=0), key, NN) * SCALE
        for m, head in enumerate(pair):
            held[:, head_cols(head)] = grads[m * total : (m + 1) * total, :]
    copies = [
        pltpu.make_async_copy(
            held.at[n * part_rows : (n + 1) * part_rows, :],
            out.at[pl.ds(start, part_rows), :],
            sems.at[n],
        )
        for n, start in enumerate(starts)
    ]
    for copy in copies:
        copy.start()
    for copy in copies:
        copy.wait()


def query_grads(info, slots, pays, probs, span, before=()):
    heads, rows, _ = probs.shape
    total = sum(pay.shape[0] for pay in pays)
    return call(
        functools.partial(query_kernel, slots, len(pays)),
        "query_grads",
        (
            jax.ShapeDtypeStruct((rows, heads * HD), F32),
            TOKEN,
        ),
        info,
        (probs, span, *pays),
        [pltpu.VMEM((total, heads * HD), F32), pltpu.SemaphoreType.DMA((len(slots),))],
        outs=(ANY, VMEM),
        in_place=before,
    )


def key_kernel(blocks, q_count, d_count, before_count, last, info, kv, *refs):
    q_refs, d_refs = refs[:q_count], refs[q_count : q_count + d_count]
    before = refs[q_count + d_count : q_count + d_count + before_count]
    if last:
        grad_k, grad_v, q_cat, d_cat, held_k, held_v, sems = refs[-7:]
    else:
        held_k, held_v, q_cat, d_cat = refs[-4:]
    rows, kv_width = kv.shape[0], kv.shape[1] // 2
    width = q_cat.shape[1]
    lanes = q_cat.shape[0]
    part_rows = lanes // sum(len(block[1]) for block in blocks)
    lane = lax.broadcasted_iota(jnp.int32, (1, lanes), 1)
    low = jnp.zeros((1, lanes), jnp.int32)
    high = jnp.full((1, lanes), rows, jnp.int32)
    at = 0
    for distance, slots, q_at, q_row, d_at, d_row in blocks:
        size = len(slots) * part_rows
        d_cat[at : at + size, :] = d_refs[d_at][d_row : d_row + size, :]
        for slot in slots:
            start = pl.multiple_of(info[2 + slot], 16)
            q_cat[at : at + part_rows, :] = q_refs[q_at][pl.ds(start + q_row, part_rows), :]
            inside = (lane >= at) & (lane < at + part_rows)
            if distance == 0:
                high = jnp.where(inside, lane - at + start, high)
            if distance == SPAN_BLOCKS - 1:
                low = jnp.where(inside, lane - at + start + 1, low)
            at += part_rows

    masked = any(block[0] in (0, SPAN_BLOCKS - 1) for block in blocks)
    key_row = lax.broadcasted_iota(jnp.int32, (rows, lanes), 0)
    allowed = (key_row >= low) & (key_row <= high)
    extra = d_cat[:, width:]
    copies = []
    for group in range(kv_width // HD):
        cols = head_cols(group)
        key = kv[:, cols]
        value = kv[:, kv_width + group * HD : kv_width + (group + 1) * HD]
        key_pairs = []
        sum_v = None
        for head in (2 * group, 2 * group + 1):
            queries = q_cat[:, head_cols(head)]
            dout = d_cat[:, head_cols(head)]
            scores = dot(
                jnp.concatenate([key, minus_ones(rows, 8 * head)], axis=1),
                jnp.concatenate([queries, extra], axis=1),
                NT,
            )
            probability = jnp.exp(scores * SCALE)
            if masked:
                probability = jnp.where(allowed, probability, 0.0)
            centred = dot(
                jnp.concatenate([value, minus_ones(rows, 8 * head + 3)], axis=1),
                jnp.concatenate([dout, extra], axis=1),
                NT,
            )
            dscores = (probability * centred).astype(BF16)
            term_v = dot(probability.astype(BF16), dout, NN)
            key_pairs.append((dscores, queries))
            sum_v = term_v if sum_v is None else sum_v + term_v
        sums = ((sum_v, held_v, grad_v if last else None), (None, held_k, grad_k if last else None))
        for n, (total, held, out) in enumerate(sums):
            if n == 1:
                total = sum(dot(ds, q, NN) for ds, q in key_pairs) * SCALE
            if before:
                total = total + before[1 - n][:, cols]
            held[:, cols] = total
            if last:
                copy = pltpu.make_async_copy(held.at[:, cols], out.at[:, cols], sems.at[2 * group + n])
                copy.start()
                copies.append(copy)
    for copy in copies:
        copy.wait()


def key_grads(info, blocks, kv, q_arrays, d_arrays, slot_rows, before=(), after=(), last=False):
    lanes = sum(len(block[1]) for block in blocks) * slot_rows
    width = q_arrays[0].shape[1]
    kv_width = kv.shape[1] // 2
    shape = jax.ShapeDtypeStruct((kv.shape[0], kv_width), F32)
    held = pltpu.VMEM(shape.shape, F32)
    return call(
        functools.partial(key_kernel, blocks, len(q_arrays), len(d_arrays), len(before), last),
        "key_grads",
        (shape, shape),
        info,
        (kv, *q_arrays, *d_arrays, *before, *after),
        [
            pltpu.VMEM((lanes, width), BF16),
            pltpu.VMEM((lanes, width + HD), BF16),
        ]
        + ([held, held, pltpu.SemaphoreType.DMA((2 * (kv_width // HD),))] if last else []),
        outs=ANY if last else VMEM,
    )


def on_device(ctx, queries, keys, values, grad_out, out_weight):
    rows, width = queries.shape
    kv_width = 2 * keys.shape[1]
    slot_rows = grad_out.shape[0]
    swap = [(i, i ^ 1) for i in range(ctx)]

    def along(x, pairs, name):
        with jax.named_scope(name):
            return lax.ppermute(x, "ctx", pairs)

    def over(x, pairs, name):
        with jax.named_scope(name):
            return lax.ppermute(x, "tp", pairs)

    def moved(distance):
        return [(i, i + distance) for i in range(ctx) if 0 <= i + distance < ctx]

    info = slot_rows

    middle = [(1, 2), (2, 1)]
    ends = [(0, 1), (1, 0), (2, 3), (3, 2)]
    outward = [(1, 0), (2, 3)]
    mid_first = over(grad_out, middle, "mid_first")
    end_first = over(grad_out, ends, "end_first")
    mid_second = over(end_first, middle, "mid_second")
    out_second = over(mid_first, outward, "out_second")

    kv, query = pack(
        [keys, values, queries],
        [(0, 0, 0), (0, 0, kv_width // 2), (1, 0, 0)],
        [(rows, kv_width), (rows, width)],
        limit=56,
        outs=VMEM,
    )
    near_kv = along(kv, moved(2), "kv_near")
    far_kv = along(kv, moved(4), "kv_far")
    near_q = along(query, moved(-2), "q_near")
    far_q = along(query, moved(-4), "q_far")
    odd_kv = along(pair_for_peer(info, 0, [kv], [near_kv], [far_kv]), swap, "kv_swap")
    odd_q = along(pair_for_peer(info, 1, [query], [near_q], [far_q]), swap, "q_swap")


    probs, mixed, stats, span = attention_probs(
        info, kv, query, near_kv, far_kv, odd_kv, (odd_q,)
    )

    def sent(pay, name):
        far = along(pay, moved(-4), name + "_far")
        near = along(pay, moved(-2), name + "_near")
        return near, far

    second_came = token_of(out_second, mid_second, cost=FETCH)
    mid_second, second_came, stats = lax.optimization_barrier((mid_second, second_came, stats))
    out_third = over(mid_second, outward, "out_third")
    statistics = (out_weight, mixed, stats)
    early, late = {0: 1, 1: 1, 2: 2}, {3: 2}
    pay_a = dout_rows(info, early, (grad_out, end_first, mid_first, out_second), *statistics, (second_came,))
    near_a, far_a = sent(pay_a, "early")
    grad_q, queries_done = query_grads(info, early, (pay_a,), probs, span)

    a, b = (0, 1, 2), (3,)
    grads = key_grads(info, ((0, a, 0, 0, 0, 0),), kv, (query,), (pay_a,), slot_rows)
    pair = pair_for_peer(info, 1, (pay_a,), (near_a,), (far_a,), (queries_done, grads[0]))
    odd_a = along(pair, swap, "early_swap")

    pay_b = dout_rows(info, late, (mid_second, out_third), *statistics, (queries_done,))
    near_b, far_b = sent(pay_b, "late")
    grad_q, queries_done = query_grads(info, late, (pay_b,), probs, span, (grad_q,))
    blocks = (
        (2, a, 1, 0, 2, 0),
        (4, a, 2, 0, 1, 0),
        (1, a, 3, 0, 3, 0),
        (3, a, 3, rows, 3, len(a) * slot_rows),
        (0, b, 0, 0, 4, 0),
    )
    q_arrays = (query, near_q, far_q, odd_q)
    d_arrays = (pay_a, far_a, near_a, odd_a, pay_b)
    grads = key_grads(info, blocks, kv, q_arrays, d_arrays, slot_rows, grads)
    after = (queries_done, grads[0])
    pair = pair_for_peer(info, 1, (pay_b,), (near_b,), (far_b,), after)
    odd_b = along(pair, swap, "late_swap")
    blocks = ((2, b, 0, 0, 1, 0), (4, b, 1, 0, 0, 0))
    grads = key_grads(info, blocks, kv, (near_q, far_q), (far_b, near_b), slot_rows, grads)
    blocks = ((1, b, 0, 0, 0, 0), (3, b, 0, rows, 0, slot_rows))
    grad_k, grad_v = key_grads(info, blocks, kv, (odd_q,), (odd_b,), slot_rows, grads, last=True)
    return (grad_q, grad_k, grad_v)


def solution(mesh):
    in_specs = (
        P("ctx", "tp"),
        P("ctx", "tp"),
        P("ctx", "tp"),
        P(("ctx", "tp"), None),
        P("tp", None),
    )
    out_specs = (P("ctx", "tp"), P("ctx", "tp"), P("ctx", "tp"))
    return jax.shard_map(
        functools.partial(on_device, mesh.shape["ctx"]),
        mesh=mesh,
        in_specs=in_specs,
        out_specs=out_specs,
        check_vma=False,
    )
```
